32 devices in a mesh: grp: 2 (over core), exp: 16 (over z, y, x).
Axes of the slice: x: 2, y: 2, z: 4, core: 2. Of those that a mesh axis runs over, the one named last changes fastest.
Arguments:
- tokens: bfloat16 [2, 18432, 512], P(None, ('grp', 'exp')), may hold values from -6 to 6
- expert_picks: int32 [2, 18432, 2], P(None, ('grp', 'exp')), may hold values from 0 to 15, all different within a row
- priority_ranks: int32 [2, 32, 576], P(None, ('grp', 'exp')), may hold values from 0 to 575, each once within a row
- attn_input: bfloat16 [512, 1536], replicated, may hold values from -0.25 to 0.25
- attn_output: bfloat16 [512, 512], replicated, may hold values from -1 to 1
- first_gain: float32 [512], replicated, may hold values from 0.5 to 1.5
- second_gain: float32 [512], replicated, may hold values from 0.5 to 1.5
- router_weight: bfloat16 [512, 16], replicated, may hold values from -0.1875 to 0.1875
- expert_up: bfloat16 [16, 512, 2048], P('exp'), may hold values from -0.25 to 0.25
- expert_down: bfloat16 [16, 2048, 512], P('exp'), may hold values from -0.25 to 0.25
- cotangent: bfloat16 [2, 18432, 512], P(None, ('grp', 'exp')), may hold values from -6 to 6
Outputs:
- block_output: bfloat16 [2, 18432, 512], P(None, ('grp', 'exp'))
- tokens_grad: float32 [2, 18432, 512], P(None, ('grp', 'exp'))
- attn_input_grad: float32 [512, 1536], replicated
- attn_output_grad: float32 [512, 512], replicated
- first_gain_grad: float32 [512], replicated
- second_gain_grad: float32 [512], replicated
- router_grad: float32 [512, 16], replicated
- expert_up_grad: float32 [16, 512, 2048], P('exp')
- expert_down_grad: float32 [16, 2048, 512], P('exp')
The draws below stay inside these ranges and needn't reach their ends.
Inputs may be any that keep to these rules, and one draw needn't show every extreme that they name: `expert_picks`: the two picks of a token differ. `priority_ranks`: for each micro-batch and device, a permutation of 0 to 575.
All inputs are finite; a program needn't handle non-finite values.
Results may differ from the reference program's by a relative error of at most 0.013.
Values may be sent and summed in bfloat16 or wider, within the bound.
No kernel may reach another device: no remote copies, remote signals or barrier semaphores. Data moves between devices by JAX's collectives and lax.ppermute only.
A program may use at most 128 MiB of HBM per device.

```python
import jax
import jax.numpy as jnp
from jax import lax

D = 512
HEADS = 8
HEAD = 64
FF = 2048
SEQ = 144
MICRO = 2
TOK_MB = 576
TOKENS = 18432
EXPERTS = 16
CAP = 36
DEVICES = 32


def shard_levels(stream_key, dims, split, low, high):
    factor_of, own = 1.0, jax.random.fold_in(stream_key, 6)
    for axis_at, shards_of in split:
        heights = jnp.exp(jax.random.uniform(jax.random.fold_in(own, axis_at), (shards_of,), jnp.float32, low / len(split), high / len(split)))
        factor_of = factor_of * jnp.repeat(heights, dims[axis_at] // shards_of).reshape([-1 if axis == axis_at else 1 for axis in range(len(dims))])
    return factor_of


def choose_distinct(rng, rows, count, top, lift):
    sequence = jax.random.permutation(jax.random.fold_in(rng, 1), count)
    pull = sequence
    for power in range(3):
        pull = pull * pull // count
    pull = pull * lift // count
    chance = jax.random.randint(jax.random.fold_in(rng, 2), (rows, count), 0, 4096) + pull
    holders = jax.random.permutation(jax.random.fold_in(rng, 3), rows)[jnp.arange(count) % rows]
    chance = jnp.where(jnp.arange(rows)[:, None] == holders[None, :], 1 << 14, chance)
    score = chance * count + jnp.arange(count)
    return lax.top_k(score.astype(jnp.int32), top)[1].astype(jnp.int32)


def gaussian(rng, dims, deviation, reach, pieces=(), held_as=jnp.bfloat16):
    values = jax.random.normal(rng, dims, jnp.float32) * deviation
    if len(pieces) > 0:
        values = shard_levels(rng, dims, pieces, -0.22, 0.18) * values
    return jnp.clip(values, min=-reach, max=reach).astype(held_as)


def setup_inputs(seed: int = 0) -> dict:
    keys = jax.random.split(jax.random.key(seed), 12)
    return {
        "tokens": gaussian(keys[0], (MICRO, TOKENS, D), 1.0, 6.0, ((1, 32),)),
        "expert_picks": choose_distinct(keys[1], MICRO * TOKENS, EXPERTS, 2, 1024).reshape((MICRO, TOKENS, 2)),
        "priority_ranks": jax.vmap(lambda own: jax.random.permutation(own, TOK_MB))(jax.random.split(keys[2], MICRO * DEVICES)).reshape((MICRO, DEVICES, TOK_MB)).astype(jnp.int32),
        "attn_input": gaussian(keys[3], (D, 3 * D), D ** -0.5, 0.25),
        "attn_output": gaussian(keys[4], (D, D), (D // 16) ** -0.5, 1.0),
        "first_gain": jnp.clip(1.0 + 0.1 * jax.random.normal(keys[5], (D,), jnp.float32), 0.5, 1.5),
        "second_gain": jnp.clip(1.0 + 0.1 * jax.random.normal(keys[6], (D,), jnp.float32), 0.5, 1.5),
        "router_weight": gaussian(keys[7], (D, EXPERTS), (2 * D) ** -0.5, 0.1875),
        "expert_up": gaussian(keys[8], (EXPERTS, D, FF), D ** -0.5, 0.25, ((0, 16),)),
        "expert_down": gaussian(keys[9], (EXPERTS, FF, D), (FF // 4) ** -0.5, 0.25, ((0, 16),)),
        "cotangent": gaussian(keys[10], (MICRO, TOKENS, D), 1.0, 6.0, ((1, 32),)),
    }


EPS = 1e-06
HIGH = lax.Precision.HIGHEST

@jax.custom_vjp
def low(v):
    return lax.optimization_barrier(v.astype(jnp.bfloat16)).astype(jnp.float32)

@jax.custom_vjp
def low_back(v):
    return v

def low_keep(v):
    return (low(v), None)

def low_pass(kept, grad):
    return (grad,)

def back_keep(v):
    return (v, None)

def back_low(kept, grad):
    return (low(grad),)
low.defvjp(low_keep, low_pass)
low_back.defvjp(back_keep, back_low)

def normalize(values):
    center = values - lax.optimization_barrier(jnp.mean(values, axis=-1, keepdims=True))
    return center * lax.rsqrt(lax.optimization_barrier(jnp.mean(center * center, axis=-1, keepdims=True)) + EPS)

def routing_slots(picks, ranks, count):
    rows = ranks.shape[0]
    priority = ranks[:, None] + rows * jnp.arange(2, dtype=jnp.int32)[None, :]
    ordered = jnp.zeros((2 * rows,), jnp.int32).at[priority.reshape(-1)].set(picks.reshape(-1))
    onehot = (ordered[:, None] == jnp.arange(count, dtype=jnp.int32)[None, :]).astype(jnp.int32)
    before = jnp.cumsum(onehot, axis=0) - onehot
    filled = lax.optimization_barrier(jnp.sum(before * onehot, axis=1))
    return filled[priority]

def attend(block):
    query = block[:, 0]
    key = block[:, 1]
    value = block[:, 2]
    scores = low_back(jnp.einsum('qhd,khd->hqk', query, key, precision=HIGH) * HEAD ** (-0.5))
    probs = jax.nn.softmax(scores, axis=-1)
    mixed = jnp.einsum('hqk,khd->qhd', low(probs), value, precision=HIGH)
    return low(low_back(mixed))

def forward(x, attn_in, attn_out, gain_one, gain_two, router, upward, downward, flat, keep_float, choose):
    total = EXPERTS * DEVICES * CAP
    h_first = low(normalize(x) * gain_one)
    qkv = low(low_back(jnp.dot(h_first, attn_in, precision=HIGH)))
    blocks = qkv.reshape(TOKENS // SEQ, SEQ, 3, HEADS, HEAD)
    mixed = lax.map(jax.checkpoint(attend), blocks).reshape(TOKENS, D)
    x_mid = x + low_back(jnp.dot(mixed, attn_out, precision=HIGH))
    h_second = low(normalize(x_mid) * gain_two)
    logits = low_back(jnp.dot(h_second, router, precision=HIGH))
    picked = lax.optimization_barrier(jnp.sum(logits[:, None, :] * choose, axis=-1))
    gates = jax.nn.softmax(picked, axis=-1)
    rows = jnp.broadcast_to(h_second[:, None, :], (TOKENS, 2, D)).reshape(TOKENS * 2, D)
    buffer = jnp.zeros((total, D), jnp.float32).at[flat.reshape(-1)].add(rows, mode='drop')
    buffer = low_back(buffer.reshape(EXPERTS, DEVICES * CAP, D))
    pre = low_back(jnp.einsum('erd,edf->erf', buffer, upward, precision=HIGH))
    act = low(jax.nn.gelu(pre))
    out = low(low_back(jnp.einsum('erf,efd->erd', act, downward, precision=HIGH))).reshape(total, D)
    pair_out = out[jnp.minimum(flat, total - 1)] * keep_float[..., None]
    return x_mid + lax.optimization_barrier(jnp.sum(gates[..., None] * pair_out, axis=1))

def reference(tokens, expert_picks, priority_ranks, attn_input, attn_output, first_gain, second_gain, router_weight, expert_up, expert_down, cotangent):
    weights = tuple((w.astype(jnp.float32) for w in (attn_input, attn_output, first_gain, second_gain, router_weight, expert_up, expert_down)))
    device_ids = jnp.arange(DEVICES, dtype=jnp.int32)[:, None, None]
    totals = None
    outputs = []
    input_grads = []
    for micro in range(MICRO):
        picks = expert_picks[micro].reshape(DEVICES, TOK_MB, 2)
        slots = jax.vmap(lambda p, r: routing_slots(p, r, EXPERTS))(picks, priority_ranks[micro])
        keep = slots < CAP
        flat = jnp.where(keep, picks * (DEVICES * CAP) + device_ids * CAP + slots, EXPERTS * DEVICES * CAP).astype(jnp.int32).reshape(TOKENS, 2)
        keep_float = keep.reshape(TOKENS, 2).astype(jnp.float32)
        choose = (expert_picks[micro][:, :, None] == jnp.arange(EXPERTS, dtype=jnp.int32)[None, None, :]).astype(jnp.float32)

        def apply(x, *params):
            return forward(x, *params, flat, keep_float, choose)
        result, pullback = jax.vjp(apply, tokens[micro].astype(jnp.float32), *weights)
        grads = pullback(cotangent[micro].astype(jnp.float32))
        outputs.append(result.astype(jnp.bfloat16))
        input_grads.append(grads[0])
        totals = grads[1:] if totals is None else tuple((a + b for a, b in zip(totals, grads[1:])))
    return (jnp.stack(outputs), jnp.stack(input_grads), totals[0], totals[1], totals[2], totals[3], totals[4], totals[5], totals[6])
```

```python
import functools

import jax
import jax.numpy as jnp
from jax import lax
from jax.experimental import pallas as pl
from jax.experimental.pallas import tpu as pltpu
from jax.sharding import PartitionSpec as P

HEADS = 8
HEAD = 64
SEQ = 144
MICRO = 2
EPS = 1e-06
GROUP = 4
GW = GROUP * HEAD
GELU_C = 0.7978845608028654
GELU_A = 0.044715
SMALL = 16

BF = jnp.bfloat16
F32 = jnp.float32
MB = 1 << 20


def nn(a, b):
    return lax.dot_general(a, b, (((1,), (0,)), ((), ())), preferred_element_type=F32)


def nt(a, b):
    return lax.dot_general(a, b, (((1,), (1,)), ((), ())), preferred_element_type=F32)


def tn(a, b):
    return lax.dot_general(a, b, (((0,), (0,)), ((), ())), preferred_element_type=F32)


def normalize(values):
    center = values - jnp.mean(values, axis=-1, keepdims=True)
    factor = lax.rsqrt(jnp.mean(center * center, axis=-1, keepdims=True) + EPS)
    return center * factor, factor


def norm_back(grad_normed, normed, factor):
    return factor * (
        grad_normed
        - jnp.mean(grad_normed, axis=-1, keepdims=True)
        - normed * jnp.mean(grad_normed * normed, axis=-1, keepdims=True)
    )


def iota(shape, dim):
    return lax.broadcasted_iota(jnp.int32, shape, dim)


def spread_heads(block):
    head = iota(block.shape, 1) // HEAD
    zero = jnp.zeros_like(block)
    return jnp.concatenate([jnp.where(head == h, block, zero) for h in range(GROUP)], axis=0)


def gather_heads(full):
    rows = full.shape[0] // GROUP
    head = iota((rows, full.shape[1]), 1) // HEAD
    total = jnp.where(head == 0, full[:rows], 0.0)
    for h in range(1, GROUP):
        total = total + jnp.where(head == h, full[h * rows : (h + 1) * rows], 0.0)
    return total


def head_block(ref, rows, part, group, width):
    start = part * width + group * GW
    return ref[rows, start : start + GW]


def fore_kernel(
    cap,
    tok_ref,
    pick_ref,
    rank_ref,
    wqkv_ref,
    wo_ref,
    g1_ref,
    g2_ref,
    router_ref,
    cot_ref,
    send_ref,
    qkv_ref,
    mixed_ref,
    x1_ref,
    lse_ref,
    meta_ref,
    h2_s,
    d0_s,
    d1_s,
):
    rows, width = x1_ref.shape
    experts = router_ref.shape[0]
    images = rows // SEQ
    x_in = tok_ref[0].astype(F32)
    normed, _ = normalize(x_in)
    h_first = (normed * g1_ref[...]).astype(BF)
    qkv_ref[...] = nn(h_first, wqkv_ref[...]).astype(BF)

    def image(i, carry):
        at = pl.ds(pl.multiple_of(i * SEQ, 16), SEQ)
        for g in range(HEADS // GROUP):
            query = spread_heads(head_block(qkv_ref, at, 0, g, width))
            key = head_block(qkv_ref, at, 1, g, width)
            value = head_block(qkv_ref, at, 2, g, width)
            scores = nt(key, query) * (HEAD**-0.5)
            peak = jnp.max(scores, axis=0, keepdims=True)
            expo = jnp.exp(scores - peak)
            denom = jnp.sum(expo, axis=0, keepdims=True)
            probs_low = (expo * (1.0 / denom)).astype(BF)
            lse_ref[pl.ds(i * (HEADS // GROUP) + g, 1), :] = peak + jnp.log(denom)
            mixed = gather_heads(tn(probs_low, value))
            mixed_ref[at, g * GW : (g + 1) * GW] = mixed.astype(BF)
        return carry

    lax.fori_loop(0, images, image, 0)

    x_mid = x_in + nn(mixed_ref[...], wo_ref[...])
    x1_ref[...] = x_mid
    normed, _ = normalize(x_mid)
    h_second = (normed * g2_ref[...]).astype(BF)
    h2_s[...] = h_second
    logits = nt(router_ref[...], h_second)

    rank_row = rank_ref[0].astype(F32)
    eye = iota((rows, rows), 0) == iota((rows, rows), 1)
    rank_col = jnp.sum(jnp.where(eye, rank_row, 0.0), axis=1, keepdims=True)
    less = jnp.where(rank_col < rank_row, 1.0, 0.0).astype(BF)
    picks = pick_ref[0]
    expert = iota((experts, rows), 0)
    on = [jnp.where(expert == picks[k : k + 1], 1.0, 0.0) for k in range(2)]
    before = [nn(on[k].astype(BF), less) for k in range(2)]
    before[1] = before[1] + jnp.sum(on[0], axis=1, keepdims=True)
    place, picked = [], []
    for k in range(2):
        slot = jnp.sum(on[k] * before[k], axis=0, keepdims=True)
        base = picks[k : k + 1].astype(F32) * (2 * cap)
        place.append(jnp.where(slot < cap - 0.5, base + slot, -9999.0))
        picked.append(jnp.sum(on[k] * logits, axis=0, keepdims=True))
    top = jnp.maximum(picked[0], picked[1])
    expo = [jnp.exp(v - top) for v in picked]
    total = expo[0] + expo[1]
    gates = [v / total for v in expo]
    stack = jnp.concatenate(
        gates + place + [picks.astype(F32)] + [jnp.zeros((2, rows), F32)], axis=0
    )
    meta = jnp.transpose(stack)
    meta_ref[...] = meta
    grad_out = cot_ref[0].astype(F32)
    d0_s[...] = (meta[:, 0:1] * grad_out).astype(BF)
    d1_s[...] = (meta[:, 1:2] * grad_out).astype(BF)
    place = [v.astype(jnp.int32) for v in place]

    total_rows = send_ref.shape[0]
    step = total_rows // 4

    def fill(c, carry):
        start = pl.multiple_of(c * step, 16)
        row = iota((step, rows), 0) + start
        one = jnp.ones((step, rows), F32)
        zero = jnp.zeros((step, rows), F32)
        first = jnp.where((row == place[0]) | (row == place[1]), one, zero).astype(BF)
        part = nn(first, h2_s[...])
        part = part + nn(jnp.where(row == place[0] + cap, one, zero).astype(BF), d0_s[...])
        part = part + nn(jnp.where(row == place[1] + cap, one, zero).astype(BF), d1_s[...])
        send_ref[pl.ds(start, step), :] = part.astype(BF)
        return carry

    lax.fori_loop(0, 4, fill, 0)


def micro_spec(shape, micro):
    return pl.BlockSpec((1,) + tuple(shape[1:]), lambda i: (micro,) + (0,) * (len(shape) - 1))


def whole_spec(shape):
    return pl.BlockSpec(tuple(shape), lambda i: (0,) * len(shape))


def params(limit, **more):
    return pltpu.CompilerParams(vmem_limit_bytes=limit * MB, **more)


def fore(micro, cap, tokens, picks_t, ranks, wqkv, wo, g1, g2, router_t, cot):
    _, rows, width = tokens.shape
    experts = router_t.shape[0]
    out_shape = (
        jax.ShapeDtypeStruct((experts * 2 * cap, width), BF),
        jax.ShapeDtypeStruct((rows, 3 * width), BF),
        jax.ShapeDtypeStruct((rows, width), BF),
        jax.ShapeDtypeStruct((rows, width), F32),
        jax.ShapeDtypeStruct((8, GROUP * SEQ), F32),
        jax.ShapeDtypeStruct((rows, 8), F32),
    )
    flops = 2 * rows * width * (4 * width + 3 * experts * 2 * cap + 4 * SEQ)
    return pl.pallas_call(
        functools.partial(fore_kernel, cap),
        grid=(1,),
        in_specs=[
            micro_spec(tokens.shape, micro),
            micro_spec(picks_t.shape, micro),
            micro_spec(ranks.shape, micro),
            whole_spec(wqkv.shape),
            whole_spec(wo.shape),
            whole_spec(g1.shape),
            whole_spec(g2.shape),
            whole_spec(router_t.shape),
            micro_spec(cot.shape, micro),
        ],
        out_specs=[whole_spec(s.shape) for s in out_shape],
        out_shape=out_shape,
        scratch_shapes=[pltpu.VMEM((rows, width), BF) for _ in range(3)],
        compiler_params=params(56),
        cost_estimate=pl.CostEstimate(flops=4 * flops, bytes_accessed=8 * MB, transcendentals=0),
        name="fore",
    )(tokens, picks_t, ranks, wqkv, wo, g1, g2, router_t, cot)


def expert_kernel(cap, first, *refs):
    if first:
        recv_ref, up_ref, down_ref, ret_ref, dup_ref, ddown_ref = refs[:6]
    else:
        recv_ref, up_ref, down_ref, aup_ref, adown_ref, ret_ref, dup_ref, ddown_ref = refs[:8]
    h_s, g_s, out_s, row_s = refs[-4:]
    step = pl.program_id(0)
    steps = pl.num_programs(0)
    slots = h_s.shape[0]

    def position(shape, dim):
        slot = iota(shape, dim)
        block = ((slot.astype(F32) + 0.5) * (1.0 / cap)).astype(jnp.int32)
        return slot + block * cap

    @pl.when(step == 0)
    def _():
        here = iota((slots, 2 * slots), 1)
        there = position((slots, 2 * slots), 0)
        pick = jnp.where(here == there, 1.0, 0.0).astype(BF)
        h_s[...] = nn(pick, recv_ref[...]).astype(BF)
        pick = jnp.where(here == there + cap, 1.0, 0.0).astype(BF)
        g_s[...] = nn(pick, recv_ref[...]).astype(BF)

    up = up_ref[0]
    down = down_ref[0]
    h = h_s[...]
    g = g_s[...]
    pre = nn(h, up)
    grad_act = nt(g, down)
    square = pre * pre
    tanh = jnp.tanh(GELU_C * pre * (1.0 + GELU_A * square))
    half = 0.5 + 0.5 * tanh
    act = (pre * half).astype(BF)
    slope = half + (0.5 * GELU_C) * pre * (1.0 - tanh * tanh) * (1.0 + 3.0 * GELU_A * square)
    grad_pre = (grad_act * slope).astype(BF)
    grad_up = tn(h, grad_pre)
    grad_down = tn(act, g)
    if not first:
        grad_up = grad_up + aup_ref[...]
        grad_down = grad_down + adown_ref[...]
    dup_ref[...] = grad_up.astype(dup_ref.dtype)
    ddown_ref[...] = grad_down.astype(ddown_ref.dtype)
    out = nn(act, down)
    row = nt(grad_pre, up)

    @pl.when(step == 0)
    def _():
        out_s[...] = out
        row_s[...] = row

    @pl.when(step > 0)
    def _():
        out_s[...] += out
        row_s[...] += row

    @pl.when(step == steps - 1)
    def _():
        here = iota((2 * slots, slots), 0)
        there = position((2 * slots, slots), 1)
        pick = jnp.where(here == there, 1.0, 0.0).astype(BF)
        total = nn(pick, out_s[...].astype(BF))
        pick = jnp.where(here == there + cap, 1.0, 0.0).astype(BF)
        total = total + nn(pick, row_s[...].astype(BF))
        ret_ref[...] = total.astype(BF)


def expert(cap, recv, up, down, earlier):
    first = earlier is None
    total, width = recv.shape
    slots = total // 2
    hidden = up.shape[2]
    tile = 512
    dtype = F32 if first else BF
    up_block = pl.BlockSpec((width, tile), lambda i: (0, i))
    down_block = pl.BlockSpec((tile, width), lambda i: (i, 0))
    in_specs = [
        whole_spec(recv.shape),
        pl.BlockSpec((1, width, tile), lambda i: (0, 0, i)),
        pl.BlockSpec((1, tile, width), lambda i: (0, i, 0)),
    ]
    args = [recv, up, down]
    if not first:
        in_specs += [up_block, down_block]
        args += list(earlier)
    return pl.pallas_call(
        functools.partial(expert_kernel, cap, first),
        grid=(hidden // tile,),
        in_specs=in_specs,
        out_specs=[whole_spec(recv.shape), up_block, down_block],
        out_shape=(
            jax.ShapeDtypeStruct(recv.shape, BF),
            jax.ShapeDtypeStruct((width, hidden), dtype),
            jax.ShapeDtypeStruct((hidden, width), dtype),
        ),
        scratch_shapes=[
            pltpu.VMEM((slots, width), BF),
            pltpu.VMEM((slots, width), BF),
            pltpu.VMEM((slots, width), F32),
            pltpu.VMEM((slots, width), F32),
        ],
        compiler_params=params(56),
        cost_estimate=pl.CostEstimate(
            flops=2 * 12 * slots * width * hidden, bytes_accessed=24 * MB, transcendentals=0
        ),
        name="expert",
    )(*args)


def back_kernel(last, *refs):
    (
        scal_ref,
        ret_ref,
        meta_ref,
        x1_ref,
        lse_ref,
        qkv_ref,
        mixed_ref,
        tok_ref,
        cot_ref,
        wqkv_ref,
        wo_ref,
        g1_ref,
        g2_ref,
        router_ref,
    ) = refs[:14]
    if last:
        in_ref, out_ref, small_ref, _, _, _ = refs[14:20]
        block_ref, dx1_ref, dqkv_ref, send_ref, keep_ref = refs[20:25]
        dmix_s, pay_s = refs[25:]
    else:
        block_ref, dx1_ref, dqkv_ref, in_ref, out_ref, small_ref = refs[14:20]
        (dmix_s,) = refs[20:]
    total = ret_ref.shape[0]
    rows, width = x1_ref.shape
    experts = router_ref.shape[0]
    meta = meta_ref[...]
    gates = [meta[:, k : k + 1] for k in range(2)]
    place = [meta[:, 2 + k : 3 + k].astype(jnp.int32) for k in range(2)]
    picks = [meta[:, 4 + k : 5 + k].astype(jnp.int32) for k in range(2)]
    cap = total // (2 * experts)
    grad_out = cot_ref[0].astype(F32)
    x_mid = x1_ref[...]
    here = iota((rows, total), 1)
    ret = ret_ref[...]
    result = x_mid
    grad_gate = []
    for k in range(2):
        pair = nn(jnp.where(here == place[k], 1.0, 0.0).astype(BF), ret)
        result = result + gates[k] * pair
        grad_gate.append(jnp.sum(grad_out * pair, axis=1, keepdims=True))
    block_ref[0] = result.astype(BF)
    both = (here == place[0] + cap) | (here == place[1] + cap)
    grad_second = nn(jnp.where(both, 1.0, 0.0).astype(BF), ret)
    mean_gate = gates[0] * grad_gate[0] + gates[1] * grad_gate[1]
    lane = iota((rows, experts), 1)
    grad_logits = jnp.zeros((rows, experts), F32)
    for k in range(2):
        grad_pick = gates[k] * (grad_gate[k] - mean_gate)
        grad_logits = grad_logits + jnp.where(lane == picks[k], grad_pick, 0.0)
    grad_logits = grad_logits.astype(BF)
    grad_second = grad_second + nn(grad_logits, router_ref[...])
    normed, factor = normalize(x_mid)
    h_second = (normed * g2_ref[...]).astype(BF)
    small = [
        tn(grad_logits, h_second),
        jnp.sum(grad_second * normed, axis=0, keepdims=True),
    ]
    grad_mid = grad_out + norm_back(grad_second * g2_ref[...], normed, factor)
    dx1_ref[0] = grad_mid
    grad_attn = grad_mid.astype(BF)
    out_grad = tn(mixed_ref[...], grad_attn)
    if not last:
        out_ref[...] = out_grad
        small_ref[0:experts, :] = small[0]
        small_ref[experts : experts + 1, :] = small[1]
    dmix_s[...] = nt(grad_attn, wo_ref[...]).astype(BF)

    def image(i, carry):
        at = pl.ds(pl.multiple_of(i * SEQ, 16), SEQ)
        for g in range(HEADS // GROUP):
            query = spread_heads(head_block(qkv_ref, at, 0, g, width))
            key = head_block(qkv_ref, at, 1, g, width)
            value = head_block(qkv_ref, at, 2, g, width)
            grad_mixed = spread_heads(dmix_s[at, g * GW : (g + 1) * GW])
            scores = nt(key, query) * (HEAD**-0.5)
            probs = jnp.exp(scores - lse_ref[pl.ds(i * (HEADS // GROUP) + g, 1), :])
            grad_probs = nt(value, grad_mixed)
            inner = jnp.sum(probs * grad_probs, axis=0, keepdims=True)
            grad_scores = (probs * (grad_probs - inner)).astype(BF)
            grad_value = nn(probs.astype(BF), grad_mixed)
            grad_key = nn(grad_scores, query) * (HEAD**-0.5)
            grad_query = gather_heads(tn(grad_scores, key)) * (HEAD**-0.5)
            for part, grad in enumerate((grad_query, grad_key, grad_value)):
                start = part * width + g * GW
                dqkv_ref[0, at, start : start + GW] = grad.astype(BF)
        return carry

    lax.fori_loop(0, rows // SEQ, image, 0)

    normed, _ = normalize(tok_ref[0].astype(F32))
    h_first = (normed * g1_ref[...]).astype(BF)
    in_grad = [
        tn(h_first, dqkv_ref[0, :, part * width : (part + 1) * width]) for part in range(3)
    ]
    if not last:
        for part in range(3):
            in_ref[:, part * width : (part + 1) * width] = in_grad[part]
        small_ref[experts + 1 :, :] = jnp.zeros((small_ref.shape[0] - experts - 1, width), F32)
        return

    in_grad = [in_grad[part] + in_ref[:, part * width : (part + 1) * width] for part in range(3)]
    out_grad = out_grad + out_ref[...]
    gain = jnp.zeros((width, 1), F32)
    for part in range(3):
        weight = wqkv_ref[:, part * width : (part + 1) * width].astype(F32)
        gain = gain + jnp.sum(weight * in_grad[part], axis=1, keepdims=True)
    eye = iota((width, width), 0) == iota((width, width), 1)
    gain = jnp.sum(jnp.where(eye, gain, 0.0), axis=0, keepdims=True) / g1_ref[...]
    slots, piece = pay_s.shape[1:3]
    for s in range(2):
        for b in range(2):
            block = (in_grad + [out_grad])[2 * s + b]
            for j in range(width // piece):
                to = (b * (width // piece) + j) ^ scal_ref[s]
                pay_s[s, to] = block[j * piece : (j + 1) * piece].astype(BF)
    router_part = small[0] + small_ref[0:experts, :]
    gain_two = small[1] + small_ref[experts : experts + 1, :]
    half = slots // 2
    span = half * piece
    for s in range(2):
        base = s * (span + SMALL * (experts // 16))
        send_ref[base : base + span, :] = pay_s[s, half:].reshape(span, width)
        keep_ref[base : base + span, :] = pay_s[s, :half].reshape(span, width)
    fill = jnp.zeros((SMALL * (experts // 16) - 2, width), F32)
    low_a = router_part.astype(BF)
    low_b = jnp.concatenate([gain_two, gain, fill], axis=0).astype(BF)
    tail = SMALL * (experts // 16)
    for ref in (send_ref, keep_ref):
        ref[span : span + tail, :] = low_a
        ref[2 * span + tail : 2 * (span + tail), :] = low_b


def back(micro, scal, plan, ret, saved, tokens, cot, wqkv, wo, g1, g2, router_t, earlier):
    last = earlier is not None
    qkv, mixed, x1, lse, meta = saved
    _, rows, width = tokens.shape
    experts = router_t.shape[0]
    slots, piece, tail = plan
    args = [scal, ret, meta, x1, lse, qkv, mixed, tokens, cot, wqkv, wo, g1, g2, router_t]
    in_specs = [pl.BlockSpec(memory_space=pltpu.SMEM)]
    in_specs += [whole_spec(a.shape) for a in args[1:7]]
    in_specs += [micro_spec(tokens.shape, micro), micro_spec(cot.shape, micro)]
    in_specs += [whole_spec(a.shape) for a in args[9:]]
    shapes = [
        jax.ShapeDtypeStruct(tokens.shape, BF),
        jax.ShapeDtypeStruct(tokens.shape, F32),
        jax.ShapeDtypeStruct((MICRO, rows, 3 * width), BF),
    ]
    out_specs = [micro_spec(s.shape, micro) for s in shapes]
    scratch = [pltpu.VMEM((rows, width), BF)]
    aliases = {}
    if last:
        block, dx1, dqkv, in_acc, out_acc, small_acc = earlier
        args += [in_acc, out_acc, small_acc, block, dx1, dqkv]
        in_specs += [whole_spec(a.shape) for a in (in_acc, out_acc, small_acc)]
        in_specs += [pl.BlockSpec(memory_space=pl.ANY)] * 3
        aliases = {17: 0, 18: 1, 19: 2}
        both = 2 * (slots // 2 * piece + tail)
        shapes += [jax.ShapeDtypeStruct((both, width), BF)] * 2
        scratch += [pltpu.VMEM((2, slots, piece, width), BF)]
    else:
        shapes += [
            jax.ShapeDtypeStruct(wqkv.shape, F32),
            jax.ShapeDtypeStruct(wo.shape, F32),
            jax.ShapeDtypeStruct((experts + 8, width), F32),
        ]
    out_specs += [whole_spec(s.shape) for s in shapes[3:]]
    flops = 2 * rows * width * (3 * ret.shape[0] + 12 * width)
    return pl.pallas_call(
        functools.partial(back_kernel, last),
        grid=(1,),
        in_specs=in_specs,
        out_specs=out_specs,
        out_shape=shapes,
        scratch_shapes=scratch,
        input_output_aliases=aliases,
        compiler_params=params(60),
        cost_estimate=pl.CostEstimate(flops=5 * flops, bytes_accessed=20 * MB, transcendentals=0),
        name="back",
    )(*args)


def finish_kernel(dqkv_ref, dx1_ref, tok_ref, wqkv_ref, g1_ref, out_ref):
    grad_first = nt(dqkv_ref[0], wqkv_ref[...])
    normed, factor = normalize(tok_ref[0].astype(F32))
    out_ref[0] = dx1_ref[0] + norm_back(grad_first * g1_ref[...], normed, factor)


def finish(dqkv, dx1, tokens, wqkv, g1):
    _, rows, width = tokens.shape
    each = rows // 2

    def spec(columns):
        return pl.BlockSpec((1, each, columns), lambda i: (i // 2, i % 2, 0))

    return pl.pallas_call(
        finish_kernel,
        grid=(2 * MICRO,),
        in_specs=[
            spec(3 * width),
            spec(width),
            spec(width),
            whole_spec(wqkv.shape),
            whole_spec(g1.shape),
        ],
        out_specs=spec(width),
        out_shape=jax.ShapeDtypeStruct(tokens.shape, F32),
        compiler_params=params(32),
        cost_estimate=pl.CostEstimate(
            flops=2 * MICRO * rows * width * 3 * width, bytes_accessed=10 * MB, transcendentals=0
        ),
        name="finish",
    )(dqkv, dx1, tokens, wqkv, g1)


def local(kernel, shapes, args, scalars=0):
    specs = [pl.BlockSpec(memory_space=pltpu.SMEM)] * scalars
    specs += [pl.BlockSpec(memory_space=pltpu.VMEM)] * (len(args) - scalars)
    size = sum(a.size * 4 for a in args)
    return pl.pallas_call(
        kernel,
        in_specs=specs,
        out_specs=[pl.BlockSpec(memory_space=pltpu.VMEM)] * len(shapes),
        out_shape=shapes,
        compiler_params=params(32),
        cost_estimate=pl.CostEstimate(flops=1000, bytes_accessed=size, transcendentals=0),
    )(*args)


def halve(keep, arrived, count, piece, tail):
    width = keep[0].shape[1]
    half = count // 2 * piece

    def kernel(*refs):
        for s in range(2):
            total = refs[s][...].astype(F32) + refs[2 + s][...].astype(F32)
            total = total.astype(BF)
            send_ref, keep_ref = refs[4 + s], refs[6 + s]
            keep_ref[:half, :] = total[:half]
            keep_ref[half:, :] = total[2 * half :]
            send_ref[...] = total[half:]

    shape = jax.ShapeDtypeStruct((half + tail, width), BF)
    made = local(kernel, [shape] * 4, list(keep) + list(arrived))
    return made[:2], made[2:]


def reduce_all(send, keep, scal, plan, width, experts):
    slots, piece, tail = plan
    size = lax.axis_size("exp")
    bits = size.bit_length() - 1
    first = [1 << b for b in range(bits - 2)]
    second = [first[b ^ 1] if (b ^ 1) < len(first) else first[b] for b in range(len(first))]
    streams = (first, second)
    low, high = 1 << (bits - 2), 1 << (bits - 1)
    groups = [low, high, low | high]

    def swap(value, mask):
        return lax.ppermute(value, "exp", [(i, i ^ mask) for i in range(size)])

    def swap_core(value):
        return lax.ppermute(value, "grp", [(0, 1), (1, 0)])

    got = swap_core(send)
    half = send.shape[0] // 2
    count = slots // 2

    def split(keep_ref, got_ref, *outs):
        half_rows = count // 2 * piece
        for s in range(2):
            at = pl.ds(s * half, half)
            total = keep_ref[at, :].astype(F32) + got_ref[at, :].astype(F32)
            total = total.astype(BF)
            outs[s][...] = total[half_rows:]
            outs[2 + s][:half_rows, :] = total[:half_rows]
            outs[2 + s][half_rows:, :] = total[2 * half_rows :]

    shape = jax.ShapeDtypeStruct((count // 2 * piece + tail, width), BF)
    made = local(split, [shape] * 4, [keep, got])
    sends, keeps = made[:2], made[2:]
    count //= 2
    for step in range(len(first) - 1):
        arrived = [swap(sends[s], streams[s][step]) for s in range(2)]
        sends, keeps = halve(keeps, arrived, count, piece, tail)
        count //= 2
    arrived = [swap(sends[s], streams[s][-1]) for s in range(2)]

    def quarter(*refs):
        for s in range(2):
            total = refs[s][...].astype(F32) + refs[2 + s][...].astype(F32)
            total = total.astype(BF)
            at = pl.ds(s * (piece + tail), piece)
            end = pl.ds(s * (piece + tail) + piece, tail)
            for j in range(4):
                refs[4 + j][at, :] = total[j * piece : (j + 1) * piece]
                refs[4 + j][end, :] = total[4 * piece :]

    shape = jax.ShapeDtypeStruct((2 * (piece + tail), width), BF)
    made = local(quarter, [shape] * 4, list(keeps) + list(arrived))
    arrived = [swap(made[1 + j], groups[j]) for j in range(3)]

    def add_up(a, b, c, d, mine_ref, small_ref):
        total = (a[...].astype(F32) + b[...].astype(F32)) + (c[...].astype(F32) + d[...].astype(F32))
        for s in range(2):
            base = s * (piece + tail)
            mine_ref[s * piece : (s + 1) * piece, :] = total[base : base + piece].astype(BF)
            small_ref[s * tail : (s + 1) * tail, :] = total[base + piece : base + piece + tail]

    mine, small = local(
        add_up,
        [
            jax.ShapeDtypeStruct((2 * piece, width), BF),
            jax.ShapeDtypeStruct((2 * tail, width), F32),
        ],
        [made[0]] + arrived,
    )

    others = [swap(mine, groups[j]) for j in range(3)]

    def lay(a, b, c, d, one_ref, two_ref):
        for j, ref in enumerate((a, b, c, d)):
            one_ref[j * piece : (j + 1) * piece, :] = ref[:piece, :]
            two_ref[j * piece : (j + 1) * piece, :] = ref[piece:, :]

    shape = jax.ShapeDtypeStruct((4 * piece, width), BF)
    have = local(lay, [shape] * 2, [mine] + others)
    for step in reversed(range(len(first))):
        arrived = [swap(have[s], streams[s][step]) for s in range(2)]
        rows = have[0].shape[0]
        if step > 0:

            def join(a, b, c, d, one_ref, two_ref):
                one_ref[:rows, :] = a[...]
                two_ref[:rows, :] = b[...]
                one_ref[rows:, :] = c[...]
                two_ref[rows:, :] = d[...]

            shape = jax.ShapeDtypeStruct((2 * rows, width), BF)
            have = local(join, [shape] * 2, list(have) + list(arrived))

    def join_all(a, b, c, d, one_ref):
        for j, ref in enumerate((a, c, b, d)):
            one_ref[j * rows : (j + 1) * rows, :] = ref[...]

    shape = jax.ShapeDtypeStruct((4 * rows, width), BF)
    (have,) = local(join_all, [shape], list(have) + list(arrived))
    other = swap_core(have)
    each = slots // 2

    def deal(scal_ref, have_ref, other_ref, in_ref, out_ref):
        blocks = width // piece

        def place(s, b, j):
            at = (b * blocks + j) ^ scal_ref[s]
            near = at < each
            start = pl.multiple_of(s * 2 * rows + (at % each) * piece, piece)
            a = have_ref[pl.ds(start, piece), :].astype(F32)
            c = other_ref[pl.ds(start, piece), :].astype(F32)
            return jnp.where(near, a, c)

        def body(j, carry):
            to = pl.ds(pl.multiple_of(j * piece, piece), piece)
            for part in range(3):
                in_ref[to, part * width : (part + 1) * width] = place(part // 2, part % 2, j)
            out_ref[to, :] = place(1, 1, j)
            return carry

        lax.fori_loop(0, blocks, body, 0)

    in_grad, out_grad = local(
        deal,
        [
            jax.ShapeDtypeStruct((width, 3 * width), F32),
            jax.ShapeDtypeStruct((width, width), F32),
        ],
        [scal, have, other],
        scalars=1,
    )
    return in_grad, out_grad, small[tail + 1], small[tail], small[:experts].T


def places(size):
    bits = size.bit_length() - 1
    core = lax.axis_index("grp")
    me = lax.axis_index("exp")
    first = list(range(bits - 2))
    second = [first[b ^ 1] if (b ^ 1) < len(first) else b for b in first]
    made = []
    for order in (first, second):
        value = core
        for b in order:
            value = value * 2 + ((me >> b) & 1)
        made.append(value * 4 + (me >> (bits - 2)))
    return jnp.stack(made).astype(jnp.int32)


def shards(
    tokens,
    expert_picks,
    priority_ranks,
    attn_input,
    attn_output,
    first_gain,
    second_gain,
    router_weight,
    expert_up,
    expert_down,
    cotangent,
):
    size = lax.axis_size("exp")
    experts = router_weight.shape[1]
    rows, width = tokens.shape[1:]
    cap = max(2, rows // size)
    total = experts * 2 * cap
    slots = 2 * size
    plan = (slots, 2 * width // slots, SMALL * (experts // 16))
    scal = places(size)
    picks_t = jnp.transpose(expert_picks, (0, 2, 1))
    router_t = router_weight.T
    g1 = first_gain.reshape(1, width)
    g2 = second_gain.reshape(1, width)

    def exchange(value):
        value = value.reshape(experts, 2 * cap, width)
        value = lax.all_to_all(value, "exp", split_axis=0, concat_axis=0, tiled=True)
        return value.reshape(total, width)

    saved, sent = [], []
    for micro in range(MICRO):
        made = fore(
            micro,
            cap,
            tokens,
            picks_t,
            priority_ranks,
            attn_input,
            attn_output,
            g1,
            g2,
            router_t,
            cotangent,
        )
        sent.append(made[0])
        saved.append(made[1:])
    arrived = [exchange(v) for v in sent]
    answer0, up0, down0 = expert(cap, arrived[0], expert_up, expert_down, None)
    answer1, up1, down1 = expert(cap, arrived[1], expert_up, expert_down, (up0, down0))
    ret = [exchange(v) for v in (answer0, answer1)]
    up_other = lax.ppermute(up1, "grp", [(0, 1), (1, 0)])
    down_other = lax.ppermute(down1, "grp", [(0, 1), (1, 0)])
    up_sum = up1.astype(F32) + up_other.astype(F32)
    down_sum = down1.astype(F32) + down_other.astype(F32)

    weights = (attn_input, attn_output, g1, g2, router_t)
    earlier = back(0, scal, plan, ret[0], saved[0], tokens, cotangent, *weights, None)
    block, dx1, dqkv, send, keep = back(
        1, scal, plan, ret[1], saved[1], tokens, cotangent, *weights, earlier
    )
    tokens_grad = finish(dqkv, dx1, tokens, attn_input, g1)
    dense = reduce_all(send, keep, scal, plan, width, experts)
    return (block, tokens_grad) + dense + (up_sum[None], down_sum[None])


def solution(mesh):
    split = P(None, ("grp", "exp"), None)
    owned = P("exp", None, None)
    in_specs = (split,) * 3 + (P(),) * 5 + (owned, owned, split)
    out_specs = (split, split) + (P(),) * 5 + (owned, owned)
    return jax.shard_map(shards, mesh=mesh, in_specs=in_specs, out_specs=out_specs, check_vma=False)
```

```python
import functools

import jax
import jax.numpy as jnp
from jax import lax
from jax.experimental import pallas as pl
from jax.experimental.pallas import tpu as pltpu
from jax.sharding import PartitionSpec as P

HEADS = 8
HEAD = 64
SEQ = 144
MICRO = 2
EPS = 1e-06
GROUP = 4
GW = GROUP * HEAD
GELU_C = 0.7978845608028654
GELU_A = 0.044715
SMALL = 16

BF = jnp.bfloat16
F32 = jnp.float32
MB = 1 << 20
FORE_MB = 60
BACK_MB = 60
FILLS = 4
IN_VMEM = pl.BlockSpec(memory_space=pltpu.VMEM)
IN_HBM = pl.BlockSpec(memory_space=pltpu.HBM)


def nn(a, b):
    return lax.dot_general(a, b, (((1,), (0,)), ((), ())), preferred_element_type=F32)


def nt(a, b):
    return lax.dot_general(a, b, (((1,), (1,)), ((), ())), preferred_element_type=F32)


def tn(a, b):
    return lax.dot_general(a, b, (((0,), (0,)), ((), ())), preferred_element_type=F32)


def normalize(values):
    center = values - jnp.mean(values, axis=-1, keepdims=True)
    factor = lax.rsqrt(jnp.mean(center * center, axis=-1, keepdims=True) + EPS)
    return center * factor, factor


def norm_back(grad_normed, normed, factor):
    return factor * (
        grad_normed
        - jnp.mean(grad_normed, axis=-1, keepdims=True)
        - normed * jnp.mean(grad_normed * normed, axis=-1, keepdims=True)
    )


def iota(shape, dim):
    return lax.broadcasted_iota(jnp.int32, shape, dim)


def spread_heads(block):
    head = iota(block.shape, 1) // HEAD
    zero = jnp.zeros_like(block)
    return jnp.concatenate([jnp.where(head == h, block, zero) for h in range(GROUP)], axis=0)


def gather_heads(full):
    rows = full.shape[0] // GROUP
    head = iota((rows, full.shape[1]), 1) // HEAD
    total = jnp.where(head == 0, full[:rows], 0.0)
    for h in range(1, GROUP):
        total = total + jnp.where(head == h, full[h * rows : (h + 1) * rows], 0.0)
    return total


def head_block(ref, rows, part, group, width):
    start = part * width + group * GW
    return ref[rows, start : start + GW]


def fore_kernel(cap, micro, *refs):
    tok_h, pick_h, rank_h, wqkv_h, wo_h, g1_h, g2_h, router_h, cot_h = refs[:9]
    send_h, qkv_h, mixed_h, x1_h, lse_h, meta_h = refs[9:15]
    tok_ref, pick_ref, rank_ref, wqkv_ref, wo_ref, g1_ref, g2_ref, router_ref, cot_ref = refs[15:24]
    send_ref, qkv_ref, mixed_ref, x1_ref, lse_ref, meta_ref = refs[24:30]
    h2_s, d0_s, d1_s, in_sem, out_sem = refs[30:]
    rows, width = x1_ref.shape
    experts = router_ref.shape[0]
    images = rows // SEQ
    pairs = (
        (pick_h.at[micro], pick_ref),
        (rank_h.at[micro], rank_ref),
        (tok_h.at[micro], tok_ref),
        (g1_h, g1_ref),
        (wqkv_h, wqkv_ref),
        (wo_h, wo_ref),
        (g2_h, g2_ref),
        (router_h, router_ref),
        (cot_h.at[micro], cot_ref),
    )
    loads = [move(a, b, in_sem.at[n]) for n, (a, b) in enumerate(pairs)]

    loads[0].wait()
    loads[1].wait()
    rank_row = rank_ref[...].astype(F32)
    eye = iota((rows, rows), 0) == iota((rows, rows), 1)
    rank_col = jnp.sum(jnp.where(eye, rank_row, 0.0), axis=1, keepdims=True)
    less = jnp.where(rank_col < rank_row, 1.0, 0.0).astype(BF)
    picks = pick_ref[...]
    expert = iota((experts, rows), 0)
    on = [jnp.where(expert == picks[k : k + 1], 1.0, 0.0) for k in range(2)]
    before = [nn(on[k].astype(BF), less) for k in range(2)]
    before[1] = before[1] + jnp.sum(on[0], axis=1, keepdims=True)
    place = []
    for k in range(2):
        slot = jnp.sum(on[k] * before[k], axis=0, keepdims=True)
        base = picks[k : k + 1].astype(F32) * (2 * cap)
        place.append(jnp.where(slot < cap - 0.5, base + slot, -9999.0))

    loads[2].wait()
    loads[3].wait()
    x_in = tok_ref[...].astype(F32)
    normed, _ = normalize(x_in)
    h_first = (normed * g1_ref[...]).astype(BF)
    loads[4].wait()
    qkv_ref[...] = nn(h_first, wqkv_ref[...]).astype(BF)
    stores = [move(qkv_ref, qkv_h, out_sem.at[1])]

    def image(i, carry):
        at = pl.ds(pl.multiple_of(i * SEQ, 16), SEQ)
        for g in range(HEADS // GROUP):
            query = spread_heads(head_block(qkv_ref, at, 0, g, width))
            key = head_block(qkv_ref, at, 1, g, width)
            value = head_block(qkv_ref, at, 2, g, width)
            scores = nt(key, query) * (HEAD**-0.5)
            peak = jnp.max(scores, axis=0, keepdims=True)
            expo = jnp.exp(scores - peak)
            denom = jnp.sum(expo, axis=0, keepdims=True)
            probs_low = (expo * (1.0 / denom)).astype(BF)
            lse_ref[pl.ds(i * (HEADS // GROUP) + g, 1), :] = peak + jnp.log(denom)
            mixed = gather_heads(tn(probs_low, value))
            mixed_ref[at, g * GW : (g + 1) * GW] = mixed.astype(BF)
        return carry

    lax.fori_loop(0, images, image, 0)

    stores.append(move(mixed_ref, mixed_h, out_sem.at[2]))
    stores.append(move(lse_ref, lse_h, out_sem.at[4]))

    for n in range(5, 9):
        loads[n].wait()
    x_mid = tok_ref[...].astype(F32) + nn(mixed_ref[...], wo_ref[...])
    x1_ref[...] = x_mid
    stores.append(move(x1_ref, x1_h, out_sem.at[3]))
    normed, _ = normalize(x_mid)
    h_second = (normed * g2_ref[...]).astype(BF)
    h2_s[...] = h_second
    logits = nt(router_ref[...], h_second)
    picked = [jnp.sum(on[k] * logits, axis=0, keepdims=True) for k in range(2)]
    top = jnp.maximum(picked[0], picked[1])
    expo = [jnp.exp(v - top) for v in picked]
    total = expo[0] + expo[1]
    gates = [v / total for v in expo]
    stack = jnp.concatenate(
        gates + place + [picks.astype(F32)] + [jnp.zeros((2, rows), F32)], axis=0
    )
    meta = jnp.transpose(stack)
    meta_ref[...] = meta
    stores.append(move(meta_ref, meta_h, out_sem.at[5]))
    grad_out = cot_ref[...].astype(F32)
    d0_s[...] = (meta[:, 0:1] * grad_out).astype(BF)
    d1_s[...] = (meta[:, 1:2] * grad_out).astype(BF)
    place = [v.astype(jnp.int32) for v in place]

    step = send_ref.shape[0] // FILLS
    for c in range(FILLS):
        start = c * step
        row = iota((step, rows), 0) + start
        one = jnp.ones((step, rows), F32)
        zero = jnp.zeros((step, rows), F32)
        first = jnp.where((row == place[0]) | (row == place[1]), one, zero).astype(BF)
        part = nn(first, h2_s[...])
        part = part + nn(jnp.where(row == place[0] + cap, one, zero).astype(BF), d0_s[...])
        part = part + nn(jnp.where(row == place[1] + cap, one, zero).astype(BF), d1_s[...])
        send_ref[pl.ds(start, step), :] = part.astype(BF)
        at = pl.ds(start, step)
        stores.append(move(send_ref.at[at], send_h.at[at], out_sem.at[6 + c]))
    for copy in stores:
        copy.wait()


def move(source, target, sem):
    copy = pltpu.make_async_copy(source, target, sem)
    copy.start()
    return copy


def micro_spec(shape, micro):
    return pl.BlockSpec((1,) + tuple(shape[1:]), lambda i: (micro,) + (0,) * (len(shape) - 1))


def whole_spec(shape):
    return pl.BlockSpec(tuple(shape), lambda i: (0,) * len(shape))


def params(limit, **more):
    return pltpu.CompilerParams(vmem_limit_bytes=limit * MB, **more)


def fore(micro, cap, tokens, picks_t, ranks, wqkv, wo, g1, g2, router_t, cot):
    _, rows, width = tokens.shape
    experts = router_t.shape[0]
    out_shape = (
        jax.ShapeDtypeStruct((experts * 2 * cap, width), BF),
        jax.ShapeDtypeStruct((rows, 3 * width), BF),
        jax.ShapeDtypeStruct((rows, width), BF),
        jax.ShapeDtypeStruct((rows, width), F32),
        jax.ShapeDtypeStruct((8, GROUP * SEQ), F32),
        jax.ShapeDtypeStruct((rows, 8), F32),
    )
    flops = 2 * rows * width * (4 * width + 3 * experts * 2 * cap + 4 * SEQ)
    return pl.pallas_call(
        functools.partial(fore_kernel, cap, micro),
        in_specs=[IN_HBM] * 9,
        out_specs=[IN_HBM] * 6,
        out_shape=out_shape,
        scratch_shapes=[
            pltpu.VMEM((rows, width), BF),
            pltpu.VMEM(picks_t.shape[1:], jnp.int32),
            pltpu.VMEM(ranks.shape[1:], jnp.int32),
            pltpu.VMEM(wqkv.shape, BF),
            pltpu.VMEM(wo.shape, BF),
            pltpu.VMEM(g1.shape, F32),
            pltpu.VMEM(g2.shape, F32),
            pltpu.VMEM(router_t.shape, BF),
            pltpu.VMEM((rows, width), BF),
        ]
        + [pltpu.VMEM(v.shape, v.dtype) for v in out_shape]
        + [pltpu.VMEM((rows, width), BF) for _ in range(3)]
        + [pltpu.SemaphoreType.DMA((9,)), pltpu.SemaphoreType.DMA((6 + FILLS,))],
        compiler_params=params(FORE_MB),
        cost_estimate=pl.CostEstimate(flops=4 * flops, bytes_accessed=8 * MB, transcendentals=0),
        name="fore",
    )(tokens, picks_t, ranks, wqkv, wo, g1, g2, router_t, cot)


def expert_kernel(cap, first, *refs):
    if first:
        recv_ref, up_ref, down_ref, ret_ref, dup_ref, ddown_ref = refs[:6]
    else:
        recv_ref, up_ref, down_ref, aup_ref, adown_ref, ret_ref, dup_ref, ddown_ref = refs[:8]
    h_s, g_s, out_s, row_s = refs[-4:]
    step = pl.program_id(0)
    steps = pl.num_programs(0)
    slots = h_s.shape[0]

    def position(shape, dim):
        slot = iota(shape, dim)
        block = ((slot.astype(F32) + 0.5) * (1.0 / cap)).astype(jnp.int32)
        return slot + block * cap

    @pl.when(step == 0)
    def _():
        here = iota((slots, 2 * slots), 1)
        there = position((slots, 2 * slots), 0)
        pick = jnp.where(here == there, 1.0, 0.0).astype(BF)
        h_s[...] = nn(pick, recv_ref[...]).astype(BF)
        pick = jnp.where(here == there + cap, 1.0, 0.0).astype(BF)
        g_s[...] = nn(pick, recv_ref[...]).astype(BF)

    up = up_ref[0]
    down = down_ref[0]
    h = h_s[...]
    g = g_s[...]
    pre = nn(h, up)
    grad_act = nt(g, down)
    square = pre * pre
    tanh = jnp.tanh(GELU_C * pre * (1.0 + GELU_A * square))
    half = 0.5 + 0.5 * tanh
    act = (pre * half).astype(BF)
    slope = half + (0.5 * GELU_C) * pre * (1.0 - tanh * tanh) * (1.0 + 3.0 * GELU_A * square)
    grad_pre = (grad_act * slope).astype(BF)
    grad_up = tn(h, grad_pre)
    grad_down = tn(act, g)
    if not first:
        grad_up = grad_up + aup_ref[...]
        grad_down = grad_down + adown_ref[...]
    dup_ref[...] = grad_up.astype(dup_ref.dtype)
    ddown_ref[...] = grad_down.astype(ddown_ref.dtype)
    out = nn(act, down)
    row = nt(grad_pre, up)

    @pl.when(step == 0)
    def _():
        out_s[...] = out
        row_s[...] = row

    @pl.when(step > 0)
    def _():
        out_s[...] += out
        row_s[...] += row

    @pl.when(step == steps - 1)
    def _():
        here = iota((2 * slots, slots), 0)
        there = position((2 * slots, slots), 1)
        pick = jnp.where(here == there, 1.0, 0.0).astype(BF)
        total = nn(pick, out_s[...].astype(BF))
        pick = jnp.where(here == there + cap, 1.0, 0.0).astype(BF)
        total = total + nn(pick, row_s[...].astype(BF))
        ret_ref[...] = total.astype(BF)


def expert(cap, recv, up, down, earlier):
    first = earlier is None
    total, width = recv.shape
    slots = total // 2
    hidden = up.shape[2]
    tile = 512
    dtype = F32 if first else BF
    up_block = pl.BlockSpec((width, tile), lambda i: (0, i))
    down_block = pl.BlockSpec((tile, width), lambda i: (i, 0))
    in_specs = [
        whole_spec(recv.shape),
        pl.BlockSpec((1, width, tile), lambda i: (0, 0, i)),
        pl.BlockSpec((1, tile, width), lambda i: (0, i, 0)),
    ]
    args = [recv, up, down]
    if not first:
        in_specs += [up_block, down_block]
        args += list(earlier)
    return pl.pallas_call(
        functools.partial(expert_kernel, cap, first),
        grid=(hidden // tile,),
        in_specs=in_specs,
        out_specs=[whole_spec(recv.shape), up_block, down_block],
        out_shape=(
            jax.ShapeDtypeStruct(recv.shape, BF),
            jax.ShapeDtypeStruct((width, hidden), dtype),
            jax.ShapeDtypeStruct((hidden, width), dtype),
        ),
        scratch_shapes=[
            pltpu.VMEM((slots, width), BF),
            pltpu.VMEM((slots, width), BF),
            pltpu.VMEM((slots, width), F32),
            pltpu.VMEM((slots, width), F32),
        ],
        compiler_params=params(60),
        cost_estimate=pl.CostEstimate(
            flops=2 * 12 * slots * width * hidden, bytes_accessed=24 * MB, transcendentals=0
        ),
        name="expert",
    )(*args)


def back_kernel(last, micro, *refs):
    take = list(refs)

    def next_refs(count):
        taken, take[:] = take[:count], take[count:]
        return taken

    (scal_ref,) = next_refs(1)
    sources = next_refs(13)
    earlier_h = next_refs(4) if last else []
    block_h, dx1_h, dqkv_h = next_refs(3)
    made_h = next_refs(2 if last else 3)
    held = next_refs(13)
    (
        ret_ref,
        meta_ref,
        x1_ref,
        cot_ref,
        g2_ref,
        router_ref,
        mixed_ref,
        wo_ref,
        qkv_ref,
        lse_ref,
        tok_ref,
        g1_ref,
        wqkv_ref,
    ) = held
    in_ref, out_ref, small_ref = next_refs(3)
    block_ref, dx1_ref, dqkv_ref, dmix_s, in_sem, out_sem = next_refs(6)
    if last:
        send_ref, keep_ref, pay_s = next_refs(3)
    sources = [h.at[micro] if h.shape[0] == MICRO else h for h in sources]
    pairs = list(zip(sources, held))
    if last:
        pairs += list(zip(earlier_h[:3], (in_ref, out_ref, small_ref)))
    loads = [move(a, b, in_sem.at[n]) for n, (a, b) in enumerate(pairs[:6])]
    stores = []
    total = ret_ref.shape[0]
    rows, width = x1_ref.shape
    experts = router_ref.shape[0]
    for n in range(4):
        loads[n].wait()
    loads += [move(a, b, in_sem.at[6 + n]) for n, (a, b) in enumerate(pairs[6:])]
    meta = meta_ref[...]
    gates = [meta[:, k : k + 1] for k in range(2)]
    place = [meta[:, 2 + k : 3 + k].astype(jnp.int32) for k in range(2)]
    picks = [meta[:, 4 + k : 5 + k].astype(jnp.int32) for k in range(2)]
    cap = total // (2 * experts)
    grad_out = cot_ref[...].astype(F32)
    x_mid = x1_ref[...]
    here = iota((rows, total), 1)
    ret = ret_ref[...]
    result = x_mid
    grad_gate = []
    for k in range(2):
        pair = nn(jnp.where(here == place[k], 1.0, 0.0).astype(BF), ret)
        result = result + gates[k] * pair
        grad_gate.append(jnp.sum(grad_out * pair, axis=1, keepdims=True))
    block_ref[...] = result.astype(BF)
    stores.append(move(block_ref, block_h.at[micro], out_sem.at[0]))
    both = (here == place[0] + cap) | (here == place[1] + cap)
    grad_second = nn(jnp.where(both, 1.0, 0.0).astype(BF), ret)
    loads[4].wait()
    loads[5].wait()
    mean_gate = gates[0] * grad_gate[0] + gates[1] * grad_gate[1]
    lane = iota((rows, experts), 1)
    grad_logits = jnp.zeros((rows, experts), F32)
    for k in range(2):
        grad_pick = gates[k] * (grad_gate[k] - mean_gate)
        grad_logits = grad_logits + jnp.where(lane == picks[k], grad_pick, 0.0)
    grad_logits = grad_logits.astype(BF)
    grad_second = grad_second + nn(grad_logits, router_ref[...])
    normed, factor = normalize(x_mid)
    h_second = (normed * g2_ref[...]).astype(BF)
    small = [
        tn(grad_logits, h_second),
        jnp.sum(grad_second * normed, axis=0, keepdims=True),
    ]
    grad_mid = grad_out + norm_back(grad_second * g2_ref[...], normed, factor)
    dx1_ref[...] = grad_mid
    stores.append(move(dx1_ref, dx1_h, out_sem.at[1]))
    for n in range(6, 10):
        loads[n].wait()
    grad_attn = grad_mid.astype(BF)
    out_grad = tn(mixed_ref[...], grad_attn)
    if not last:
        out_ref[...] = out_grad
        small_ref[0:experts, :] = small[0]
        small_ref[experts : experts + 1, :] = small[1]
        small_ref[experts + 1 :, :] = jnp.zeros((small_ref.shape[0] - experts - 1, width), F32)
        stores.append(move(out_ref, made_h[1], out_sem.at[4]))
        stores.append(move(small_ref, made_h[2], out_sem.at[5]))
    dmix_s[...] = nt(grad_attn, wo_ref[...]).astype(BF)

    def image(i, carry):
        at = pl.ds(pl.multiple_of(i * SEQ, 16), SEQ)
        for g in range(HEADS // GROUP):
            query = spread_heads(head_block(qkv_ref, at, 0, g, width))
            key = head_block(qkv_ref, at, 1, g, width)
            value = head_block(qkv_ref, at, 2, g, width)
            grad_mixed = spread_heads(dmix_s[at, g * GW : (g + 1) * GW])
            scores = nt(key, query) * (HEAD**-0.5)
            probs = jnp.exp(scores - lse_ref[pl.ds(i * (HEADS // GROUP) + g, 1), :])
            grad_probs = nt(value, grad_mixed)
            inner = jnp.sum(probs * grad_probs, axis=0, keepdims=True)
            grad_scores = (probs * (grad_probs - inner)).astype(BF)
            grad_value = nn(probs.astype(BF), grad_mixed)
            grad_key = nn(grad_scores, query) * (HEAD**-0.5)
            grad_query = gather_heads(tn(grad_scores, key)) * (HEAD**-0.5)
            for part, grad in enumerate((grad_query, grad_key, grad_value)):
                start = part * width + g * GW
                dqkv_ref[at, start : start + GW] = grad.astype(BF)
        return carry

    lax.fori_loop(0, rows // SEQ, image, 0)

    stores.append(move(dqkv_ref, dqkv_h, out_sem.at[2]))
    for copy in loads[10:]:
        copy.wait()
    normed, _ = normalize(tok_ref[...].astype(F32))
    h_first = (normed * g1_ref[...]).astype(BF)
    in_grad = [
        tn(h_first, dqkv_ref[:, part * width : (part + 1) * width]) for part in range(3)
    ]
    if not last:
        for part in range(3):
            in_ref[:, part * width : (part + 1) * width] = in_grad[part]
        stores.append(move(in_ref, made_h[0], out_sem.at[3]))
        for copy in stores:
            copy.wait()
        return

    in_grad = [in_grad[part] + in_ref[:, part * width : (part + 1) * width] for part in range(3)]
    out_grad = out_grad + out_ref[...]
    gain = jnp.zeros((width, 1), F32)
    for part in range(3):
        weight = wqkv_ref[:, part * width : (part + 1) * width].astype(F32)
        gain = gain + jnp.sum(weight * in_grad[part], axis=1, keepdims=True)
    eye = iota((width, width), 0) == iota((width, width), 1)
    gain = jnp.sum(jnp.where(eye, gain, 0.0), axis=0, keepdims=True) / g1_ref[...]
    slots, piece = pay_s.shape[1:3]
    for s in range(2):
        for b in range(2):
            block = (in_grad + [out_grad])[2 * s + b]
            for j in range(width // piece):
                to = (b * (width // piece) + j) ^ scal_ref[s]
                pay_s[s, to] = block[j * piece : (j + 1) * piece].astype(BF)
    router_part = small[0] + small_ref[0:experts, :]
    gain_two = small[1] + small_ref[experts : experts + 1, :]
    half = slots // 2
    span = half * piece
    for s in range(2):
        base = s * (span + SMALL * (experts // 16))
        send_ref[base : base + span, :] = pay_s[s, half:].reshape(span, width)
        keep_ref[base : base + span, :] = pay_s[s, :half].reshape(span, width)
    fill = jnp.zeros((SMALL * (experts // 16) - 2, width), F32)
    low_a = router_part.astype(BF)
    low_b = jnp.concatenate([gain_two, gain, fill], axis=0).astype(BF)
    tail = SMALL * (experts // 16)
    for ref in (send_ref, keep_ref):
        ref[span : span + tail, :] = low_a
        ref[2 * span + tail : 2 * (span + tail), :] = low_b
    stores.append(move(send_ref, made_h[0], out_sem.at[3]))
    stores.append(move(keep_ref, made_h[1], out_sem.at[4]))
    for copy in stores:
        copy.wait()


def back(micro, scal, plan, ret, saved, tokens, cot, wqkv, wo, g1, g2, router_t, earlier):
    last = earlier is not None
    qkv, mixed, x1, lse, meta = saved
    _, rows, width = tokens.shape
    experts = router_t.shape[0]
    slots, piece, tail = plan
    ins = [ret, meta, x1, cot, g2, router_t, mixed, wo, qkv, lse, tokens, g1, wqkv]
    shapes = [
        jax.ShapeDtypeStruct(tokens.shape, BF),
        jax.ShapeDtypeStruct((rows, width), F32),
        jax.ShapeDtypeStruct((rows, 3 * width), BF),
    ]
    sums = [
        jax.ShapeDtypeStruct(wqkv.shape, F32),
        jax.ShapeDtypeStruct(wo.shape, F32),
        jax.ShapeDtypeStruct((experts + 8, width), F32),
    ]

    def hold(value):
        shape = value.shape[1:] if value.shape[0] == MICRO else value.shape
        return pltpu.VMEM(shape, value.dtype)

    scratch = [hold(a) for a in ins + sums + shapes]
    scratch += [
        pltpu.VMEM((rows, width), BF),
        pltpu.SemaphoreType.DMA((16,)),
        pltpu.SemaphoreType.DMA((6,)),
    ]
    aliases = {}
    if last:
        block, *sums = earlier
        args = [scal] + ins + sums + [block]
        aliases = {17: 0}
        both = 2 * (slots // 2 * piece + tail)
        pay = jax.ShapeDtypeStruct((both, width), BF)
        shapes += [pay, pay]
        scratch += [hold(pay), hold(pay), pltpu.VMEM((2, slots, piece, width), BF)]
    else:
        args = [scal] + ins
        shapes += sums
    in_specs = [pl.BlockSpec(memory_space=pltpu.SMEM)] + [IN_HBM] * (len(args) - 1)
    out_specs = [IN_HBM] * len(shapes)
    flops = 2 * rows * width * (3 * ret.shape[0] + 12 * width)
    return pl.pallas_call(
        functools.partial(back_kernel, last, micro),
        in_specs=in_specs,
        out_specs=out_specs,
        out_shape=shapes,
        scratch_shapes=scratch,
        input_output_aliases=aliases,
        compiler_params=params(BACK_MB),
        cost_estimate=pl.CostEstimate(flops=5 * flops, bytes_accessed=20 * MB, transcendentals=0),
        name="back",
    )(*args)


def finish_kernel(dqkv0, dqkv1, dx0, dx1, tok_ref, wqkv_ref, g1_ref, out_ref):
    def one(dqkv_ref, dx1_ref):
        grad_first = nt(dqkv_ref[...], wqkv_ref[...])
        normed, factor = normalize(tok_ref[0].astype(F32))
        out_ref[0] = dx1_ref[...] + norm_back(grad_first * g1_ref[...], normed, factor)

    @pl.when(pl.program_id(0) < 2)
    def _():
        one(dqkv0, dx0)

    @pl.when(pl.program_id(0) >= 2)
    def _():
        one(dqkv1, dx1)


def finish(dqkv, dx1, tokens, wqkv, g1):
    _, rows, width = tokens.shape
    each = rows // 2

    def early(columns):
        return pl.BlockSpec((each, columns), lambda i: (jnp.minimum(i, 1), 0))

    def late(columns):
        return pl.BlockSpec((each, columns), lambda i: (jnp.maximum(i - 2, 0), 0))

    both = pl.BlockSpec((1, each, width), lambda i: (i // 2, i % 2, 0))
    return pl.pallas_call(
        finish_kernel,
        grid=(2 * MICRO,),
        in_specs=[
            early(3 * width),
            late(3 * width),
            early(width),
            late(width),
            both,
            whole_spec(wqkv.shape),
            whole_spec(g1.shape),
        ],
        out_specs=both,
        out_shape=jax.ShapeDtypeStruct(tokens.shape, F32),
        compiler_params=params(16),
        cost_estimate=pl.CostEstimate(
            flops=2 * MICRO * rows * width * 3 * width, bytes_accessed=10 * MB, transcendentals=0
        ),
        name="finish",
    )(*dqkv, *dx1, tokens, wqkv, g1)


def local(kernel, shapes, args, scalars=0, scratch=()):
    specs = [pl.BlockSpec(memory_space=pltpu.SMEM)] * scalars
    specs += [pl.BlockSpec(memory_space=pltpu.VMEM)] * (len(args) - scalars)
    size = sum(a.size * 4 for a in args)
    return pl.pallas_call(
        kernel,
        in_specs=specs,
        out_specs=[pl.BlockSpec(memory_space=pltpu.VMEM)] * len(shapes),
        out_shape=shapes,
        scratch_shapes=list(scratch),
        compiler_params=params(32),
        cost_estimate=pl.CostEstimate(flops=1000, bytes_accessed=size, transcendentals=0),
    )(*args)


def halve(keep, arrived, count, piece, tail):
    width = keep[0].shape[1]
    half = count // 2 * piece

    def kernel(*refs):
        for s in range(2):
            total = refs[s][...].astype(F32) + refs[2 + s][...].astype(F32)
            total = total.astype(BF)
            send_ref, keep_ref = refs[4 + s], refs[6 + s]
            keep_ref[:half, :] = total[:half]
            keep_ref[half:, :] = total[2 * half :]
            send_ref[...] = total[half:]

    shape = jax.ShapeDtypeStruct((half + tail, width), BF)
    made = local(kernel, [shape] * 4, list(keep) + list(arrived))
    return made[:2], made[2:]


def reduce_all(send, keep, scal, plan, width, experts, beside):
    slots, piece, tail = plan
    size = lax.axis_size("exp")
    bits = size.bit_length() - 1
    first = [1 << b for b in range(bits - 2)]
    second = [first[b ^ 1] if (b ^ 1) < len(first) else first[b] for b in range(len(first))]
    streams = (first, second)
    low, high = 1 << (bits - 2), 1 << (bits - 1)
    groups = [low, high, low | high]

    def swap(value, mask):
        return lax.ppermute(value, "exp", [(i, i ^ mask) for i in range(size)])

    def swap_core(value):
        return lax.ppermute(value, "grp", [(0, 1), (1, 0)])

    got = swap_core(send)
    half = send.shape[0] // 2
    count = slots // 2

    def split(keep_ref, got_ref, *outs):
        half_rows = count // 2 * piece
        for s in range(2):
            at = pl.ds(s * half, half)
            total = keep_ref[at, :].astype(F32) + got_ref[at, :].astype(F32)
            total = total.astype(BF)
            outs[s][...] = total[half_rows:]
            outs[2 + s][:half_rows, :] = total[:half_rows]
            outs[2 + s][half_rows:, :] = total[2 * half_rows :]

    shape = jax.ShapeDtypeStruct((count // 2 * piece + tail, width), BF)
    made = local(split, [shape] * 4, [keep, got])
    sends, keeps = made[:2], made[2:]
    count //= 2
    extra = [work() for work in beside]
    for step in range(len(first) - 1):
        arrived = [swap(sends[s], streams[s][step]) for s in range(2)]
        if step == 0:
            *arrived, extra[0] = lax.optimization_barrier((*arrived, extra[0]))
        sends, keeps = halve(keeps, arrived, count, piece, tail)
        count //= 2
    arrived = [swap(sends[s], streams[s][-1]) for s in range(2)]

    share = 2 * tail // 4
    span = 2 * piece + share

    def quarter(scal_ref, *refs):
        made = []
        for s in range(2):
            total = refs[s][...].astype(F32) + refs[2 + s][...].astype(F32)
            total = total.astype(BF)
            for j in range(4):
                refs[4 + j][s * piece : (s + 1) * piece, :] = total[j * piece : (j + 1) * piece]
            made.append(total[4 * piece :].astype(F32))
        small_s = refs[8]
        small_s[...] = jnp.concatenate(made, axis=0)
        for j in range(4):
            part = pl.multiple_of((scal_ref[2] ^ j) * share, share)
            refs[4 + j][2 * piece :, :] = small_s[pl.ds(part, share), :].astype(BF)

    shape = jax.ShapeDtypeStruct((span, width), BF)
    made = local(
        quarter,
        [shape] * 4,
        [scal] + list(keeps) + list(arrived),
        scalars=1,
        scratch=[pltpu.VMEM((2 * tail, width), F32)],
    )
    arrived = [swap(made[1 + j], groups[j]) for j in range(3)]
    *arrived, extra[1] = lax.optimization_barrier((*arrived, extra[1]))

    def add_up(a, b, c, d, mine_ref):
        total = (a[...].astype(F32) + b[...].astype(F32)) + (c[...].astype(F32) + d[...].astype(F32))
        mine_ref[...] = total.astype(BF)

    (mine,) = local(add_up, [shape], [made[0]] + arrived)

    others = [swap(mine, groups[j]) for j in range(3)]

    def lay(scal_ref, a, b, c, d, one_ref, two_ref, small_ref):
        for j, ref in enumerate((a, b, c, d)):
            one_ref[j * piece : (j + 1) * piece, :] = ref[:piece, :]
            two_ref[j * piece : (j + 1) * piece, :] = ref[piece : 2 * piece, :]
            part = pl.multiple_of((scal_ref[2] ^ j) * share, share)
            small_ref[pl.ds(part, share), :] = ref[2 * piece :, :].astype(F32)

    shape = jax.ShapeDtypeStruct((4 * piece, width), BF)
    *have, small = local(
        lay,
        [shape] * 2 + [jax.ShapeDtypeStruct((2 * tail, width), F32)],
        [scal, mine] + others,
        scalars=1,
    )
    vectors = (small[tail + 1], small[tail], small[:experts].T)
    for step in reversed(range(len(first))):
        arrived = [swap(have[s], streams[s][step]) for s in range(2)]
        rows = have[0].shape[0]
        if step == len(first) - 1:
            *arrived, vectors = lax.optimization_barrier((*arrived, vectors))
        if step == 0:
            *arrived, extra[2] = lax.optimization_barrier((*arrived, extra[2]))
        if step > 0:

            def join(a, b, c, d, one_ref, two_ref):
                one_ref[:rows, :] = a[...]
                two_ref[:rows, :] = b[...]
                one_ref[rows:, :] = c[...]
                two_ref[rows:, :] = d[...]

            shape = jax.ShapeDtypeStruct((2 * rows, width), BF)
            have = local(join, [shape] * 2, list(have) + list(arrived))

    def join_all(a, b, c, d, one_ref):
        for j, ref in enumerate((a, c, b, d)):
            one_ref[j * rows : (j + 1) * rows, :] = ref[...]

    shape = jax.ShapeDtypeStruct((4 * rows, width), BF)
    (have,) = local(join_all, [shape], list(have) + list(arrived))
    other = swap_core(have)
    each = slots // 2

    def deal(scal_ref, have_ref, other_ref, in_ref, out_ref):
        blocks = width // piece

        def place(s, b, j):
            at = (b * blocks + j) ^ scal_ref[s]
            near = at < each
            start = pl.multiple_of(s * 2 * rows + (at % each) * piece, piece)
            a = have_ref[pl.ds(start, piece), :].astype(F32)
            c = other_ref[pl.ds(start, piece), :].astype(F32)
            return jnp.where(near, a, c)

        def body(j, carry):
            to = pl.ds(pl.multiple_of(j * piece, piece), piece)
            for part in range(3):
                in_ref[to, part * width : (part + 1) * width] = place(part // 2, part % 2, j)
            out_ref[to, :] = place(1, 1, j)
            return carry

        lax.fori_loop(0, blocks, body, 0)

    in_grad, out_grad = local(
        deal,
        [
            jax.ShapeDtypeStruct((width, 3 * width), F32),
            jax.ShapeDtypeStruct((width, width), F32),
        ],
        [scal, have, other],
        scalars=1,
    )
    return in_grad, out_grad, *vectors, *extra


def places(size):
    bits = size.bit_length() - 1
    core = lax.axis_index("grp")
    me = lax.axis_index("exp")
    first = list(range(bits - 2))
    second = [first[b ^ 1] if (b ^ 1) < len(first) else b for b in first]
    made = []
    for order in (first, second):
        value = core
        for b in order:
            value = value * 2 + ((me >> b) & 1)
        made.append(value * 4 + (me >> (bits - 2)))
    made.append(me >> (bits - 2))
    return jnp.stack(made).astype(jnp.int32)


def shards(
    tokens,
    expert_picks,
    priority_ranks,
    attn_input,
    attn_output,
    first_gain,
    second_gain,
    router_weight,
    expert_up,
    expert_down,
    cotangent,
):
    size = lax.axis_size("exp")
    experts = router_weight.shape[1]
    rows, width = tokens.shape[1:]
    cap = max(2, rows // size)
    total = experts * 2 * cap
    slots = 2 * size
    plan = (slots, 2 * width // slots, SMALL * (experts // 16))
    scal = places(size)
    picks_t = jnp.transpose(expert_picks, (0, 2, 1))
    router_t = router_weight.T
    g1 = first_gain.reshape(1, width)
    g2 = second_gain.reshape(1, width)

    def exchange(value):
        value = value.reshape(experts, 2 * cap, width)
        value = lax.all_to_all(value, "exp", split_axis=0, concat_axis=0, tiled=True)
        return value.reshape(total, width)

    saved, sent = [], []
    for micro in range(MICRO):
        made = fore(
            micro,
            cap,
            tokens,
            picks_t,
            priority_ranks,
            attn_input,
            attn_output,
            g1,
            g2,
            router_t,
            cotangent,
        )
        sent.append(made[0])
        saved.append(made[1:])
    arrived = [exchange(v) for v in sent]
    answer0, up0, down0 = expert(cap, arrived[0], expert_up, expert_down, None)
    answer1, up1, down1 = expert(cap, arrived[1], expert_up, expert_down, (up0, down0))
    ret = [exchange(v) for v in (answer0, answer1)]
    up_other = lax.ppermute(up1, "grp", [(0, 1), (1, 0)])
    down_other = lax.ppermute(down1, "grp", [(0, 1), (1, 0)])

    weights = (attn_input, attn_output, g1, g2, router_t)
    block, dx0, dqkv0, *sums = back(
        0, scal, plan, ret[0], saved[0], tokens, cotangent, *weights, None
    )
    block, dx1, dqkv1, send, keep = back(
        1, scal, plan, ret[1], saved[1], tokens, cotangent, *weights, (block, *sums)
    )

    beside = (
        lambda: finish((dqkv0, dqkv1), (dx0, dx1), tokens, attn_input, g1),
        lambda: up1.astype(F32) + up_other.astype(F32),
        lambda: down1.astype(F32) + down_other.astype(F32),
    )
    *dense, tokens_grad, up_sum, down_sum = reduce_all(
        send, keep, scal, plan, width, experts, beside
    )
    return (block, tokens_grad, *dense, up_sum[None], down_sum[None])


def solution(mesh):
    split = P(None, ("grp", "exp"), None)
    owned = P("exp", None, None)
    in_specs = (split,) * 3 + (P(),) * 5 + (owned, owned, split)
    out_specs = (split, split) + (P(),) * 5 + (owned, owned)
    return jax.shard_map(shards, mesh=mesh, in_specs=in_specs, out_specs=out_specs, check_vma=False)
```

```python
import functools

import jax
import jax.numpy as jnp
from jax import lax
from jax.experimental import pallas as pl
from jax.experimental.pallas import tpu as pltpu
from jax.sharding import PartitionSpec as P

HEADS = 8
HEAD = 64
SEQ = 144
MICRO = 2
EPS = 1e-06
FORE_HEADS = 2
BACK_HEADS = 4
GELU_C = 0.7978845608028654
GELU_A = 0.044715
SMALL = 32

BF = jnp.bfloat16
F32 = jnp.float32
MB = 1 << 20
FORE_MB = 60
EXPERT_MB = 48
BACK_MB = 60
FINISH_MB = 60
LAST_MB = 50
FILLS = 4
IN_VMEM = pl.BlockSpec(memory_space=pltpu.VMEM)
IN_HBM = pl.BlockSpec(memory_space=pltpu.HBM)


def nn(a, b):
    return lax.dot_general(a, b, (((1,), (0,)), ((), ())), preferred_element_type=F32)


def nt(a, b):
    return lax.dot_general(a, b, (((1,), (1,)), ((), ())), preferred_element_type=F32)


def tn(a, b):
    return lax.dot_general(a, b, (((0,), (0,)), ((), ())), preferred_element_type=F32)


def normalize(values):
    center = values - jnp.mean(values, axis=-1, keepdims=True)
    factor = lax.rsqrt(jnp.mean(center * center, axis=-1, keepdims=True) + EPS)
    return center * factor, factor


def norm_back(grad_normed, normed, factor):
    return factor * (
        grad_normed
        - jnp.mean(grad_normed, axis=-1, keepdims=True)
        - normed * jnp.mean(grad_normed * normed, axis=-1, keepdims=True)
    )


def iota(shape, dim):
    return lax.broadcasted_iota(jnp.int32, shape, dim)


def spread_heads(block):
    head = iota(block.shape, 1) // HEAD
    zero = jnp.zeros_like(block)
    count = block.shape[1] // HEAD
    return jnp.concatenate([jnp.where(head == h, block, zero) for h in range(count)], axis=0)


def gather_heads(full):
    count = full.shape[1] // HEAD
    rows = full.shape[0] // count
    head = iota((rows, full.shape[1]), 1) // HEAD
    total = jnp.where(head == 0, full[:rows], 0.0)
    for h in range(1, count):
        total = total + jnp.where(head == h, full[h * rows : (h + 1) * rows], 0.0)
    return total


def head_block(ref, rows, part, group, count, width):
    start = part * width + group * count * HEAD
    return ref[rows, start : start + count * HEAD]


def fore_kernel(cap, micro, *refs):
    tok_h, pick_h, rank_h, wqkv_h, wo_h, g1_h, g2_h, router_h, cot_h = refs[:9]
    send_h, qkv_h, mixed_h, x1_h, lse_h, meta_h = refs[9:15]
    tok_ref, pick_ref, rank_ref, wqkv_ref, wo_ref, g1_ref, g2_ref, router_ref, cot_ref = refs[15:24]
    send_ref, qkv_ref, mixed_ref, x1_ref, lse_ref, meta_ref = refs[24:30]
    all_s, in_sem, out_sem = refs[30:]
    rows, width = x1_ref.shape
    experts = router_ref.shape[0]
    images = rows // SEQ
    pairs = (
        (pick_h.at[micro], pick_ref),
        (rank_h.at[micro], rank_ref),
        (tok_h.at[micro], tok_ref),
        (g1_h, g1_ref),
        (wqkv_h, wqkv_ref),
        (wo_h, wo_ref),
        (g2_h, g2_ref),
        (router_h, router_ref),
        (cot_h.at[micro], cot_ref),
    )
    loads = [move(a, b, in_sem.at[n]) for n, (a, b) in enumerate(pairs)]

    loads[0].wait()
    loads[1].wait()
    rank_row = rank_ref[...].astype(F32)
    eye = iota((rows, rows), 0) == iota((rows, rows), 1)
    rank_col = jnp.sum(jnp.where(eye, rank_row, 0.0), axis=1, keepdims=True)
    less = jnp.where(rank_col < rank_row, 1.0, 0.0).astype(BF)
    picks = pick_ref[...]
    expert = iota((experts, rows), 0)
    on = [jnp.where(expert == picks[k : k + 1], 1.0, 0.0) for k in range(2)]
    before = [nn(on[k].astype(BF), less) for k in range(2)]
    before[1] = before[1] + jnp.sum(on[0], axis=1, keepdims=True)
    place = []
    for k in range(2):
        slot = jnp.sum(on[k] * before[k], axis=0, keepdims=True)
        base = picks[k : k + 1].astype(F32) * (2 * cap)
        place.append(jnp.where(slot < cap - 0.5, base + slot, -9999.0))

    loads[2].wait()
    loads[3].wait()
    x_in = tok_ref[...].astype(F32)
    normed, _ = normalize(x_in)
    h_first = (normed * g1_ref[...]).astype(BF)
    loads[4].wait()
    qkv_ref[...] = nn(h_first, wqkv_ref[...]).astype(BF)
    stores = [move(qkv_ref, qkv_h, out_sem.at[1])]

    groups = HEADS // FORE_HEADS
    wide = FORE_HEADS * HEAD
    for i in range(images):
        at = pl.ds(i * SEQ, SEQ)
        for g in range(groups):
            query = spread_heads(head_block(qkv_ref, at, 0, g, FORE_HEADS, width))
            key = head_block(qkv_ref, at, 1, g, FORE_HEADS, width)
            value = head_block(qkv_ref, at, 2, g, FORE_HEADS, width)
            scores = nt(key, query) * (HEAD**-0.5)
            peak = jnp.max(scores, axis=0, keepdims=True)
            expo = jnp.exp(scores - peak)
            denom = jnp.sum(expo, axis=0, keepdims=True)
            probs_low = (expo * (1.0 / denom)).astype(BF)
            line = i * groups + g
            lse_ref[line : line + 1, :] = peak + jnp.log(denom)
            mixed = gather_heads(tn(probs_low, value))
            mixed_ref[at, g * wide : (g + 1) * wide] = mixed.astype(BF)

    stores.append(move(mixed_ref, mixed_h, out_sem.at[2]))
    stores.append(move(lse_ref, lse_h, out_sem.at[4]))

    for n in range(5, 9):
        loads[n].wait()
    x_mid = tok_ref[...].astype(F32) + nn(mixed_ref[...], wo_ref[...])
    x1_ref[...] = x_mid
    stores.append(move(x1_ref, x1_h, out_sem.at[3]))
    normed, _ = normalize(x_mid)
    h_second = (normed * g2_ref[...]).astype(BF)
    all_s[:rows, :] = h_second
    logits = nt(router_ref[...], h_second)
    picked = [jnp.sum(on[k] * logits, axis=0, keepdims=True) for k in range(2)]
    top = jnp.maximum(picked[0], picked[1])
    expo = [jnp.exp(v - top) for v in picked]
    total = expo[0] + expo[1]
    gates = [v / total for v in expo]
    stack = jnp.concatenate(
        gates + place + [picks.astype(F32)] + [jnp.zeros((2, rows), F32)], axis=0
    )
    meta = jnp.transpose(stack)
    meta_ref[...] = meta
    stores.append(move(meta_ref, meta_h, out_sem.at[5]))
    grad_out = cot_ref[...].astype(F32)
    all_s[rows : 2 * rows, :] = (meta[:, 0:1] * grad_out).astype(BF)
    all_s[2 * rows :, :] = (meta[:, 1:2] * grad_out).astype(BF)
    place = [v.astype(jnp.int32) for v in place]

    gone = jnp.full((1, 2 * rows), -1, jnp.int32)
    pos_a = jnp.concatenate([place[0], place[0] + cap, place[1] + cap], axis=1)
    pos_b = jnp.concatenate([place[1], gone], axis=1)
    step = send_ref.shape[0] // FILLS
    for c in range(FILLS):
        start = c * step
        row = iota((step, 3 * rows), 0) + start
        first = jnp.where((row == pos_a) | (row == pos_b), 1.0, 0.0).astype(BF)
        part = nn(first, all_s[...])
        send_ref[pl.ds(start, step), :] = part.astype(BF)
        at = pl.ds(start, step)
        stores.append(move(send_ref.at[at], send_h.at[at], out_sem.at[6 + c]))
    for copy in stores:
        copy.wait()


def move(source, target, sem):
    copy = pltpu.make_async_copy(source, target, sem)
    copy.start()
    return copy


def micro_spec(shape, micro):
    return pl.BlockSpec((1,) + tuple(shape[1:]), lambda i: (micro,) + (0,) * (len(shape) - 1))


def whole_spec(shape):
    return pl.BlockSpec(tuple(shape), lambda i: (0,) * len(shape))


def params(limit, **more):
    return pltpu.CompilerParams(vmem_limit_bytes=limit * MB, **more)


def fore(micro, cap, tokens, picks_t, ranks, wqkv, wo, g1, g2, router_t, cot):
    _, rows, width = tokens.shape
    experts = router_t.shape[0]
    out_shape = (
        jax.ShapeDtypeStruct((experts * 2 * cap, width), BF),
        jax.ShapeDtypeStruct((rows, 3 * width), BF),
        jax.ShapeDtypeStruct((rows, width), BF),
        jax.ShapeDtypeStruct((rows, width), F32),
        jax.ShapeDtypeStruct((rows // SEQ * HEADS // FORE_HEADS, FORE_HEADS * SEQ), F32),
        jax.ShapeDtypeStruct((rows, 8), F32),
    )
    flops = 2 * rows * width * (4 * width + 3 * experts * 2 * cap + 4 * SEQ)
    return pl.pallas_call(
        functools.partial(fore_kernel, cap, micro),
        in_specs=[IN_HBM] * 9,
        out_specs=[IN_HBM] * 6,
        out_shape=out_shape,
        scratch_shapes=[
            pltpu.VMEM((rows, width), BF),
            pltpu.VMEM(picks_t.shape[1:], jnp.int32),
            pltpu.VMEM(ranks.shape[1:], jnp.int32),
            pltpu.VMEM(wqkv.shape, BF),
            pltpu.VMEM(wo.shape, BF),
            pltpu.VMEM(g1.shape, F32),
            pltpu.VMEM(g2.shape, F32),
            pltpu.VMEM(router_t.shape, BF),
            pltpu.VMEM((rows, width), BF),
        ]
        + [pltpu.VMEM(v.shape, v.dtype) for v in out_shape]
        + [pltpu.VMEM((3 * rows, width), BF)]
        + [pltpu.SemaphoreType.DMA((9,)), pltpu.SemaphoreType.DMA((6 + FILLS,))],
        compiler_params=params(FORE_MB),
        cost_estimate=pl.CostEstimate(flops=4 * flops, bytes_accessed=8 * MB, transcendentals=0),
        name="fore",
    )(tokens, picks_t, ranks, wqkv, wo, g1, g2, router_t, cot)


def expert_kernel(cap, first, *refs):
    if first:
        recv_ref, up_ref, down_ref, ret_ref, dup_ref, ddown_ref = refs[:6]
    else:
        recv_ref, up_ref, down_ref, aup_ref, adown_ref, ret_ref, dup_ref, ddown_ref = refs[:8]
    h_s, g_s, out_s, row_s = refs[-4:]
    step = pl.program_id(0)
    steps = pl.num_programs(0)
    slots = h_s.shape[0]

    def position(shape, dim):
        slot = iota(shape, dim)
        block = ((slot.astype(F32) + 0.5) * (1.0 / cap)).astype(jnp.int32)
        return slot + block * cap

    @pl.when(step == 0)
    def _():
        here = iota((slots, 2 * slots), 1)
        there = position((slots, 2 * slots), 0)
        pick = jnp.where(here == there, 1.0, 0.0).astype(BF)
        h_s[...] = nn(pick, recv_ref[...]).astype(BF)
        pick = jnp.where(here == there + cap, 1.0, 0.0).astype(BF)
        g_s[...] = nn(pick, recv_ref[...]).astype(BF)

    up = up_ref[0]
    down = down_ref[0]
    h = h_s[...]
    g = g_s[...]
    pre = nn(h, up)
    grad_act = nt(g, down)
    square = pre * pre
    tanh = jnp.tanh(GELU_C * pre * (1.0 + GELU_A * square))
    half = 0.5 + 0.5 * tanh
    act = (pre * half).astype(BF)
    slope = half + (0.5 * GELU_C) * pre * (1.0 - tanh * tanh) * (1.0 + 3.0 * GELU_A * square)
    grad_pre = (grad_act * slope).astype(BF)
    grad_up = tn(h, grad_pre)
    grad_down = tn(act, g)
    if not first:
        grad_up = grad_up + aup_ref[...]
        grad_down = grad_down + adown_ref[...]
    dup_ref[...] = grad_up.astype(dup_ref.dtype)
    ddown_ref[...] = grad_down.astype(ddown_ref.dtype)
    out = nn(act, down)
    row = nt(grad_pre, up)

    @pl.when(step == 0)
    def _():
        out_s[...] = out
        row_s[...] = row

    @pl.when(step > 0)
    def _():
        out_s[...] += out
        row_s[...] += row

    @pl.when(step == steps - 1)
    def _():
        here = iota((2 * slots, slots), 0)
        there = position((2 * slots, slots), 1)
        pick = jnp.where(here == there, 1.0, 0.0).astype(BF)
        total = nn(pick, out_s[...].astype(BF))
        pick = jnp.where(here == there + cap, 1.0, 0.0).astype(BF)
        total = total + nn(pick, row_s[...].astype(BF))
        ret_ref[...] = total.astype(BF)


def expert(cap, recv, up, down, earlier):
    first = earlier is None
    total, width = recv.shape
    slots = total // 2
    hidden = up.shape[2]
    tile = 512
    dtype = F32 if first else BF
    up_block = pl.BlockSpec((width, tile), lambda i: (0, i))
    down_block = pl.BlockSpec((tile, width), lambda i: (i, 0))
    in_specs = [
        whole_spec(recv.shape),
        pl.BlockSpec((1, width, tile), lambda i: (0, 0, i)),
        pl.BlockSpec((1, tile, width), lambda i: (0, i, 0)),
    ]
    args = [recv, up, down]
    if not first:
        in_specs += [up_block, down_block]
        args += list(earlier)
    return pl.pallas_call(
        functools.partial(expert_kernel, cap, first),
        grid=(hidden // tile,),
        in_specs=in_specs,
        out_specs=[whole_spec(recv.shape), up_block, down_block],
        out_shape=(
            jax.ShapeDtypeStruct(recv.shape, BF),
            jax.ShapeDtypeStruct((width, hidden), dtype),
            jax.ShapeDtypeStruct((hidden, width), dtype),
        ),
        scratch_shapes=[
            pltpu.VMEM((slots, width), BF),
            pltpu.VMEM((slots, width), BF),
            pltpu.VMEM((slots, width), F32),
            pltpu.VMEM((slots, width), F32),
        ],
        compiler_params=params(EXPERT_MB),
        cost_estimate=pl.CostEstimate(
            flops=2 * 12 * slots * width * hidden, bytes_accessed=24 * MB, transcendentals=0
        ),
        name="expert",
    )(*args)


def back_kernel(last, micro, *refs):
    take = list(refs)

    def next_refs(count):
        taken, take[:] = take[:count], take[count:]
        return taken

    scal_ref, ret_ref = next_refs(2)
    sources = next_refs(BACK_INS)
    earlier_h = next_refs(4) if last else []
    block_h, dx1_h, dqkv_h = next_refs(3)
    made_h = next_refs(4 if last else 3)
    held = next_refs(BACK_INS)
    (
        meta_ref,
        cot_ref,
        x1_ref,
        g2_ref,
        router_ref,
        mixed_ref,
        wo_ref,
        qkv_ref,
        lse_ref,
        tok_ref,
        g1_ref,
        wqkv_ref,
    ) = held
    in_ref, out_ref, small_ref = next_refs(3)
    block_ref, dx1_ref, dqkv_ref, dmix_s, in_sem, out_sem = next_refs(6)
    if last:
        tail_s, pay_s = next_refs(2)
    sources = [h.at[micro] if h.shape[0] == MICRO else h for h in sources]
    pairs = list(zip(sources, held))
    if last:
        pairs += list(zip(earlier_h[:3], (in_ref, out_ref, small_ref)))
    else:
        pairs = pairs[:-1]
    loads = [move(a, b, in_sem.at[n]) for n, (a, b) in enumerate(pairs[:8])]
    stores = []
    total = ret_ref.shape[0]
    rows, width = x1_ref.shape
    experts = router_ref.shape[0]

    def store(source, target):
        stores.append(move(source, target, out_sem.at[len(stores)]))

    loads[0].wait()
    meta = meta_ref[...]
    gates = [meta[:, k : k + 1] for k in range(2)]
    place = [meta[:, 2 + k : 3 + k].astype(jnp.int32) for k in range(2)]
    picks = [meta[:, 4 + k : 5 + k].astype(jnp.int32) for k in range(2)]
    cap = total // (2 * experts)
    here = iota((rows, total), 1)
    ret = ret_ref[...]
    both = (here == place[0] + cap) | (here == place[1] + cap)
    grad_second = nn(jnp.where(both, 1.0, 0.0).astype(BF), ret)
    pair_out = [nn(jnp.where(here == place[k], 1.0, 0.0).astype(BF), ret) for k in range(2)]
    for n in range(1, 5):
        loads[n].wait()
    loads += [move(a, b, in_sem.at[8 + n]) for n, (a, b) in enumerate(pairs[8:])]
    grad_out = cot_ref[...].astype(F32)
    x_mid = x1_ref[...]
    result = x_mid
    grad_gate = []
    for k in range(2):
        result = result + gates[k] * pair_out[k]
        grad_gate.append(jnp.sum(grad_out * pair_out[k], axis=1, keepdims=True))
    block_ref[...] = result.astype(BF)
    store(block_ref, block_h.at[micro])
    mean_gate = gates[0] * grad_gate[0] + gates[1] * grad_gate[1]
    lane = iota((rows, experts), 1)
    grad_logits = jnp.zeros((rows, experts), F32)
    for k in range(2):
        grad_pick = gates[k] * (grad_gate[k] - mean_gate)
        grad_logits = grad_logits + jnp.where(lane == picks[k], grad_pick, 0.0)
    grad_logits = grad_logits.astype(BF)
    grad_second = grad_second + nn(grad_logits, router_ref[...])
    normed, factor = normalize(x_mid)
    h_second = (normed * g2_ref[...]).astype(BF)
    small = [
        tn(grad_logits, h_second),
        jnp.sum(grad_second * normed, axis=0, keepdims=True),
    ]
    grad_mid = grad_out + norm_back(grad_second * g2_ref[...], normed, factor)
    dx1_ref[...] = grad_mid
    store(dx1_ref, dx1_h)
    for n in range(5, 9):
        loads[n].wait()
    grad_attn = grad_mid.astype(BF)
    out_grad = tn(mixed_ref[...], grad_attn)
    if last:
        slots = 2 * lax.axis_size("exp")
        half = slots // 2
        piece = width // half
        span = half * piece
        tail = SMALL * (experts // 16)

        def lay(s, b, block):
            mine = scal_ref[2] == b
            start = jnp.where(mine, 0, half)
            order = jnp.where(mine, scal_ref[0], scal_ref[1])
            for j in range(half):
                to = pl.multiple_of((start + (j ^ order)) * piece, piece)
                pay_s[s, pl.ds(to, piece), :] = block[j * piece : (j + 1) * piece].astype(BF)

        for copy in loads[13:15]:
            copy.wait()
        lay(1, 1, out_grad + out_ref[...].astype(F32))
        small[0] = small[0] + small_ref[0:experts, :]
        small[1] = small[1] + small_ref[experts : experts + 1, :]
        tail_s[:experts, :] = small[0].astype(BF)
    else:
        out_ref[...] = out_grad.astype(BF)
        small_ref[0:experts, :] = small[0]
        small_ref[experts : experts + 1, :] = small[1]
        small_ref[experts + 1 :, :] = jnp.zeros((small_ref.shape[0] - experts - 1, width), F32)
        store(out_ref, made_h[1])
        store(small_ref, made_h[2])
    dmix_s[...] = nt(grad_attn, wo_ref[...]).astype(BF)

    groups = HEADS // BACK_HEADS
    wide = BACK_HEADS * HEAD
    lines = BACK_HEADS // FORE_HEADS
    def image(i, carry):
        at = pl.ds(pl.multiple_of(i * SEQ, 16), SEQ)
        for g in range(groups):
            query = spread_heads(head_block(qkv_ref, at, 0, g, BACK_HEADS, width))
            key = head_block(qkv_ref, at, 1, g, BACK_HEADS, width)
            value = head_block(qkv_ref, at, 2, g, BACK_HEADS, width)
            grad_mixed = spread_heads(dmix_s[at, g * wide : (g + 1) * wide])
            scores = nt(key, query) * (HEAD**-0.5)
            line = (i * groups + g) * lines
            level = [lse_ref[pl.ds(line + n, 1), :] for n in range(lines)]
            probs = jnp.exp(scores - jnp.concatenate(level, axis=1))
            grad_probs = nt(value, grad_mixed)
            inner = jnp.sum(probs * grad_probs, axis=0, keepdims=True)
            grad_scores = (probs * (grad_probs - inner)).astype(BF)
            grad_value = nn(probs.astype(BF), grad_mixed)
            grad_key = nn(grad_scores, query) * (HEAD**-0.5)
            grad_query = gather_heads(tn(grad_scores, key)) * (HEAD**-0.5)
            for part, grad in enumerate((grad_query, grad_key, grad_value)):
                start = part * width + g * wide
                dqkv_ref[at, start : start + wide] = grad.astype(BF)
        return carry

    lax.fori_loop(0, rows // SEQ, image, 0)

    store(dqkv_ref, dqkv_h)
    loads[9].wait()
    loads[10].wait()
    normed, _ = normalize(tok_ref[...].astype(F32))
    h_first = (normed * g1_ref[...]).astype(BF)
    if last:
        loads[11].wait()
        loads[12].wait()
    gain = jnp.zeros((width, 1), F32)
    for part in (2, 0, 1):
        columns = slice(part * width, (part + 1) * width)
        in_grad = tn(h_first, dqkv_ref[:, columns])
        if not last:
            in_ref[:, columns] = in_grad.astype(BF)
            continue
        in_grad = in_grad + in_ref[:, columns].astype(F32)
        gain = gain + jnp.sum(wqkv_ref[:, columns].astype(F32) * in_grad, axis=1, keepdims=True)
        lay(part // 2, part % 2, in_grad)
        if part != 0:
            s = part // 2
            store(pay_s.at[s, pl.ds(span, span)], made_h[s].at[pl.ds(0, span)])
            store(pay_s.at[s, pl.ds(0, span)], made_h[2 + s].at[pl.ds(0, span)])
    if last:
        eye = iota((width, width), 0) == iota((width, width), 1)
        gain = jnp.sum(jnp.where(eye, gain, 0.0), axis=0, keepdims=True) / g1_ref[...]
        fill = jnp.zeros((tail - experts - 2, width), F32)
        tail_s[experts:, :] = jnp.concatenate([small[1], gain, fill], axis=0).astype(BF)
        for target in (made_h[0], made_h[2]):
            store(tail_s, target.at[pl.ds(span, tail)])
    else:
        store(in_ref, made_h[0])
    for copy in stores:
        copy.wait()


BACK_INS = 12


def back(micro, scal, plan, ret, saved, tokens, cot, wqkv, wo, g1, g2, router_t, earlier):
    last = earlier is not None
    qkv, mixed, x1, lse, meta = saved
    _, rows, width = tokens.shape
    experts = router_t.shape[0]
    slots, piece, tail = plan
    ins = [meta, cot, x1, g2, router_t, mixed, wo, qkv, lse, tokens, g1, wqkv]
    shapes = [
        jax.ShapeDtypeStruct(tokens.shape, BF),
        jax.ShapeDtypeStruct((rows, width), F32),
        jax.ShapeDtypeStruct((rows, 3 * width), BF),
    ]
    sums = [
        jax.ShapeDtypeStruct(wqkv.shape, BF),
        jax.ShapeDtypeStruct(wo.shape, BF),
        jax.ShapeDtypeStruct((experts + 8, width), F32),
    ]

    def hold(value):
        shape = value.shape[1:] if value.shape[0] == MICRO else value.shape
        return pltpu.VMEM(shape, value.dtype)

    scratch = [hold(a) for a in ins + sums + shapes]
    scratch += [
        pltpu.VMEM((rows, width), BF),
        pltpu.SemaphoreType.DMA((16,)),
        pltpu.SemaphoreType.DMA((12,)),
    ]
    aliases = {}
    if last:
        block, *sums = earlier
        args = [scal, ret] + ins + sums + [block]
        aliases = {17: 0}
        span = slots // 2 * piece
        shapes += [jax.ShapeDtypeStruct((span + more, width), BF) for more in (tail, 0)] * 2
        scratch += [pltpu.VMEM((tail, width), BF), pltpu.VMEM((2, slots * piece, width), BF)]
    else:
        args = [scal, ret] + ins
        shapes += sums
    in_specs = [pl.BlockSpec(memory_space=pltpu.SMEM), IN_VMEM] + [IN_HBM] * (len(args) - 2)
    out_specs = [IN_HBM] * len(shapes)
    flops = 2 * rows * width * (3 * ret.shape[0] + 12 * width)
    return pl.pallas_call(
        functools.partial(back_kernel, last, micro),
        in_specs=in_specs,
        out_specs=out_specs,
        out_shape=shapes,
        scratch_shapes=scratch,
        input_output_aliases=aliases,
        compiler_params=params(LAST_MB if last else BACK_MB),
        cost_estimate=pl.CostEstimate(flops=5 * flops, bytes_accessed=20 * MB, transcendentals=0),
        name="back",
    )(*args)


def finish_kernel(dqkv_ref, dx1_ref, tok_ref, wqkv_ref, g1_ref, *refs):
    grad_first = nt(dqkv_ref[...], wqkv_ref[...])
    normed, factor = normalize(tok_ref[0].astype(F32))
    refs[-1][0] = dx1_ref[...] + norm_back(grad_first * g1_ref[...], normed, factor)


def finish(micro, dqkv, dx1, tokens, wqkv, g1, earlier):
    _, rows, width = tokens.shape
    each = rows // 2
    both = pl.BlockSpec((1, each, width), lambda i: (micro, i, 0))
    in_specs = [
        pl.BlockSpec((each, 3 * width), lambda i: (i, 0)),
        pl.BlockSpec((each, width), lambda i: (i, 0)),
        both,
        whole_spec(wqkv.shape),
        whole_spec(g1.shape),
    ]
    args = [dqkv, dx1, tokens, wqkv, g1]
    if earlier is not None:
        args.append(earlier)
        in_specs.append(IN_HBM)
    return pl.pallas_call(
        finish_kernel,
        grid=(2,),
        in_specs=in_specs,
        out_specs=both,
        out_shape=jax.ShapeDtypeStruct(tokens.shape, F32),
        input_output_aliases={} if earlier is None else {5: 0},
        compiler_params=params(FINISH_MB),
        cost_estimate=pl.CostEstimate(
            flops=2 * rows * width * 3 * width, bytes_accessed=6 * MB, transcendentals=0
        ),
        name="finish",
    )(*args)


def local(kernel, shapes, args, scalars=0, scratch=()):
    specs = [pl.BlockSpec(memory_space=pltpu.SMEM)] * scalars
    specs += [pl.BlockSpec(memory_space=pltpu.VMEM)] * (len(args) - scalars)
    size = sum(a.size * 4 for a in args)
    return pl.pallas_call(
        kernel,
        in_specs=specs,
        out_specs=[pl.BlockSpec(memory_space=pltpu.VMEM)] * len(shapes),
        out_shape=shapes,
        scratch_shapes=list(scratch),
        compiler_params=params(32),
        cost_estimate=pl.CostEstimate(flops=1000, bytes_accessed=size, transcendentals=0),
    )(*args)


def halve(keep, arrived, count, piece):
    rows, width = keep.shape
    half = count // 2 * piece
    tail = rows - 2 * half

    def kernel(keep_ref, arrived_ref, send_out, keep_out):
        total = (keep_ref[...].astype(F32) + arrived_ref[...].astype(F32)).astype(BF)
        keep_out[:half, :] = total[:half]
        if tail:
            keep_out[half:, :] = total[2 * half :]
        send_out[...] = total[half:]

    shape = jax.ShapeDtypeStruct((half + tail, width), BF)
    return local(kernel, [shape] * 2, [keep, arrived])


def join(first, second):
    rows, width = first.shape

    def kernel(a, b, out):
        out[:rows, :] = a[...]
        out[rows:, :] = b[...]

    (made,) = local(kernel, [jax.ShapeDtypeStruct((2 * rows, width), BF)], [first, second])
    return made


def reduce_all(sends, keeps, scal, plan, width, experts, beside):
    slots, piece, tail = plan
    size = lax.axis_size("exp")
    bits = size.bit_length() - 1
    orders = halving_orders(size)
    low, high = 1 << (bits - 2), 1 << (bits - 1)
    groups = [low, high, low | high]

    def swap(value, step):
        pairs = []
        for core in range(2):
            mask = 1 << orders[core][step]
            pairs += [(core * size + i, core * size + (i ^ mask)) for i in range(size)]
        return lax.ppermute(value, ("grp", "exp"), pairs)

    def swap_far(value, mask):
        return lax.ppermute(value, "exp", [(i, i ^ mask) for i in range(size)])

    def swap_core(value):
        return lax.ppermute(value, "grp", [(0, 1), (1, 0)])

    arrived = [swap_core(v) for v in sends]
    count = slots // 2
    steps = bits - 2
    for step in range(steps):
        made = [halve(keeps[s], arrived[s], count, piece) for s in range(2)]
        count //= 2
        arrived = [swap(made[s][0], step) for s in range(2)]
        keeps = [v[1] for v in made]

    share = tail // 4
    span = 2 * piece + share

    def quarter(scal_ref, *refs):
        small_s = refs[8]
        for s in range(2):
            total = refs[s][...].astype(F32) + refs[2 + s][...].astype(F32)
            for j in range(4):
                block = total[j * piece : (j + 1) * piece]
                refs[4 + j][s * piece : (s + 1) * piece, :] = block.astype(BF)
            if s == 0:
                small_s[...] = total[4 * piece :]
        for j in range(4):
            part = pl.multiple_of((scal_ref[3] ^ j) * share, share)
            refs[4 + j][2 * piece :, :] = small_s[pl.ds(part, share), :].astype(BF)

    shape = jax.ShapeDtypeStruct((span, width), BF)
    made = local(
        quarter,
        [shape] * 4,
        [scal] + list(keeps) + list(arrived),
        scalars=1,
        scratch=[pltpu.VMEM((tail, width), F32)],
    )
    arrived = [swap_far(made[1 + j], groups[j]) for j in range(3)]
    extra = beside()
    *arrived, extra = lax.optimization_barrier((*arrived, extra))

    def add_up(a, b, c, d, mine_ref):
        total = (a[...].astype(F32) + b[...].astype(F32)) + (c[...].astype(F32) + d[...].astype(F32))
        mine_ref[...] = total.astype(BF)

    (mine,) = local(add_up, [shape], [made[0]] + arrived)

    others = [swap_far(mine, groups[j]) for j in range(3)]

    def lay(scal_ref, a, b, c, d, one_ref, two_ref, small_ref):
        for j, ref in enumerate((a, b, c, d)):
            one_ref[j * piece : (j + 1) * piece, :] = ref[:piece, :]
            two_ref[j * piece : (j + 1) * piece, :] = ref[piece : 2 * piece, :]
            part = pl.multiple_of((scal_ref[3] ^ j) * share, share)
            small_ref[pl.ds(part, share), :] = ref[2 * piece :, :].astype(F32)

    shape = jax.ShapeDtypeStruct((4 * piece, width), BF)
    *have, small = local(
        lay,
        [shape] * 2 + [jax.ShapeDtypeStruct((tail, width), F32)],
        [scal, mine] + others,
        scalars=1,
    )
    vectors = (small[experts + 1], small[experts], small[:experts].T)
    for step in reversed(range(steps)):
        arrived = [swap(have[s], step) for s in range(2)]
        if step == 0:
            arrived[1], vectors = lax.optimization_barrier((arrived[1], vectors))
        have = [join(have[s], arrived[s]) for s in range(2)]
    other = [swap_core(v) for v in have]
    each = slots // 2

    def deal(halves, mine, *refs):
        scal_ref, refs = refs[0], refs[1:]
        in_h, out_h, block_s, sems = refs[-4:]
        core = scal_ref[2]
        part = core if mine else 1 - core
        order = scal_ref[0] if mine else scal_ref[1]
        copies = []
        for n, s in enumerate(halves):
            for pos in range(each):
                to = pl.multiple_of((pos ^ order) * piece, piece)
                block = refs[n][pos * piece : (pos + 1) * piece, :].astype(F32)
                block_s[n, pl.ds(to, piece), :] = block
            if s == 0:
                columns = pl.ds(pl.multiple_of(part * width, width), width)
                copies.append(move(block_s.at[n], in_h.at[:, columns], sems.at[0]))
            else:

                @pl.when(part == 0)
                def _():
                    move(block_s.at[n], in_h.at[:, pl.ds(2 * width, width)], sems.at[1]).wait()

                @pl.when(part == 1)
                def _():
                    move(block_s.at[n], out_h, sems.at[1]).wait()

        for copy in copies:
            copy.wait()

    def dealt(halves, values, grads):
        mine = grads is None
        grads = [] if mine else list(grads)
        count = len(values)
        return pl.pallas_call(
            functools.partial(deal, halves, mine),
            in_specs=[pl.BlockSpec(memory_space=pltpu.SMEM)]
            + [IN_VMEM] * count
            + [IN_HBM] * len(grads),
            out_specs=[IN_HBM, IN_HBM],
            out_shape=(
                jax.ShapeDtypeStruct((width, 3 * width), F32),
                jax.ShapeDtypeStruct((width, width), F32),
            ),
            input_output_aliases={} if mine else {1 + count: 0, 2 + count: 1},
            scratch_shapes=[
                pltpu.VMEM((count, width, width), F32),
                pltpu.SemaphoreType.DMA((2,)),
            ],
            compiler_params=params(16),
            cost_estimate=pl.CostEstimate(flops=1000, bytes_accessed=4 * MB, transcendentals=0),
            name="deal",
        )(scal, *values, *grads)

    grads = dealt((0, 1), have, None)
    in_grad, out_grad = dealt((0, 1), other, grads)
    return in_grad, out_grad, *vectors, extra


def halving_orders(size):
    bits = size.bit_length() - 1
    first = list(range(bits - 2))
    second = [first[b ^ 1] if (b ^ 1) < len(first) else b for b in first]
    return first, second


def places(size):
    bits = size.bit_length() - 1
    core = lax.axis_index("grp")
    me = lax.axis_index("exp")
    last = me >> (bits - 2)
    made = []
    for order in halving_orders(size):
        value = jnp.zeros_like(me)
        for b in order:
            value = value * 2 + ((me >> b) & 1)
        made.append(value * 4 + last)
    own = jnp.where(core == 0, made[0], made[1])
    other = jnp.where(core == 0, made[1], made[0])
    return jnp.stack([own, other, core, last]).astype(jnp.int32)


def shards(
    tokens,
    expert_picks,
    priority_ranks,
    attn_input,
    attn_output,
    first_gain,
    second_gain,
    router_weight,
    expert_up,
    expert_down,
    cotangent,
):
    size = lax.axis_size("exp")
    experts = router_weight.shape[1]
    rows, width = tokens.shape[1:]
    cap = max(2, rows // size)
    total = experts * 2 * cap
    slots = 2 * size
    plan = (slots, 2 * width // slots, SMALL * (experts // 16))
    scal = places(size)
    picks_t = jnp.transpose(expert_picks, (0, 2, 1))
    router_t = router_weight.T
    g1 = first_gain.reshape(1, width)
    g2 = second_gain.reshape(1, width)

    def exchange(value):
        value = value.reshape(experts, 2 * cap, width)
        value = lax.all_to_all(value, "exp", split_axis=0, concat_axis=0, tiled=True)
        return value.reshape(total, width)

    saved, sent = [], []
    for micro in range(MICRO):
        made = fore(
            micro,
            cap,
            tokens,
            picks_t,
            priority_ranks,
            attn_input,
            attn_output,
            g1,
            g2,
            router_t,
            cotangent,
        )
        sent.append(made[0])
        saved.append(made[1:])
    arrived = [exchange(v) for v in sent]
    answer0, up0, down0 = expert(cap, arrived[0], expert_up, expert_down, None)
    answer1, up1, down1 = expert(cap, arrived[1], expert_up, expert_down, (up0, down0))
    ret = [exchange(v) for v in (answer0, answer1)]
    up_other = lax.ppermute(up1, "grp", [(0, 1), (1, 0)])
    down_other = lax.ppermute(down1, "grp", [(0, 1), (1, 0)])

    weights = (attn_input, attn_output, g1, g2, router_t)
    block, dx0, dqkv0, *sums = back(
        0, scal, plan, ret[0], saved[0], tokens, cotangent, *weights, None
    )
    halves = lax.optimization_barrier((up1, up_other, down1, down_other, sums[2]))
    up_sum = halves[0].astype(F32) + halves[1].astype(F32)
    down_sum = halves[2].astype(F32) + halves[3].astype(F32)
    first = finish(0, dqkv0, dx0, tokens, attn_input, g1, None)
    first, up_sum, down_sum, sums[2] = lax.optimization_barrier((first, up_sum, down_sum, halves[4]))
    block, dx1, dqkv1, *pay = back(
        1, scal, plan, ret[1], saved[1], tokens, cotangent, *weights, (block, *sums)
    )

    def beside():
        return finish(1, dqkv1, dx1, tokens, attn_input, g1, first)

    *dense, tokens_grad = reduce_all(pay[:2], pay[2:], scal, plan, width, experts, beside)
    return (block, tokens_grad, *dense, up_sum[None], down_sum[None])


def solution(mesh):
    split = P(None, ("grp", "exp"), None)
    owned = P("exp", None, None)
    in_specs = (split,) * 3 + (P(),) * 5 + (owned, owned, split)
    out_specs = (split, split) + (P(),) * 5 + (owned, owned)
    return jax.shard_map(shards, mesh=mesh, in_specs=in_specs, out_specs=out_specs, check_vma=False)
```

```python
import functools

import jax
import jax.numpy as jnp
from jax import lax
from jax.experimental import pallas as pl
from jax.experimental.pallas import tpu as pltpu
from jax.sharding import PartitionSpec as P

HEADS = 8
HEAD = 64
SEQ = 144
MICRO = 2
EPS = 1e-06
FORE_HEADS = 2
BACK_HEADS = 4
GELU_C = 0.7978845608028654
GELU_A = 0.044715
SMALL = 32

BF = jnp.bfloat16
F32 = jnp.float32
MB = 1 << 20
FORE_MB = 60
EXPERT_MB = 48
BACK_MB = 60
FINISH_MB = 60
LAST_MB = 50
FILLS = 4
IN_VMEM = pl.BlockSpec(memory_space=pltpu.VMEM)
IN_HBM = pl.BlockSpec(memory_space=pltpu.HBM)


def nn(a, b):
    return lax.dot_general(a, b, (((1,), (0,)), ((), ())), preferred_element_type=F32)


def nt(a, b):
    return lax.dot_general(a, b, (((1,), (1,)), ((), ())), preferred_element_type=F32)


def tn(a, b):
    return lax.dot_general(a, b, (((0,), (0,)), ((), ())), preferred_element_type=F32)


def normalize(values):
    center = values - jnp.mean(values, axis=-1, keepdims=True)
    factor = lax.rsqrt(jnp.mean(center * center, axis=-1, keepdims=True) + EPS)
    return center * factor, factor


def norm_back(grad_normed, normed, factor):
    return factor * (
        grad_normed
        - jnp.mean(grad_normed, axis=-1, keepdims=True)
        - normed * jnp.mean(grad_normed * normed, axis=-1, keepdims=True)
    )


def iota(shape, dim):
    return lax.broadcasted_iota(jnp.int32, shape, dim)


def spread_heads(block):
    head = iota(block.shape, 1) // HEAD
    zero = jnp.zeros_like(block)
    count = block.shape[1] // HEAD
    return jnp.concatenate([jnp.where(head == h, block, zero) for h in range(count)], axis=0)


def gather_heads(full):
    count = full.shape[1] // HEAD
    rows = full.shape[0] // count
    head = iota((rows, full.shape[1]), 1) // HEAD
    total = jnp.where(head == 0, full[:rows], 0.0)
    for h in range(1, count):
        total = total + jnp.where(head == h, full[h * rows : (h + 1) * rows], 0.0)
    return total


def head_block(ref, rows, part, group, count, width):
    start = part * width + group * count * HEAD
    return ref[rows, start : start + count * HEAD]


def fore_kernel(cap, micro, *refs):
    tok_h, pick_h, rank_h, wqkv_h, wo_h, g1_h, g2_h, router_h, cot_h = refs[:9]
    send_h, qkv_h, mixed_h, x1_h, lse_h, meta_h = refs[9:15]
    tok_ref, pick_ref, rank_ref, wqkv_ref, wo_ref, g1_ref, g2_ref, router_ref, cot_ref = refs[15:24]
    send_ref, qkv_ref, mixed_ref, x1_ref, lse_ref, meta_ref = refs[24:30]
    all_s, in_sem, out_sem = refs[30:]
    rows, width = x1_ref.shape
    experts = router_ref.shape[0]
    images = rows // SEQ
    pairs = (
        (pick_h.at[micro], pick_ref),
        (rank_h.at[micro], rank_ref),
        (tok_h.at[micro], tok_ref),
        (g1_h, g1_ref),
        (wqkv_h, wqkv_ref),
        (wo_h, wo_ref),
        (g2_h, g2_ref),
        (router_h, router_ref),
        (cot_h.at[micro], cot_ref),
    )
    loads = [move(a, b, in_sem.at[n]) for n, (a, b) in enumerate(pairs)]

    loads[0].wait()
    loads[1].wait()
    rank_row = rank_ref[...].astype(F32)
    eye = iota((rows, rows), 0) == iota((rows, rows), 1)
    rank_col = jnp.sum(jnp.where(eye, rank_row, 0.0), axis=1, keepdims=True)
    less = jnp.where(rank_col < rank_row, 1.0, 0.0).astype(BF)
    picks = pick_ref[...]
    expert = iota((experts, rows), 0)
    on = [jnp.where(expert == picks[k : k + 1], 1.0, 0.0) for k in range(2)]
    before = [nn(on[k].astype(BF), less) for k in range(2)]
    before[1] = before[1] + jnp.sum(on[0], axis=1, keepdims=True)
    place = []
    for k in range(2):
        slot = jnp.sum(on[k] * before[k], axis=0, keepdims=True)
        base = picks[k : k + 1].astype(F32) * (2 * cap)
        place.append(jnp.where(slot < cap - 0.5, base + slot, -9999.0))

    loads[2].wait()
    loads[3].wait()
    x_in = tok_ref[...].astype(F32)
    normed, _ = normalize(x_in)
    h_first = (normed * g1_ref[...]).astype(BF)
    loads[4].wait()
    qkv_ref[...] = nn(h_first, wqkv_ref[...]).astype(BF)
    stores = [move(qkv_ref, qkv_h, out_sem.at[1])]

    groups = HEADS // FORE_HEADS
    wide = FORE_HEADS * HEAD
    def image(i, carry):
        at = pl.ds(pl.multiple_of(i * SEQ, 16), SEQ)
        for g in range(groups):
            query = spread_heads(head_block(qkv_ref, at, 0, g, FORE_HEADS, width))
            key = head_block(qkv_ref, at, 1, g, FORE_HEADS, width)
            value = head_block(qkv_ref, at, 2, g, FORE_HEADS, width)
            scores = nt(key, query) * (HEAD**-0.5)
            peak = jnp.max(scores, axis=0, keepdims=True)
            expo = jnp.exp(scores - peak)
            denom = jnp.sum(expo, axis=0, keepdims=True)
            probs_low = (expo * (1.0 / denom)).astype(BF)
            line = i * groups + g
            lse_ref[pl.ds(line, 1), :] = peak + jnp.log(denom)
            mixed = gather_heads(tn(probs_low, value))
            mixed_ref[at, g * wide : (g + 1) * wide] = mixed.astype(BF)
        return carry

    lax.fori_loop(0, images, image, 0, unroll=micro == 0)

    stores.append(move(mixed_ref, mixed_h, out_sem.at[2]))
    stores.append(move(lse_ref, lse_h, out_sem.at[4]))

    for n in range(5, 9):
        loads[n].wait()
    x_mid = tok_ref[...].astype(F32) + nn(mixed_ref[...], wo_ref[...])
    x1_ref[...] = x_mid
    stores.append(move(x1_ref, x1_h, out_sem.at[3]))
    normed, _ = normalize(x_mid)
    h_second = (normed * g2_ref[...]).astype(BF)
    all_s[:rows, :] = h_second
    logits = nt(router_ref[...], h_second)
    picked = [jnp.sum(on[k] * logits, axis=0, keepdims=True) for k in range(2)]
    top = jnp.maximum(picked[0], picked[1])
    expo = [jnp.exp(v - top) for v in picked]
    total = expo[0] + expo[1]
    gates = [v / total for v in expo]
    stack = jnp.concatenate(
        gates + place + [picks.astype(F32)] + [jnp.zeros((2, rows), F32)], axis=0
    )
    meta = jnp.transpose(stack)
    meta_ref[...] = meta
    stores.append(move(meta_ref, meta_h, out_sem.at[5]))
    grad_out = cot_ref[...].astype(F32)
    all_s[rows : 2 * rows, :] = (meta[:, 0:1] * grad_out).astype(BF)
    all_s[2 * rows :, :] = (meta[:, 1:2] * grad_out).astype(BF)
    place = [v.astype(jnp.int32) for v in place]

    gone = jnp.full((1, 2 * rows), -1, jnp.int32)
    pos_a = jnp.concatenate([place[0], place[0] + cap, place[1] + cap], axis=1)
    pos_b = jnp.concatenate([place[1], gone], axis=1)
    step = send_ref.shape[0] // FILLS
    for c in range(FILLS):
        start = c * step
        row = iota((step, 3 * rows), 0) + start
        first = jnp.where((row == pos_a) | (row == pos_b), 1.0, 0.0).astype(BF)
        part = nn(first, all_s[...])
        send_ref[pl.ds(start, step), :] = part.astype(BF)
        at = pl.ds(start, step)
        stores.append(move(send_ref.at[at], send_h.at[at], out_sem.at[6 + c]))
    for copy in stores:
        copy.wait()


def move(source, target, sem):
    copy = pltpu.make_async_copy(source, target, sem)
    copy.start()
    return copy


def micro_spec(shape, micro):
    return pl.BlockSpec((1,) + tuple(shape[1:]), lambda i: (micro,) + (0,) * (len(shape) - 1))


def whole_spec(shape):
    return pl.BlockSpec(tuple(shape), lambda i: (0,) * len(shape))


def params(limit, **more):
    return pltpu.CompilerParams(vmem_limit_bytes=limit * MB, **more)


def fore(micro, cap, tokens, picks_t, ranks, wqkv, wo, g1, g2, router_t, cot):
    _, rows, width = tokens.shape
    experts = router_t.shape[0]
    out_shape = (
        jax.ShapeDtypeStruct((experts * 2 * cap, width), BF),
        jax.ShapeDtypeStruct((rows, 3 * width), BF),
        jax.ShapeDtypeStruct((rows, width), BF),
        jax.ShapeDtypeStruct((rows, width), F32),
        jax.ShapeDtypeStruct((rows // SEQ * HEADS // FORE_HEADS, FORE_HEADS * SEQ), F32),
        jax.ShapeDtypeStruct((rows, 8), F32),
    )
    flops = 2 * rows * width * (4 * width + 3 * experts * 2 * cap + 4 * SEQ)
    return pl.pallas_call(
        functools.partial(fore_kernel, cap, micro),
        in_specs=[IN_HBM] * 9,
        out_specs=[IN_HBM] * 6,
        out_shape=out_shape,
        scratch_shapes=[
            pltpu.VMEM((rows, width), BF),
            pltpu.VMEM(picks_t.shape[1:], jnp.int32),
            pltpu.VMEM(ranks.shape[1:], jnp.int32),
            pltpu.VMEM(wqkv.shape, BF),
            pltpu.VMEM(wo.shape, BF),
            pltpu.VMEM(g1.shape, F32),
            pltpu.VMEM(g2.shape, F32),
            pltpu.VMEM(router_t.shape, BF),
            pltpu.VMEM((rows, width), BF),
        ]
        + [pltpu.VMEM(v.shape, v.dtype) for v in out_shape]
        + [pltpu.VMEM((3 * rows, width), BF)]
        + [pltpu.SemaphoreType.DMA((9,)), pltpu.SemaphoreType.DMA((6 + FILLS,))],
        compiler_params=params(FORE_MB),
        cost_estimate=pl.CostEstimate(flops=4 * flops, bytes_accessed=8 * MB, transcendentals=0),
        name="fore",
    )(tokens, picks_t, ranks, wqkv, wo, g1, g2, router_t, cot)


def expert_kernel(cap, first, *refs):
    if first:
        recv_ref, up_ref, down_ref, ret_ref, dup_ref, ddown_ref = refs[:6]
    else:
        recv_ref, up_ref, down_ref, aup_ref, adown_ref, ret_ref, dup_ref, ddown_ref = refs[:8]
    h_s, g_s, out_s, row_s = refs[-4:]
    step = pl.program_id(0)
    steps = pl.num_programs(0)
    slots = h_s.shape[0]

    def position(shape, dim, start):
        slot = iota(shape, dim) + start
        block = ((slot.astype(F32) + 0.5) * (1.0 / cap)).astype(jnp.int32)
        return slot + block * cap

    part = slots // 4

    @pl.when(step == 0)
    def _():
        def take(c, carry):
            at = pl.ds(pl.multiple_of(c * part, 16), part)
            here = iota((part, 2 * slots), 1)
            there = position((part, 2 * slots), 0, c * part)
            pick = jnp.where(here == there, 1.0, 0.0).astype(BF)
            h_s[at, :] = nn(pick, recv_ref[...]).astype(BF)
            pick = jnp.where(here == there + cap, 1.0, 0.0).astype(BF)
            g_s[at, :] = nn(pick, recv_ref[...]).astype(BF)
            return carry

        lax.fori_loop(0, 4, take, 0)

    up = up_ref[0]
    down = down_ref[0]
    h = h_s[...]
    g = g_s[...]
    pre = nn(h, up)
    grad_act = nt(g, down)
    square = pre * pre
    tanh = jnp.tanh(GELU_C * pre * (1.0 + GELU_A * square))
    half = 0.5 + 0.5 * tanh
    act = (pre * half).astype(BF)
    slope = half + (0.5 * GELU_C) * pre * (1.0 - tanh * tanh) * (1.0 + 3.0 * GELU_A * square)
    grad_pre = (grad_act * slope).astype(BF)
    grad_up = tn(h, grad_pre)
    grad_down = tn(act, g)
    if not first:
        grad_up = grad_up + aup_ref[...]
        grad_down = grad_down + adown_ref[...]
    dup_ref[...] = grad_up.astype(dup_ref.dtype)
    ddown_ref[...] = grad_down.astype(ddown_ref.dtype)
    out = nn(act, down)
    row = nt(grad_pre, up)

    @pl.when(step == 0)
    def _():
        out_s[...] = out
        row_s[...] = row

    @pl.when(step > 0)
    def _():
        out_s[...] += out
        row_s[...] += row

    @pl.when(step == steps - 1)
    def _():
        def give(c, carry):
            at = pl.ds(pl.multiple_of(c * 2 * part, 16), 2 * part)
            here = iota((2 * part, slots), 0) + c * 2 * part
            there = position((2 * part, slots), 1, 0)
            pick = jnp.where(here == there, 1.0, 0.0).astype(BF)
            total = nn(pick, out_s[...].astype(BF))
            pick = jnp.where(here == there + cap, 1.0, 0.0).astype(BF)
            total = total + nn(pick, row_s[...].astype(BF))
            ret_ref[at, :] = total.astype(BF)
            return carry

        lax.fori_loop(0, 4, give, 0)


def expert(cap, recv, up, down, earlier):
    first = earlier is None
    total, width = recv.shape
    slots = total // 2
    hidden = up.shape[2]
    tile = 512
    dtype = F32 if first else BF
    up_block = pl.BlockSpec((width, tile), lambda i: (0, i))
    down_block = pl.BlockSpec((tile, width), lambda i: (i, 0))
    in_specs = [
        whole_spec(recv.shape),
        pl.BlockSpec((1, width, tile), lambda i: (0, 0, i)),
        pl.BlockSpec((1, tile, width), lambda i: (0, i, 0)),
    ]
    args = [recv, up, down]
    if not first:
        in_specs += [up_block, down_block]
        args += list(earlier)
    return pl.pallas_call(
        functools.partial(expert_kernel, cap, first),
        grid=(hidden // tile,),
        in_specs=in_specs,
        out_specs=[whole_spec(recv.shape), up_block, down_block],
        out_shape=(
            jax.ShapeDtypeStruct(recv.shape, BF),
            jax.ShapeDtypeStruct((width, hidden), dtype),
            jax.ShapeDtypeStruct((hidden, width), dtype),
        ),
        scratch_shapes=[
            pltpu.VMEM((slots, width), BF),
            pltpu.VMEM((slots, width), BF),
            pltpu.VMEM((slots, width), F32),
            pltpu.VMEM((slots, width), F32),
        ],
        compiler_params=params(EXPERT_MB),
        cost_estimate=pl.CostEstimate(
            flops=2 * 12 * slots * width * hidden, bytes_accessed=24 * MB, transcendentals=0
        ),
        name="expert",
    )(*args)


def back_kernel(last, micro, *refs):
    take = list(refs)

    def next_refs(count):
        taken, take[:] = take[:count], take[count:]
        return taken

    scal_ref, ret_ref = next_refs(2)
    sources = next_refs(BACK_INS)
    earlier_h = next_refs(4) if last else []
    block_h, dx1_h, dqkv_h = next_refs(3)
    made_h = next_refs(4 if last else 3)
    held = next_refs(BACK_INS)
    (
        meta_ref,
        cot_ref,
        x1_ref,
        g2_ref,
        router_ref,
        mixed_ref,
        wo_ref,
        qkv_ref,
        lse_ref,
        tok_ref,
        g1_ref,
        wqkv_ref,
    ) = held
    in_ref, out_ref, small_ref = next_refs(3)
    block_ref, dx1_ref, dqkv_ref, dmix_s, in_sem, out_sem = next_refs(6)
    if last:
        tail_s, pay_s = next_refs(2)
    sources = [h.at[micro] if h.shape[0] == MICRO else h for h in sources]
    pairs = list(zip(sources, held))
    if last:
        pairs += list(zip(earlier_h[:3], (in_ref, out_ref, small_ref)))
    else:
        pairs = pairs[:-1]
    loads = [move(a, b, in_sem.at[n]) for n, (a, b) in enumerate(pairs[:8])]
    stores = []
    total = ret_ref.shape[0]
    rows, width = x1_ref.shape
    experts = router_ref.shape[0]

    def store(source, target):
        stores.append(move(source, target, out_sem.at[len(stores)]))

    loads[0].wait()
    meta = meta_ref[...]
    gates = [meta[:, k : k + 1] for k in range(2)]
    place = [meta[:, 2 + k : 3 + k].astype(jnp.int32) for k in range(2)]
    picks = [meta[:, 4 + k : 5 + k].astype(jnp.int32) for k in range(2)]
    cap = total // (2 * experts)
    here = iota((rows, total), 1)
    ret = ret_ref[...]
    both = (here == place[0] + cap) | (here == place[1] + cap)
    grad_second = nn(jnp.where(both, 1.0, 0.0).astype(BF), ret)
    pair_out = [nn(jnp.where(here == place[k], 1.0, 0.0).astype(BF), ret) for k in range(2)]
    for n in range(1, 5):
        loads[n].wait()
    loads += [move(a, b, in_sem.at[8 + n]) for n, (a, b) in enumerate(pairs[8:])]
    grad_out = cot_ref[...].astype(F32)
    x_mid = x1_ref[...]
    result = x_mid
    grad_gate = []
    for k in range(2):
        result = result + gates[k] * pair_out[k]
        grad_gate.append(jnp.sum(grad_out * pair_out[k], axis=1, keepdims=True))
    block_ref[...] = result.astype(BF)
    store(block_ref, block_h.at[micro])
    mean_gate = gates[0] * grad_gate[0] + gates[1] * grad_gate[1]
    lane = iota((rows, experts), 1)
    grad_logits = jnp.zeros((rows, experts), F32)
    for k in range(2):
        grad_pick = gates[k] * (grad_gate[k] - mean_gate)
        grad_logits = grad_logits + jnp.where(lane == picks[k], grad_pick, 0.0)
    grad_logits = grad_logits.astype(BF)
    grad_second = grad_second + nn(grad_logits, router_ref[...])
    normed, factor = normalize(x_mid)
    h_second = (normed * g2_ref[...]).astype(BF)
    small = [
        tn(grad_logits, h_second),
        jnp.sum(grad_second * normed, axis=0, keepdims=True),
    ]
    grad_mid = grad_out + norm_back(grad_second * g2_ref[...], normed, factor)
    dx1_ref[...] = grad_mid
    store(dx1_ref, dx1_h)
    for n in range(5, 9):
        loads[n].wait()
    grad_attn = grad_mid.astype(BF)
    out_grad = tn(mixed_ref[...], grad_attn)
    if last:
        slots = 2 * lax.axis_size("exp")
        half = slots // 2
        piece = width // half
        span = half * piece
        tail = SMALL * (experts // 16)

        def lay(s, b, block):
            mine = scal_ref[2] == b
            start = jnp.where(mine, 0, half)
            order = jnp.where(mine, scal_ref[0], scal_ref[1])
            for j in range(half):
                to = pl.multiple_of((start + (j ^ order)) * piece, piece)
                pay_s[s, pl.ds(to, piece), :] = block[j * piece : (j + 1) * piece].astype(BF)

        for copy in loads[13:15]:
            copy.wait()
        lay(1, 1, out_grad + out_ref[...].astype(F32))
        small[0] = small[0] + small_ref[0:experts, :]
        small[1] = small[1] + small_ref[experts : experts + 1, :]
        tail_s[:experts, :] = small[0].astype(BF)
    else:
        out_ref[...] = out_grad.astype(BF)
        small_ref[0:experts, :] = small[0]
        small_ref[experts : experts + 1, :] = small[1]
        small_ref[experts + 1 :, :] = jnp.zeros((small_ref.shape[0] - experts - 1, width), F32)
        store(out_ref, made_h[1])
        store(small_ref, made_h[2])
    dmix_s[...] = nt(grad_attn, wo_ref[...]).astype(BF)

    groups = HEADS // BACK_HEADS
    wide = BACK_HEADS * HEAD
    lines = BACK_HEADS // FORE_HEADS
    def image(i, carry):
        at = pl.ds(pl.multiple_of(i * SEQ, 16), SEQ)
        for g in range(groups):
            query = spread_heads(head_block(qkv_ref, at, 0, g, BACK_HEADS, width))
            key = head_block(qkv_ref, at, 1, g, BACK_HEADS, width)
            value = head_block(qkv_ref, at, 2, g, BACK_HEADS, width)
            grad_mixed = spread_heads(dmix_s[at, g * wide : (g + 1) * wide])
            scores = nt(key, query) * (HEAD**-0.5)
            line = (i * groups + g) * lines
            level = [lse_ref[pl.ds(line + n, 1), :] for n in range(lines)]
            probs = jnp.exp(scores - jnp.concatenate(level, axis=1))
            grad_probs = nt(value, grad_mixed)
            inner = jnp.sum(probs * grad_probs, axis=0, keepdims=True)
            grad_scores = (probs * (grad_probs - inner)).astype(BF)
            grad_value = nn(probs.astype(BF), grad_mixed)
            grad_key = nn(grad_scores, query) * (HEAD**-0.5)
            grad_query = gather_heads(tn(grad_scores, key)) * (HEAD**-0.5)
            for part, grad in enumerate((grad_query, grad_key, grad_value)):
                start = part * width + g * wide
                dqkv_ref[at, start : start + wide] = grad.astype(BF)
        return carry

    lax.fori_loop(0, rows // SEQ, image, 0)

    store(dqkv_ref, dqkv_h)
    loads[9].wait()
    loads[10].wait()
    normed, _ = normalize(tok_ref[...].astype(F32))
    h_first = (normed * g1_ref[...]).astype(BF)
    if last:
        loads[11].wait()
        loads[12].wait()
    gain = jnp.zeros((width, 1), F32)
    for part in (2, 0, 1):
        columns = slice(part * width, (part + 1) * width)
        in_grad = tn(h_first, dqkv_ref[:, columns])
        if not last:
            in_ref[:, columns] = in_grad.astype(BF)
            continue
        in_grad = in_grad + in_ref[:, columns].astype(F32)
        gain = gain + jnp.sum(wqkv_ref[:, columns].astype(F32) * in_grad, axis=1, keepdims=True)
        lay(part // 2, part % 2, in_grad)
        if part != 0:
            s = part // 2
            store(pay_s.at[s, pl.ds(span, span)], made_h[s].at[pl.ds(0, span)])
            store(pay_s.at[s, pl.ds(0, span)], made_h[2 + s].at[pl.ds(0, span)])
    if last:
        eye = iota((width, width), 0) == iota((width, width), 1)
        gain = jnp.sum(jnp.where(eye, gain, 0.0), axis=0, keepdims=True) / g1_ref[...]
        fill = jnp.zeros((tail - experts - 2, width), F32)
        tail_s[experts:, :] = jnp.concatenate([small[1], gain, fill], axis=0).astype(BF)
        for target in (made_h[0], made_h[2]):
            store(tail_s, target.at[pl.ds(span, tail)])
    else:
        store(in_ref, made_h[0])
    for copy in stores:
        copy.wait()


BACK_INS = 12


def back(micro, scal, plan, ret, saved, tokens, cot, wqkv, wo, g1, g2, router_t, earlier):
    last = earlier is not None
    qkv, mixed, x1, lse, meta = saved
    _, rows, width = tokens.shape
    experts = router_t.shape[0]
    slots, piece, tail = plan
    ins = [meta, cot, x1, g2, router_t, mixed, wo, qkv, lse, tokens, g1, wqkv]
    shapes = [
        jax.ShapeDtypeStruct(tokens.shape, BF),
        jax.ShapeDtypeStruct((rows, width), F32),
        jax.ShapeDtypeStruct((rows, 3 * width), BF),
    ]
    sums = [
        jax.ShapeDtypeStruct(wqkv.shape, BF),
        jax.ShapeDtypeStruct(wo.shape, BF),
        jax.ShapeDtypeStruct((experts + 8, width), F32),
    ]

    def hold(value):
        shape = value.shape[1:] if value.shape[0] == MICRO else value.shape
        return pltpu.VMEM(shape, value.dtype)

    scratch = [hold(a) for a in ins + sums + shapes]
    scratch += [
        pltpu.VMEM((rows, width), BF),
        pltpu.SemaphoreType.DMA((16,)),
        pltpu.SemaphoreType.DMA((12,)),
    ]
    aliases = {}
    if last:
        block, *sums = earlier
        args = [scal, ret] + ins + sums + [block]
        aliases = {17: 0}
        span = slots // 2 * piece
        shapes += [jax.ShapeDtypeStruct((span + more, width), BF) for more in (tail, 0)] * 2
        scratch += [pltpu.VMEM((tail, width), BF), pltpu.VMEM((2, slots * piece, width), BF)]
    else:
        args = [scal, ret] + ins
        shapes += sums
    in_specs = [pl.BlockSpec(memory_space=pltpu.SMEM), IN_VMEM] + [IN_HBM] * (len(args) - 2)
    out_specs = [IN_HBM] * len(shapes)
    flops = 2 * rows * width * (3 * ret.shape[0] + 12 * width)
    return pl.pallas_call(
        functools.partial(back_kernel, last, micro),
        in_specs=in_specs,
        out_specs=out_specs,
        out_shape=shapes,
        scratch_shapes=scratch,
        input_output_aliases=aliases,
        compiler_params=params(LAST_MB if last else BACK_MB),
        cost_estimate=pl.CostEstimate(flops=5 * flops, bytes_accessed=20 * MB, transcendentals=0),
        name="back",
    )(*args)


def finish_kernel(dqkv_ref, dx1_ref, tok_ref, wqkv_ref, g1_ref, *refs):
    grad_first = nt(dqkv_ref[...], wqkv_ref[...])
    normed, factor = normalize(tok_ref[0].astype(F32))
    refs[-1][0] = dx1_ref[...] + norm_back(grad_first * g1_ref[...], normed, factor)


def finish(micro, dqkv, dx1, tokens, wqkv, g1, earlier):
    _, rows, width = tokens.shape
    each = rows // 2
    both = pl.BlockSpec((1, each, width), lambda i: (micro, i, 0))
    in_specs = [
        pl.BlockSpec((each, 3 * width), lambda i: (i, 0)),
        pl.BlockSpec((each, width), lambda i: (i, 0)),
        both,
        whole_spec(wqkv.shape),
        whole_spec(g1.shape),
    ]
    args = [dqkv, dx1, tokens, wqkv, g1]
    if earlier is not None:
        args.append(earlier)
        in_specs.append(IN_HBM)
    return pl.pallas_call(
        finish_kernel,
        grid=(2,),
        in_specs=in_specs,
        out_specs=both,
        out_shape=jax.ShapeDtypeStruct(tokens.shape, F32),
        input_output_aliases={} if earlier is None else {5: 0},
        compiler_params=params(FINISH_MB),
        cost_estimate=pl.CostEstimate(
            flops=2 * rows * width * 3 * width, bytes_accessed=6 * MB, transcendentals=0
        ),
        name="finish",
    )(*args)


def local(kernel, shapes, args, scalars=0, scratch=()):
    specs = [pl.BlockSpec(memory_space=pltpu.SMEM)] * scalars
    specs += [pl.BlockSpec(memory_space=pltpu.VMEM)] * (len(args) - scalars)
    size = sum(a.size * 4 for a in args)
    return pl.pallas_call(
        kernel,
        in_specs=specs,
        out_specs=[pl.BlockSpec(memory_space=pltpu.VMEM)] * len(shapes),
        out_shape=shapes,
        scratch_shapes=list(scratch),
        compiler_params=params(32),
        cost_estimate=pl.CostEstimate(flops=1000, bytes_accessed=size, transcendentals=0),
    )(*args)


def halve(keep, arrived, count, piece):
    rows, width = keep.shape
    half = count // 2 * piece
    tail = rows - 2 * half

    def kernel(keep_ref, arrived_ref, send_out, keep_out):
        total = (keep_ref[...].astype(F32) + arrived_ref[...].astype(F32)).astype(BF)
        keep_out[:half, :] = total[:half]
        if tail:
            keep_out[half:, :] = total[2 * half :]
        send_out[...] = total[half:]

    shape = jax.ShapeDtypeStruct((half + tail, width), BF)
    return local(kernel, [shape] * 2, [keep, arrived])


def join(first, second):
    rows, width = first.shape

    def kernel(a, b, out):
        out[:rows, :] = a[...]
        out[rows:, :] = b[...]

    (made,) = local(kernel, [jax.ShapeDtypeStruct((2 * rows, width), BF)], [first, second])
    return made


def reduce_all(sends, keeps, scal, plan, width, experts, beside):
    slots, piece, tail = plan
    size = lax.axis_size("exp")
    bits = size.bit_length() - 1
    orders = halving_orders(size)
    low, high = 1 << (bits - 2), 1 << (bits - 1)
    groups = [low, high, low | high]

    def swap(value, step):
        pairs = []
        for core in range(2):
            mask = 1 << orders[core][step]
            pairs += [(core * size + i, core * size + (i ^ mask)) for i in range(size)]
        return lax.ppermute(value, ("grp", "exp"), pairs)

    def swap_far(value, mask):
        return lax.ppermute(value, "exp", [(i, i ^ mask) for i in range(size)])

    def swap_core(value):
        return lax.ppermute(value, "grp", [(0, 1), (1, 0)])

    arrived = [swap_core(v) for v in sends]
    count = slots // 2
    steps = bits - 2
    for step in range(steps):
        made = [halve(keeps[s], arrived[s], count, piece) for s in range(2)]
        count //= 2
        arrived = [swap(made[s][0], step) for s in range(2)]
        keeps = [v[1] for v in made]

    share = tail // 4
    span = 2 * piece + share

    def quarter(scal_ref, *refs):
        small_s = refs[8]
        for s in range(2):
            total = refs[s][...].astype(F32) + refs[2 + s][...].astype(F32)
            for j in range(4):
                block = total[j * piece : (j + 1) * piece]
                refs[4 + j][s * piece : (s + 1) * piece, :] = block.astype(BF)
            if s == 0:
                small_s[...] = total[4 * piece :]
        for j in range(4):
            part = pl.multiple_of((scal_ref[3] ^ j) * share, share)
            refs[4 + j][2 * piece :, :] = small_s[pl.ds(part, share), :].astype(BF)

    shape = jax.ShapeDtypeStruct((span, width), BF)
    made = local(
        quarter,
        [shape] * 4,
        [scal] + list(keeps) + list(arrived),
        scalars=1,
        scratch=[pltpu.VMEM((tail, width), F32)],
    )
    arrived = [swap_far(made[1 + j], groups[j]) for j in range(3)]
    extra = beside()
    *arrived, extra = lax.optimization_barrier((*arrived, extra))

    def add_up(a, b, c, d, mine_ref):
        total = (a[...].astype(F32) + b[...].astype(F32)) + (c[...].astype(F32) + d[...].astype(F32))
        mine_ref[...] = total.astype(BF)

    (mine,) = local(add_up, [shape], [made[0]] + arrived)

    others = [swap_far(mine, groups[j]) for j in range(3)]

    def lay(scal_ref, a, b, c, d, one_ref, two_ref, small_ref):
        for j, ref in enumerate((a, b, c, d)):
            one_ref[j * piece : (j + 1) * piece, :] = ref[:piece, :]
            two_ref[j * piece : (j + 1) * piece, :] = ref[piece : 2 * piece, :]
            part = pl.multiple_of((scal_ref[3] ^ j) * share, share)
            small_ref[pl.ds(part, share), :] = ref[2 * piece :, :].astype(F32)

    shape = jax.ShapeDtypeStruct((4 * piece, width), BF)
    *have, small = local(
        lay,
        [shape] * 2 + [jax.ShapeDtypeStruct((tail, width), F32)],
        [scal, mine] + others,
        scalars=1,
    )
    vectors = (small[experts + 1], small[experts], small[:experts].T)
    for step in reversed(range(steps)):
        arrived = [swap(have[s], step) for s in range(2)]
        if step == 0:
            arrived[1], vectors = lax.optimization_barrier((arrived[1], vectors))
        have = [join(have[s], arrived[s]) for s in range(2)]
    other = [swap_core(v) for v in have]
    each = slots // 2

    def deal(halves, mine, *refs):
        scal_ref, refs = refs[0], refs[1:]
        in_h, out_h, block_s, sems = refs[-4:]
        core = scal_ref[2]
        part = core if mine else 1 - core
        order = scal_ref[0] if mine else scal_ref[1]
        copies = []
        for n, s in enumerate(halves):
            for pos in range(each):
                to = pl.multiple_of((pos ^ order) * piece, piece)
                block = refs[n][pos * piece : (pos + 1) * piece, :].astype(F32)
                block_s[n, pl.ds(to, piece), :] = block
            if s == 0:
                columns = pl.ds(pl.multiple_of(part * width, width), width)
                copies.append(move(block_s.at[n], in_h.at[:, columns], sems.at[0]))
            else:

                @pl.when(part == 0)
                def _():
                    move(block_s.at[n], in_h.at[:, pl.ds(2 * width, width)], sems.at[1]).wait()

                @pl.when(part == 1)
                def _():
                    move(block_s.at[n], out_h, sems.at[1]).wait()

        for copy in copies:
            copy.wait()

    def dealt(halves, values, grads):
        mine = grads is None
        grads = [] if mine else list(grads)
        count = len(values)
        return pl.pallas_call(
            functools.partial(deal, halves, mine),
            in_specs=[pl.BlockSpec(memory_space=pltpu.SMEM)]
            + [IN_VMEM] * count
            + [IN_HBM] * len(grads),
            out_specs=[IN_HBM, IN_HBM],
            out_shape=(
                jax.ShapeDtypeStruct((width, 3 * width), F32),
                jax.ShapeDtypeStruct((width, width), F32),
            ),
            input_output_aliases={} if mine else {1 + count: 0, 2 + count: 1},
            scratch_shapes=[
                pltpu.VMEM((count, width, width), F32),
                pltpu.SemaphoreType.DMA((2,)),
            ],
            compiler_params=params(16),
            cost_estimate=pl.CostEstimate(flops=1000, bytes_accessed=4 * MB, transcendentals=0),
            name="deal",
        )(scal, *values, *grads)

    grads = dealt((0, 1), have, None)
    in_grad, out_grad = dealt((0, 1), other, grads)
    return in_grad, out_grad, *vectors, extra


def halving_orders(size):
    bits = size.bit_length() - 1
    first = list(range(bits - 2))
    second = [first[b ^ 1] if (b ^ 1) < len(first) else b for b in first]
    return first, second


def places(size):
    bits = size.bit_length() - 1
    core = lax.axis_index("grp")
    me = lax.axis_index("exp")
    last = me >> (bits - 2)
    made = []
    for order in halving_orders(size):
        value = jnp.zeros_like(me)
        for b in order:
            value = value * 2 + ((me >> b) & 1)
        made.append(value * 4 + last)
    own = jnp.where(core == 0, made[0], made[1])
    other = jnp.where(core == 0, made[1], made[0])
    return jnp.stack([own, other, core, last]).astype(jnp.int32)


def shards(
    tokens,
    expert_picks,
    priority_ranks,
    attn_input,
    attn_output,
    first_gain,
    second_gain,
    router_weight,
    expert_up,
    expert_down,
    cotangent,
):
    size = lax.axis_size("exp")
    experts = router_weight.shape[1]
    rows, width = tokens.shape[1:]
    cap = max(2, rows // size)
    total = experts * 2 * cap
    slots = 2 * size
    plan = (slots, 2 * width // slots, SMALL * (experts // 16))
    scal = places(size)
    picks_t = jnp.transpose(expert_picks, (0, 2, 1))
    router_t = router_weight.T
    g1 = first_gain.reshape(1, width)
    g2 = second_gain.reshape(1, width)

    def exchange(value):
        value = value.reshape(experts, 2 * cap, width)
        value = lax.all_to_all(value, "exp", split_axis=0, concat_axis=0, tiled=True)
        return value.reshape(total, width)

    saved, sent = [], []
    for micro in range(MICRO):
        made = fore(
            micro,
            cap,
            tokens,
            picks_t,
            priority_ranks,
            attn_input,
            attn_output,
            g1,
            g2,
            router_t,
            cotangent,
        )
        sent.append(made[0])
        saved.append(made[1:])
    arrived = [exchange(v) for v in sent]
    answer0, up0, down0 = expert(cap, arrived[0], expert_up, expert_down, None)
    answer1, up1, down1 = expert(cap, arrived[1], expert_up, expert_down, (up0, down0))
    ret = [exchange(v) for v in (answer0, answer1)]
    up_other = lax.ppermute(up1, "grp", [(0, 1), (1, 0)])
    down_other = lax.ppermute(down1, "grp", [(0, 1), (1, 0)])

    weights = (attn_input, attn_output, g1, g2, router_t)
    block, dx0, dqkv0, *sums = back(
        0, scal, plan, ret[0], saved[0], tokens, cotangent, *weights, None
    )
    halves = lax.optimization_barrier((up1, up_other, down1, down_other, sums[2]))
    up_sum = halves[0].astype(F32) + halves[1].astype(F32)
    down_sum = halves[2].astype(F32) + halves[3].astype(F32)
    first = finish(0, dqkv0, dx0, tokens, attn_input, g1, None)
    first, up_sum, down_sum, sums[2] = lax.optimization_barrier((first, up_sum, down_sum, halves[4]))
    block, dx1, dqkv1, *pay = back(
        1, scal, plan, ret[1], saved[1], tokens, cotangent, *weights, (block, *sums)
    )

    def beside():
        return finish(1, dqkv1, dx1, tokens, attn_input, g1, first)

    *dense, tokens_grad = reduce_all(pay[:2], pay[2:], scal, plan, width, experts, beside)
    return (block, tokens_grad, *dense, up_sum[None], down_sum[None])


def solution(mesh):
    split = P(None, ("grp", "exp"), None)
    owned = P("exp", None, None)
    in_specs = (split,) * 3 + (P(),) * 5 + (owned, owned, split)
    out_specs = (split, split) + (P(),) * 5 + (owned, owned)
    return jax.shard_map(shards, mesh=mesh, in_specs=in_specs, out_specs=out_specs, check_vma=False)
```

```python
import functools

import jax
import jax.numpy as jnp
from jax import lax
from jax.experimental import pallas as pl
from jax.experimental.pallas import tpu as pltpu
from jax.sharding import PartitionSpec as P

HEADS = 8
HEAD = 64
SEQ = 144
MICRO = 2
EPS = 1e-06
FORE_HEADS = 2
BACK_HEADS = 4
GELU_C = 0.7978845608028654
GELU_A = 0.044715
SMALL = 32

BF = jnp.bfloat16
F32 = jnp.float32
MB = 1 << 20
FORE_MB = 60
EXPERT_MB = 48
BACK_MB = 60
FINISH_MB = 60
LAST_MB = 50
FILLS = 4
IN_VMEM = pl.BlockSpec(memory_space=pltpu.VMEM)
IN_HBM = pl.BlockSpec(memory_space=pltpu.HBM)


def nn(a, b):
    return lax.dot_general(a, b, (((1,), (0,)), ((), ())), preferred_element_type=F32)


def nt(a, b):
    return lax.dot_general(a, b, (((1,), (1,)), ((), ())), preferred_element_type=F32)


def tn(a, b):
    return lax.dot_general(a, b, (((0,), (0,)), ((), ())), preferred_element_type=F32)


def normalize(values):
    center = values - jnp.mean(values, axis=-1, keepdims=True)
    factor = lax.rsqrt(jnp.mean(center * center, axis=-1, keepdims=True) + EPS)
    return center * factor, factor


def norm_back(grad_normed, normed, factor):
    return factor * (
        grad_normed
        - jnp.mean(grad_normed, axis=-1, keepdims=True)
        - normed * jnp.mean(grad_normed * normed, axis=-1, keepdims=True)
    )


def iota(shape, dim):
    return lax.broadcasted_iota(jnp.int32, shape, dim)


def spread_heads(block):
    head = iota(block.shape, 1) // HEAD
    zero = jnp.zeros_like(block)
    count = block.shape[1] // HEAD
    return jnp.concatenate([jnp.where(head == h, block, zero) for h in range(count)], axis=0)


def gather_heads(full):
    count = full.shape[1] // HEAD
    rows = full.shape[0] // count
    head = iota((rows, full.shape[1]), 1) // HEAD
    total = jnp.where(head == 0, full[:rows], 0.0)
    for h in range(1, count):
        total = total + jnp.where(head == h, full[h * rows : (h + 1) * rows], 0.0)
    return total


def head_block(ref, rows, part, group, count, width):
    start = part * width + group * count * HEAD
    return ref[rows, start : start + count * HEAD]


def fore_kernel(cap, micro, *refs):
    tok_h, pick_h, rank_h, wqkv_h, wo_h, g1_h, g2_h, router_h, cot_h = refs[:9]
    send_h, qkv_h, mixed_h, x1_h, lse_h, meta_h = refs[9:15]
    tok_ref, pick_ref, rank_ref, wqkv_ref, wo_ref, g1_ref, g2_ref, router_ref, cot_ref = refs[15:24]
    send_ref, qkv_ref, mixed_ref, x1_ref, lse_ref, meta_ref = refs[24:30]
    all_s, in_sem, out_sem = refs[30:]
    rows, width = x1_ref.shape
    experts = router_ref.shape[0]
    images = rows // SEQ
    pairs = (
        (pick_h.at[micro], pick_ref),
        (rank_h.at[micro], rank_ref),
        (tok_h.at[micro], tok_ref),
        (g1_h, g1_ref),
        (wqkv_h, wqkv_ref),
        (wo_h, wo_ref),
        (g2_h, g2_ref),
        (router_h, router_ref),
        (cot_h.at[micro], cot_ref),
    )
    loads = [move(a, b, in_sem.at[n]) for n, (a, b) in enumerate(pairs)]

    loads[0].wait()
    loads[1].wait()
    rank_row = rank_ref[...].astype(F32)
    eye = iota((rows, rows), 0) == iota((rows, rows), 1)
    rank_col = jnp.sum(jnp.where(eye, rank_row, 0.0), axis=1, keepdims=True)
    less = jnp.where(rank_col < rank_row, 1.0, 0.0).astype(BF)
    picks = pick_ref[...]
    expert = iota((experts, rows), 0)
    on = [jnp.where(expert == picks[k : k + 1], 1.0, 0.0) for k in range(2)]
    before = [nn(on[k].astype(BF), less) for k in range(2)]
    before[1] = before[1] + jnp.sum(on[0], axis=1, keepdims=True)
    place = []
    for k in range(2):
        slot = jnp.sum(on[k] * before[k], axis=0, keepdims=True)
        base = picks[k : k + 1].astype(F32) * (2 * cap)
        place.append(jnp.where(slot < cap - 0.5, base + slot, -9999.0))

    loads[2].wait()
    loads[3].wait()
    x_in = tok_ref[...].astype(F32)
    normed, _ = normalize(x_in)
    h_first = (normed * g1_ref[...]).astype(BF)
    loads[4].wait()
    qkv_ref[...] = nn(h_first, wqkv_ref[...]).astype(BF)
    stores = [move(qkv_ref, qkv_h, out_sem.at[1])]

    groups = HEADS // FORE_HEADS
    wide = FORE_HEADS * HEAD
    def image(i, carry):
        at = pl.ds(pl.multiple_of(i * SEQ, 16), SEQ)
        for g in range(groups):
            query = spread_heads(head_block(qkv_ref, at, 0, g, FORE_HEADS, width))
            key = head_block(qkv_ref, at, 1, g, FORE_HEADS, width)
            value = head_block(qkv_ref, at, 2, g, FORE_HEADS, width)
            scores = nt(key, query) * (HEAD**-0.5)
            peak = jnp.max(scores, axis=0, keepdims=True)
            expo = jnp.exp(scores - peak)
            denom = jnp.sum(expo, axis=0, keepdims=True)
            probs_low = (expo * (1.0 / denom)).astype(BF)
            line = i * groups + g
            lse_ref[pl.ds(line, 1), :] = peak + jnp.log(denom)
            mixed = gather_heads(tn(probs_low, value))
            mixed_ref[at, g * wide : (g + 1) * wide] = mixed.astype(BF)
        return carry

    lax.fori_loop(0, images, image, 0, unroll=micro == 0)

    stores.append(move(mixed_ref, mixed_h, out_sem.at[2]))
    stores.append(move(lse_ref, lse_h, out_sem.at[4]))

    for n in range(5, 9):
        loads[n].wait()
    x_mid = tok_ref[...].astype(F32) + nn(mixed_ref[...], wo_ref[...])
    x1_ref[...] = x_mid
    stores.append(move(x1_ref, x1_h, out_sem.at[3]))
    normed, _ = normalize(x_mid)
    h_second = (normed * g2_ref[...]).astype(BF)
    all_s[:rows, :] = h_second
    logits = nt(router_ref[...], h_second)
    picked = [jnp.sum(on[k] * logits, axis=0, keepdims=True) for k in range(2)]
    top = jnp.maximum(picked[0], picked[1])
    expo = [jnp.exp(v - top) for v in picked]
    total = expo[0] + expo[1]
    gates = [v / total for v in expo]
    stack = jnp.concatenate(
        gates + place + [picks.astype(F32)] + [jnp.zeros((2, rows), F32)], axis=0
    )
    meta = jnp.transpose(stack)
    meta_ref[...] = meta
    stores.append(move(meta_ref, meta_h, out_sem.at[5]))
    grad_out = cot_ref[...].astype(F32)
    all_s[rows : 2 * rows, :] = (meta[:, 0:1] * grad_out).astype(BF)
    all_s[2 * rows :, :] = (meta[:, 1:2] * grad_out).astype(BF)
    place = [v.astype(jnp.int32) for v in place]

    gone = jnp.full((1, 2 * rows), -1, jnp.int32)
    pos_a = jnp.concatenate([place[0], place[0] + cap, place[1] + cap], axis=1)
    pos_b = jnp.concatenate([place[1], gone], axis=1)
    step = send_ref.shape[0] // FILLS
    for c in range(FILLS):
        start = c * step
        row = iota((step, 3 * rows), 0) + start
        first = jnp.where((row == pos_a) | (row == pos_b), 1.0, 0.0).astype(BF)
        part = nn(first, all_s[...])
        send_ref[pl.ds(start, step), :] = part.astype(BF)
        at = pl.ds(start, step)
        stores.append(move(send_ref.at[at], send_h.at[at], out_sem.at[6 + c]))
    for copy in stores:
        copy.wait()


def move(source, target, sem):
    copy = pltpu.make_async_copy(source, target, sem)
    copy.start()
    return copy


def micro_spec(shape, micro):
    return pl.BlockSpec((1,) + tuple(shape[1:]), lambda i: (micro,) + (0,) * (len(shape) - 1))


def whole_spec(shape):
    return pl.BlockSpec(tuple(shape), lambda i: (0,) * len(shape))


def params(limit, **more):
    return pltpu.CompilerParams(vmem_limit_bytes=limit * MB, **more)


def fore(micro, cap, tokens, picks_t, ranks, wqkv, wo, g1, g2, router_t, cot):
    _, rows, width = tokens.shape
    experts = router_t.shape[0]
    out_shape = (
        jax.ShapeDtypeStruct((experts * 2 * cap, width), BF),
        jax.ShapeDtypeStruct((rows, 3 * width), BF),
        jax.ShapeDtypeStruct((rows, width), BF),
        jax.ShapeDtypeStruct((rows, width), F32),
        jax.ShapeDtypeStruct((rows // SEQ * HEADS // FORE_HEADS, FORE_HEADS * SEQ), F32),
        jax.ShapeDtypeStruct((rows, 8), F32),
    )
    flops = 2 * rows * width * (4 * width + 3 * experts * 2 * cap + 4 * SEQ)
    return pl.pallas_call(
        functools.partial(fore_kernel, cap, micro),
        in_specs=[IN_HBM] * 9,
        out_specs=[IN_HBM] * 6,
        out_shape=out_shape,
        scratch_shapes=[
            pltpu.VMEM((rows, width), BF),
            pltpu.VMEM(picks_t.shape[1:], jnp.int32),
            pltpu.VMEM(ranks.shape[1:], jnp.int32),
            pltpu.VMEM(wqkv.shape, BF),
            pltpu.VMEM(wo.shape, BF),
            pltpu.VMEM(g1.shape, F32),
            pltpu.VMEM(g2.shape, F32),
            pltpu.VMEM(router_t.shape, BF),
            pltpu.VMEM((rows, width), BF),
        ]
        + [pltpu.VMEM(v.shape, v.dtype) for v in out_shape]
        + [pltpu.VMEM((3 * rows, width), BF)]
        + [pltpu.SemaphoreType.DMA((9,)), pltpu.SemaphoreType.DMA((6 + FILLS,))],
        compiler_params=params(FORE_MB),
        cost_estimate=pl.CostEstimate(flops=4 * flops, bytes_accessed=8 * MB, transcendentals=0),
        name="fore",
    )(tokens, picks_t, ranks, wqkv, wo, g1, g2, router_t, cot)


def expert_kernel(cap, first, *refs):
    if first:
        recv_ref, up_ref, down_ref, ret_ref, dup_ref, ddown_ref = refs[:6]
    else:
        recv_ref, up_ref, down_ref, aup_ref, adown_ref, ret_ref, dup_ref, ddown_ref = refs[:8]
    h_s, g_s, out_s, row_s = refs[-4:]
    step = pl.program_id(0)
    steps = pl.num_programs(0)
    slots = h_s.shape[0]

    def position(shape, dim, start):
        slot = iota(shape, dim) + start
        block = ((slot.astype(F32) + 0.5) * (1.0 / cap)).astype(jnp.int32)
        return slot + block * cap

    part = slots // 4

    @pl.when(step == 0)
    def _():
        def take(c, carry):
            at = pl.ds(pl.multiple_of(c * part, 16), part)
            here = iota((part, 2 * slots), 1)
            there = position((part, 2 * slots), 0, c * part)
            pick = jnp.where(here == there, 1.0, 0.0).astype(BF)
            h_s[at, :] = nn(pick, recv_ref[...]).astype(BF)
            pick = jnp.where(here == there + cap, 1.0, 0.0).astype(BF)
            g_s[at, :] = nn(pick, recv_ref[...]).astype(BF)
            return carry

        lax.fori_loop(0, 4, take, 0)

    up = up_ref[0]
    down = down_ref[0]
    h = h_s[...]
    g = g_s[...]
    pre = nn(h, up)
    grad_act = nt(g, down)
    square = pre * pre
    tanh = jnp.tanh(GELU_C * pre * (1.0 + GELU_A * square))
    half = 0.5 + 0.5 * tanh
    act = (pre * half).astype(BF)
    slope = half + (0.5 * GELU_C) * pre * (1.0 - tanh * tanh) * (1.0 + 3.0 * GELU_A * square)
    grad_pre = (grad_act * slope).astype(BF)
    grad_up = tn(h, grad_pre)
    grad_down = tn(act, g)
    if not first:
        grad_up = grad_up + aup_ref[...]
        grad_down = grad_down + adown_ref[...]
    dup_ref[...] = grad_up.astype(dup_ref.dtype)
    ddown_ref[...] = grad_down.astype(ddown_ref.dtype)
    out = nn(act, down)
    row = nt(grad_pre, up)

    @pl.when(step == 0)
    def _():
        out_s[...] = out
        row_s[...] = row

    @pl.when(step > 0)
    def _():
        out_s[...] += out
        row_s[...] += row

    @pl.when(step == steps - 1)
    def _():
        def give(c, carry):
            at = pl.ds(pl.multiple_of(c * 2 * part, 16), 2 * part)
            here = iota((2 * part, slots), 0) + c * 2 * part
            there = position((2 * part, slots), 1, 0)
            pick = jnp.where(here == there, 1.0, 0.0).astype(BF)
            total = nn(pick, out_s[...].astype(BF))
            pick = jnp.where(here == there + cap, 1.0, 0.0).astype(BF)
            total = total + nn(pick, row_s[...].astype(BF))
            ret_ref[at, :] = total.astype(BF)
            return carry

        lax.fori_loop(0, 4, give, 0)


def expert(cap, recv, up, down, earlier):
    first = earlier is None
    total, width = recv.shape
    slots = total // 2
    hidden = up.shape[2]
    tile = 512
    dtype = F32 if first else BF
    up_block = pl.BlockSpec((width, tile), lambda i: (0, i))
    down_block = pl.BlockSpec((tile, width), lambda i: (i, 0))
    in_specs = [
        whole_spec(recv.shape),
        pl.BlockSpec((1, width, tile), lambda i: (0, 0, i)),
        pl.BlockSpec((1, tile, width), lambda i: (0, i, 0)),
    ]
    args = [recv, up, down]
    if not first:
        in_specs += [up_block, down_block]
        args += list(earlier)
    return pl.pallas_call(
        functools.partial(expert_kernel, cap, first),
        grid=(hidden // tile,),
        in_specs=in_specs,
        out_specs=[whole_spec(recv.shape), up_block, down_block],
        out_shape=(
            jax.ShapeDtypeStruct(recv.shape, BF),
            jax.ShapeDtypeStruct((width, hidden), dtype),
            jax.ShapeDtypeStruct((hidden, width), dtype),
        ),
        scratch_shapes=[
            pltpu.VMEM((slots, width), BF),
            pltpu.VMEM((slots, width), BF),
            pltpu.VMEM((slots, width), F32),
            pltpu.VMEM((slots, width), F32),
        ],
        compiler_params=params(EXPERT_MB),
        cost_estimate=pl.CostEstimate(
            flops=2 * 12 * slots * width * hidden, bytes_accessed=24 * MB, transcendentals=0
        ),
        name="expert",
    )(*args)


def back_kernel(last, micro, *refs):
    take = list(refs)

    def next_refs(count):
        taken, take[:] = take[:count], take[count:]
        return taken

    scal_ref, ret_ref = next_refs(2)
    sources = next_refs(BACK_INS)
    earlier_h = next_refs(4) if last else []
    block_h, dx1_h = next_refs(2)
    (dqkv_h,) = next_refs(1) if last else (None,)
    made_h = next_refs(4 if last else 3)
    held = next_refs(BACK_INS)
    (
        meta_ref,
        cot_ref,
        x1_ref,
        g2_ref,
        router_ref,
        mixed_ref,
        wo_ref,
        qkv_ref,
        lse_ref,
        tok_ref,
        g1_ref,
        wqkv_ref,
    ) = held
    in_ref, out_ref, small_ref = next_refs(3)
    block_ref, dx1_ref, dqkv_ref, dmix_s, in_sem, out_sem = next_refs(6)
    if last:
        tail_s, pay_s = next_refs(2)
    sources = [h.at[micro] if h.shape[0] == MICRO else h for h in sources]
    pairs = list(zip(sources, held))
    if last:
        pairs += list(zip(earlier_h[:3], (in_ref, out_ref, small_ref)))
    loads = [move(a, b, in_sem.at[n]) for n, (a, b) in enumerate(pairs[:8])]
    stores = []
    total = ret_ref.shape[0]
    rows, width = x1_ref.shape
    experts = router_ref.shape[0]

    def store(source, target):
        stores.append(move(source, target, out_sem.at[len(stores)]))

    loads[0].wait()
    meta = meta_ref[...]
    gates = [meta[:, k : k + 1] for k in range(2)]
    place = [meta[:, 2 + k : 3 + k].astype(jnp.int32) for k in range(2)]
    picks = [meta[:, 4 + k : 5 + k].astype(jnp.int32) for k in range(2)]
    cap = total // (2 * experts)
    here = iota((rows, total), 1)
    ret = ret_ref[...]
    both = (here == place[0] + cap) | (here == place[1] + cap)
    grad_second = nn(jnp.where(both, 1.0, 0.0).astype(BF), ret)
    pair_out = [nn(jnp.where(here == place[k], 1.0, 0.0).astype(BF), ret) for k in range(2)]
    for n in range(1, 5):
        loads[n].wait()
    loads += [move(a, b, in_sem.at[8 + n]) for n, (a, b) in enumerate(pairs[8:])]
    grad_out = cot_ref[...].astype(F32)
    x_mid = x1_ref[...]
    result = x_mid
    grad_gate = []
    for k in range(2):
        result = result + gates[k] * pair_out[k]
        grad_gate.append(jnp.sum(grad_out * pair_out[k], axis=1, keepdims=True))
    block_ref[...] = result.astype(BF)
    store(block_ref, block_h.at[micro])
    mean_gate = gates[0] * grad_gate[0] + gates[1] * grad_gate[1]
    lane = iota((rows, experts), 1)
    grad_logits = jnp.zeros((rows, experts), F32)
    for k in range(2):
        grad_pick = gates[k] * (grad_gate[k] - mean_gate)
        grad_logits = grad_logits + jnp.where(lane == picks[k], grad_pick, 0.0)
    grad_logits = grad_logits.astype(BF)
    grad_second = grad_second + nn(grad_logits, router_ref[...])
    normed, factor = normalize(x_mid)
    h_second = (normed * g2_ref[...]).astype(BF)
    small = [
        tn(grad_logits, h_second),
        jnp.sum(grad_second * normed, axis=0, keepdims=True),
    ]
    grad_mid = grad_out + norm_back(grad_second * g2_ref[...], normed, factor)
    dx1_ref[...] = grad_mid
    if last:
        store(dx1_ref, dx1_h)
    for n in range(5, 9):
        loads[n].wait()
    grad_attn = grad_mid.astype(BF)
    out_grad = tn(mixed_ref[...], grad_attn)
    if last:
        slots = 2 * lax.axis_size("exp")
        half = slots // 2
        piece = width // half
        span = half * piece
        tail = SMALL * (experts // 16)

        def lay(s, b, block):
            mine = scal_ref[2] == b
            start = jnp.where(mine, 0, half)
            order = jnp.where(mine, scal_ref[0], scal_ref[1])
            for j in range(half):
                to = pl.multiple_of((start + (j ^ order)) * piece, piece)
                pay_s[s, pl.ds(to, piece), :] = block[j * piece : (j + 1) * piece].astype(BF)

        for copy in loads[13:15]:
            copy.wait()
        lay(1, 1, out_grad + out_ref[...].astype(F32))
        small[0] = small[0] + small_ref[0:experts, :]
        small[1] = small[1] + small_ref[experts : experts + 1, :]
        tail_s[:experts, :] = small[0].astype(BF)
    else:
        out_ref[...] = out_grad.astype(BF)
        small_ref[0:experts, :] = small[0]
        small_ref[experts : experts + 1, :] = small[1]
        small_ref[experts + 1 :, :] = jnp.zeros((small_ref.shape[0] - experts - 1, width), F32)
        store(out_ref, made_h[1])
        store(small_ref, made_h[2])
    dmix_s[...] = nt(grad_attn, wo_ref[...]).astype(BF)

    groups = HEADS // BACK_HEADS
    wide = BACK_HEADS * HEAD
    lines = BACK_HEADS // FORE_HEADS
    def image(i, carry):
        at = pl.ds(pl.multiple_of(i * SEQ, 16), SEQ)
        for g in range(groups):
            query = spread_heads(head_block(qkv_ref, at, 0, g, BACK_HEADS, width))
            key = head_block(qkv_ref, at, 1, g, BACK_HEADS, width)
            value = head_block(qkv_ref, at, 2, g, BACK_HEADS, width)
            grad_mixed = spread_heads(dmix_s[at, g * wide : (g + 1) * wide])
            scores = nt(key, query) * (HEAD**-0.5)
            line = (i * groups + g) * lines
            level = [lse_ref[pl.ds(line + n, 1), :] for n in range(lines)]
            probs = jnp.exp(scores - jnp.concatenate(level, axis=1))
            grad_probs = nt(value, grad_mixed)
            inner = jnp.sum(probs * grad_probs, axis=0, keepdims=True)
            grad_scores = (probs * (grad_probs - inner)).astype(BF)
            grad_value = nn(probs.astype(BF), grad_mixed)
            grad_key = nn(grad_scores, query) * (HEAD**-0.5)
            grad_query = gather_heads(tn(grad_scores, key)) * (HEAD**-0.5)
            for part, grad in enumerate((grad_query, grad_key, grad_value)):
                start = part * width + g * wide
                dqkv_ref[at, start : start + wide] = grad.astype(BF)
        return carry

    lax.fori_loop(0, rows // SEQ, image, 0)

    if last:
        store(dqkv_ref, dqkv_h)
    for n in range(9, 13 if last else 12):
        loads[n].wait()
    normed, factor = normalize(tok_ref[...].astype(F32))
    h_first = (normed * g1_ref[...]).astype(BF)
    gain = jnp.zeros((width, 1), F32)
    for part in (2, 0, 1):
        columns = slice(part * width, (part + 1) * width)
        in_grad = tn(h_first, dqkv_ref[:, columns])
        if not last:
            in_ref[:, columns] = in_grad.astype(BF)
            continue
        in_grad = in_grad + in_ref[:, columns].astype(F32)
        gain = gain + jnp.sum(wqkv_ref[:, columns].astype(F32) * in_grad, axis=1, keepdims=True)
        lay(part // 2, part % 2, in_grad)
        if part != 0:
            s = part // 2
            store(pay_s.at[s, pl.ds(span, span)], made_h[s].at[pl.ds(0, span)])
            store(pay_s.at[s, pl.ds(0, span)], made_h[2 + s].at[pl.ds(0, span)])
    if last:
        eye = iota((width, width), 0) == iota((width, width), 1)
        gain = jnp.sum(jnp.where(eye, gain, 0.0), axis=0, keepdims=True) / g1_ref[...]
        fill = jnp.zeros((tail - experts - 2, width), F32)
        tail_s[experts:, :] = jnp.concatenate([small[1], gain, fill], axis=0).astype(BF)
        for target in (made_h[0], made_h[2]):
            store(tail_s, target.at[pl.ds(span, tail)])
    else:
        store(in_ref, made_h[0])
        grad_first = nt(dqkv_ref[...], wqkv_ref[...]) * g1_ref[...]
        dx1_ref[...] = dx1_ref[...] + norm_back(grad_first, normed, factor)
        store(dx1_ref, dx1_h.at[micro])
    for copy in stores:
        copy.wait()


BACK_INS = 12


def back(micro, scal, plan, ret, saved, tokens, cot, wqkv, wo, g1, g2, router_t, earlier):
    last = earlier is not None
    qkv, mixed, x1, lse, meta = saved
    _, rows, width = tokens.shape
    experts = router_t.shape[0]
    slots, piece, tail = plan
    ins = [meta, cot, x1, g2, router_t, mixed, wo, qkv, lse, tokens, g1, wqkv]
    shapes = [
        jax.ShapeDtypeStruct(tokens.shape, BF),
        jax.ShapeDtypeStruct((rows, width), F32),
        jax.ShapeDtypeStruct((rows, 3 * width), BF),
    ]
    kept = list(shapes)
    if not last:
        shapes = [shapes[0], jax.ShapeDtypeStruct(tokens.shape, F32)]
    sums = [
        jax.ShapeDtypeStruct(wqkv.shape, BF),
        jax.ShapeDtypeStruct(wo.shape, BF),
        jax.ShapeDtypeStruct((experts + 8, width), F32),
    ]

    def hold(value):
        shape = value.shape[1:] if value.shape[0] == MICRO else value.shape
        return pltpu.VMEM(shape, value.dtype)

    scratch = [hold(a) for a in ins + sums + kept]
    scratch += [
        pltpu.VMEM((rows, width), BF),
        pltpu.SemaphoreType.DMA((16,)),
        pltpu.SemaphoreType.DMA((12,)),
    ]
    aliases = {}
    if last:
        block, *sums = earlier
        args = [scal, ret] + ins + sums + [block]
        aliases = {17: 0}
        span = slots // 2 * piece
        shapes += [jax.ShapeDtypeStruct((span + more, width), BF) for more in (tail, 0)] * 2
        scratch += [pltpu.VMEM((tail, width), BF), pltpu.VMEM((2, slots * piece, width), BF)]
    else:
        args = [scal, ret] + ins
        shapes += sums
    in_specs = [pl.BlockSpec(memory_space=pltpu.SMEM), IN_VMEM] + [IN_HBM] * (len(args) - 2)
    out_specs = [IN_HBM] * len(shapes)
    flops = 2 * rows * width * (3 * ret.shape[0] + 12 * width)
    return pl.pallas_call(
        functools.partial(back_kernel, last, micro),
        in_specs=in_specs,
        out_specs=out_specs,
        out_shape=shapes,
        scratch_shapes=scratch,
        input_output_aliases=aliases,
        compiler_params=params(LAST_MB if last else BACK_MB),
        cost_estimate=pl.CostEstimate(flops=5 * flops, bytes_accessed=20 * MB, transcendentals=0),
        name="back",
    )(*args)


def finish_kernel(dqkv_ref, dx1_ref, tok_ref, wqkv_ref, g1_ref, *refs):
    grad_first = nt(dqkv_ref[...], wqkv_ref[...])
    normed, factor = normalize(tok_ref[0].astype(F32))
    refs[-1][0] = dx1_ref[...] + norm_back(grad_first * g1_ref[...], normed, factor)


def finish(micro, dqkv, dx1, tokens, wqkv, g1, earlier):
    _, rows, width = tokens.shape
    each = rows // 2
    both = pl.BlockSpec((1, each, width), lambda i: (micro, i, 0))
    in_specs = [
        pl.BlockSpec((each, 3 * width), lambda i: (i, 0)),
        pl.BlockSpec((each, width), lambda i: (i, 0)),
        both,
        whole_spec(wqkv.shape),
        whole_spec(g1.shape),
    ]
    args = [dqkv, dx1, tokens, wqkv, g1, earlier]
    in_specs.append(IN_HBM)
    return pl.pallas_call(
        finish_kernel,
        grid=(2,),
        in_specs=in_specs,
        out_specs=both,
        out_shape=jax.ShapeDtypeStruct(tokens.shape, F32),
        input_output_aliases={5: 0},
        compiler_params=params(FINISH_MB),
        cost_estimate=pl.CostEstimate(
            flops=2 * rows * width * 3 * width, bytes_accessed=6 * MB, transcendentals=0
        ),
        name="finish",
    )(*args)


def local(kernel, shapes, args, scalars=0, scratch=()):
    specs = [pl.BlockSpec(memory_space=pltpu.SMEM)] * scalars
    specs += [pl.BlockSpec(memory_space=pltpu.VMEM)] * (len(args) - scalars)
    size = sum(a.size * 4 for a in args)
    return pl.pallas_call(
        kernel,
        in_specs=specs,
        out_specs=[pl.BlockSpec(memory_space=pltpu.VMEM)] * len(shapes),
        out_shape=shapes,
        scratch_shapes=list(scratch),
        compiler_params=params(32),
        cost_estimate=pl.CostEstimate(flops=1000, bytes_accessed=size, transcendentals=0),
    )(*args)


def halve(keep, arrived, count, piece):
    rows, width = keep.shape
    half = count // 2 * piece
    tail = rows - 2 * half

    def kernel(keep_ref, arrived_ref, send_out, keep_out):
        total = (keep_ref[...].astype(F32) + arrived_ref[...].astype(F32)).astype(BF)
        keep_out[:half, :] = total[:half]
        if tail:
            keep_out[half:, :] = total[2 * half :]
        send_out[...] = total[half:]

    shape = jax.ShapeDtypeStruct((half + tail, width), BF)
    return local(kernel, [shape] * 2, [keep, arrived])


def join(first, second):
    rows, width = first.shape

    def kernel(a, b, out):
        out[:rows, :] = a[...]
        out[rows:, :] = b[...]

    (made,) = local(kernel, [jax.ShapeDtypeStruct((2 * rows, width), BF)], [first, second])
    return made


def reduce_all(sends, keeps, scal, plan, width, experts, beside):
    slots, piece, tail = plan
    size = lax.axis_size("exp")
    bits = size.bit_length() - 1
    orders = halving_orders(size)
    low, high = 1 << (bits - 2), 1 << (bits - 1)
    groups = [low, high, low | high]

    def swap(value, step):
        pairs = []
        for core in range(2):
            mask = 1 << orders[core][step]
            pairs += [(core * size + i, core * size + (i ^ mask)) for i in range(size)]
        return lax.ppermute(value, ("grp", "exp"), pairs)

    def swap_far(value, mask):
        return lax.ppermute(value, "exp", [(i, i ^ mask) for i in range(size)])

    def swap_core(value):
        return lax.ppermute(value, "grp", [(0, 1), (1, 0)])

    arrived = [swap_core(v) for v in sends]
    count = slots // 2
    steps = bits - 2
    for step in range(steps):
        made = [halve(keeps[s], arrived[s], count, piece) for s in range(2)]
        count //= 2
        arrived = [swap(made[s][0], step) for s in range(2)]
        keeps = [v[1] for v in made]

    share = tail // 4
    span = 2 * piece + share

    def quarter(scal_ref, *refs):
        small_s = refs[8]
        for s in range(2):
            total = refs[s][...].astype(F32) + refs[2 + s][...].astype(F32)
            for j in range(4):
                block = total[j * piece : (j + 1) * piece]
                refs[4 + j][s * piece : (s + 1) * piece, :] = block.astype(BF)
            if s == 0:
                small_s[...] = total[4 * piece :]
        for j in range(4):
            part = pl.multiple_of((scal_ref[3] ^ j) * share, share)
            refs[4 + j][2 * piece :, :] = small_s[pl.ds(part, share), :].astype(BF)

    shape = jax.ShapeDtypeStruct((span, width), BF)
    made = local(
        quarter,
        [shape] * 4,
        [scal] + list(keeps) + list(arrived),
        scalars=1,
        scratch=[pltpu.VMEM((tail, width), F32)],
    )
    arrived = [swap_far(made[1 + j], groups[j]) for j in range(3)]
    extra = beside()
    *arrived, extra = lax.optimization_barrier((*arrived, extra))

    def add_up(a, b, c, d, mine_ref):
        total = (a[...].astype(F32) + b[...].astype(F32)) + (c[...].astype(F32) + d[...].astype(F32))
        mine_ref[...] = total.astype(BF)

    (mine,) = local(add_up, [shape], [made[0]] + arrived)

    others = [swap_far(mine, groups[j]) for j in range(3)]

    def lay(scal_ref, a, b, c, d, one_ref, two_ref, small_ref):
        for j, ref in enumerate((a, b, c, d)):
            one_ref[j * piece : (j + 1) * piece, :] = ref[:piece, :]
            two_ref[j * piece : (j + 1) * piece, :] = ref[piece : 2 * piece, :]
            part = pl.multiple_of((scal_ref[3] ^ j) * share, share)
            small_ref[pl.ds(part, share), :] = ref[2 * piece :, :].astype(F32)

    shape = jax.ShapeDtypeStruct((4 * piece, width), BF)
    *have, small = local(
        lay,
        [shape] * 2 + [jax.ShapeDtypeStruct((tail, width), F32)],
        [scal, mine] + others,
        scalars=1,
    )
    vectors = (small[experts + 1], small[experts], small[:experts].T)
    for step in reversed(range(steps)):
        arrived = [swap(have[s], step) for s in range(2)]
        if step == 0:
            arrived[1], vectors = lax.optimization_barrier((arrived[1], vectors))
        have = [join(have[s], arrived[s]) for s in range(2)]
    other = [swap_core(v) for v in have]
    each = slots // 2

    def deal(halves, mine, *refs):
        scal_ref, refs = refs[0], refs[1:]
        in_h, out_h, block_s, sems = refs[-4:]
        core = scal_ref[2]
        part = core if mine else 1 - core
        order = scal_ref[0] if mine else scal_ref[1]
        copies = []
        for n, s in enumerate(halves):
            for pos in range(each):
                to = pl.multiple_of((pos ^ order) * piece, piece)
                block = refs[n][pos * piece : (pos + 1) * piece, :].astype(F32)
                block_s[n, pl.ds(to, piece), :] = block
            if s == 0:
                columns = pl.ds(pl.multiple_of(part * width, width), width)
                copies.append(move(block_s.at[n], in_h.at[:, columns], sems.at[0]))
            else:

                @pl.when(part == 0)
                def _():
                    move(block_s.at[n], in_h.at[:, pl.ds(2 * width, width)], sems.at[1]).wait()

                @pl.when(part == 1)
                def _():
                    move(block_s.at[n], out_h, sems.at[1]).wait()

        for copy in copies:
            copy.wait()

    def dealt(halves, values, grads):
        mine = grads is None
        grads = [] if mine else list(grads)
        count = len(values)
        return pl.pallas_call(
            functools.partial(deal, halves, mine),
            in_specs=[pl.BlockSpec(memory_space=pltpu.SMEM)]
            + [IN_VMEM] * count
            + [IN_HBM] * len(grads),
            out_specs=[IN_HBM, IN_HBM],
            out_shape=(
                jax.ShapeDtypeStruct((width, 3 * width), F32),
                jax.ShapeDtypeStruct((width, width), F32),
            ),
            input_output_aliases={} if mine else {1 + count: 0, 2 + count: 1},
            scratch_shapes=[
                pltpu.VMEM((count, width, width), F32),
                pltpu.SemaphoreType.DMA((2,)),
            ],
            compiler_params=params(16),
            cost_estimate=pl.CostEstimate(flops=1000, bytes_accessed=4 * MB, transcendentals=0),
            name="deal",
        )(scal, *values, *grads)

    grads = dealt((0, 1), have, None)
    in_grad, out_grad = dealt((0, 1), other, grads)
    return in_grad, out_grad, *vectors, extra


def halving_orders(size):
    bits = size.bit_length() - 1
    first = list(range(bits - 2))
    second = [first[b ^ 1] if (b ^ 1) < len(first) else b for b in first]
    return first, second


def places(size):
    bits = size.bit_length() - 1
    core = lax.axis_index("grp")
    me = lax.axis_index("exp")
    last = me >> (bits - 2)
    made = []
    for order in halving_orders(size):
        value = jnp.zeros_like(me)
        for b in order:
            value = value * 2 + ((me >> b) & 1)
        made.append(value * 4 + last)
    own = jnp.where(core == 0, made[0], made[1])
    other = jnp.where(core == 0, made[1], made[0])
    return jnp.stack([own, other, core, last]).astype(jnp.int32)


def shards(
    tokens,
    expert_picks,
    priority_ranks,
    attn_input,
    attn_output,
    first_gain,
    second_gain,
    router_weight,
    expert_up,
    expert_down,
    cotangent,
):
    size = lax.axis_size("exp")
    experts = router_weight.shape[1]
    rows, width = tokens.shape[1:]
    cap = max(2, rows // size)
    total = experts * 2 * cap
    slots = 2 * size
    plan = (slots, 2 * width // slots, SMALL * (experts // 16))
    scal = places(size)
    picks_t = jnp.transpose(expert_picks, (0, 2, 1))
    router_t = router_weight.T
    g1 = first_gain.reshape(1, width)
    g2 = second_gain.reshape(1, width)

    def exchange(value):
        value = value.reshape(experts, 2 * cap, width)
        value = lax.all_to_all(value, "exp", split_axis=0, concat_axis=0, tiled=True)
        return value.reshape(total, width)

    saved, sent = [], []
    for micro in range(MICRO):
        made = fore(
            micro,
            cap,
            tokens,
            picks_t,
            priority_ranks,
            attn_input,
            attn_output,
            g1,
            g2,
            router_t,
            cotangent,
        )
        sent.append(made[0])
        saved.append(made[1:])
    arrived = [exchange(v) for v in sent]
    answer0, up0, down0 = expert(cap, arrived[0], expert_up, expert_down, None)
    answer1, up1, down1 = expert(cap, arrived[1], expert_up, expert_down, (up0, down0))
    ret = [exchange(v) for v in (answer0, answer1)]
    up_other = lax.ppermute(up1, "grp", [(0, 1), (1, 0)])
    down_other = lax.ppermute(down1, "grp", [(0, 1), (1, 0)])

    weights = (attn_input, attn_output, g1, g2, router_t)
    block, grad0, *sums = back(
        0, scal, plan, ret[0], saved[0], tokens, cotangent, *weights, None
    )
    halves = lax.optimization_barrier((up1, up_other, down1, down_other, sums[2]))
    up_sum = halves[0].astype(F32) + halves[1].astype(F32)
    down_sum = halves[2].astype(F32) + halves[3].astype(F32)
    up_sum, down_sum, sums[2] = lax.optimization_barrier((up_sum, down_sum, halves[4]))
    block, dx1, dqkv1, *pay = back(
        1, scal, plan, ret[1], saved[1], tokens, cotangent, *weights, (block, *sums)
    )

    def beside():
        return finish(1, dqkv1, dx1, tokens, attn_input, g1, grad0)

    *dense, tokens_grad = reduce_all(pay[:2], pay[2:], scal, plan, width, experts, beside)
    return (block, tokens_grad, *dense, up_sum[None], down_sum[None])


def solution(mesh):
    split = P(None, ("grp", "exp"), None)
    owned = P("exp", None, None)
    in_specs = (split,) * 3 + (P(),) * 5 + (owned, owned, split)
    out_specs = (split, split) + (P(),) * 5 + (owned, owned)
    return jax.shard_map(shards, mesh=mesh, in_specs=in_specs, out_specs=out_specs, check_vma=False)
```

```python
import functools

import jax
import jax.numpy as jnp
from jax import lax
from jax.experimental import pallas as pl
from jax.experimental.pallas import tpu as pltpu
from jax.sharding import PartitionSpec as P

HEADS = 8
HEAD = 64
SEQ = 144
MICRO = 2
EPS = 1e-06
FORE_HEADS = 2
BACK_HEADS = 4
GELU_C = 0.7978845608028654
GELU_A = 0.044715
SMALL = 32

BF = jnp.bfloat16
F32 = jnp.float32
MB = 1 << 20
FORE_MB = 60
EXPERT_MB = 48
BACK_MB = 60
FINISH_MB = 60
LAST_MB = 50
FILLS = 4
IN_VMEM = pl.BlockSpec(memory_space=pltpu.VMEM)
IN_HBM = pl.BlockSpec(memory_space=pltpu.HBM)


def nn(a, b):
    return lax.dot_general(a, b, (((1,), (0,)), ((), ())), preferred_element_type=F32)


def nt(a, b):
    return lax.dot_general(a, b, (((1,), (1,)), ((), ())), preferred_element_type=F32)


def tn(a, b):
    return lax.dot_general(a, b, (((0,), (0,)), ((), ())), preferred_element_type=F32)


def normalize(values):
    center = values - jnp.mean(values, axis=-1, keepdims=True)
    factor = lax.rsqrt(jnp.mean(center * center, axis=-1, keepdims=True) + EPS)
    return center * factor, factor


def norm_back(grad_normed, normed, factor):
    return factor * (
        grad_normed
        - jnp.mean(grad_normed, axis=-1, keepdims=True)
        - normed * jnp.mean(grad_normed * normed, axis=-1, keepdims=True)
    )


def iota(shape, dim):
    return lax.broadcasted_iota(jnp.int32, shape, dim)


def spread_heads(block):
    head = iota(block.shape, 1) // HEAD
    zero = jnp.zeros_like(block)
    count = block.shape[1] // HEAD
    return jnp.concatenate([jnp.where(head == h, block, zero) for h in range(count)], axis=0)


def gather_heads(full):
    count = full.shape[1] // HEAD
    rows = full.shape[0] // count
    head = iota((rows, full.shape[1]), 1) // HEAD
    total = jnp.where(head == 0, full[:rows], 0.0)
    for h in range(1, count):
        total = total + jnp.where(head == h, full[h * rows : (h + 1) * rows], 0.0)
    return total


def head_block(ref, rows, part, group, count, width):
    start = part * width + group * count * HEAD
    return ref[rows, start : start + count * HEAD]


def fore_kernel(cap, micro, *refs):
    tok_h, pick_h, rank_h, wqkv_h, wo_h, g1_h, g2_h, router_h, cot_h = refs[:9]
    count = 6 if micro == 0 else 7
    outs, refs = refs[9 : 9 + count], refs[9 + count :]
    send_h, qkv_h, mixed_h, x1_h, level_h, meta_h = outs[:6]
    tok_ref, pick_ref, rank_ref, wqkv_ref, wo_ref, g1_ref, g2_ref, router_ref, cot_ref = refs[:9]
    held, refs = refs[9 : 9 + count], refs[9 + count :]
    send_ref, qkv_ref, mixed_ref, x1_ref, level_ref, meta_ref = held[:6]
    all_s, in_sem, out_sem = refs
    rows, width = x1_ref.shape
    experts = router_ref.shape[0]
    images = rows // SEQ
    pairs = (
        (pick_h.at[micro], pick_ref),
        (rank_h.at[micro], rank_ref),
        (tok_h.at[micro], tok_ref),
        (g1_h, g1_ref),
        (wqkv_h, wqkv_ref),
        (wo_h, wo_ref),
        (g2_h, g2_ref),
        (router_h, router_ref),
        (cot_h.at[micro], cot_ref),
    )
    loads = [move(a, b, in_sem.at[n]) for n, (a, b) in enumerate(pairs)]

    loads[0].wait()
    loads[1].wait()
    rank_row = rank_ref[...].astype(F32)
    eye = iota((rows, rows), 0) == iota((rows, rows), 1)
    rank_col = jnp.sum(jnp.where(eye, rank_row, 0.0), axis=1, keepdims=True)
    less = jnp.where(rank_col < rank_row, 1.0, 0.0).astype(BF)
    picks = pick_ref[...]
    expert = iota((experts, rows), 0)
    on = [jnp.where(expert == picks[k : k + 1], 1.0, 0.0) for k in range(2)]
    before = [nn(on[k].astype(BF), less) for k in range(2)]
    before[1] = before[1] + jnp.sum(on[0], axis=1, keepdims=True)
    place = []
    for k in range(2):
        slot = jnp.sum(on[k] * before[k], axis=0, keepdims=True)
        base = picks[k : k + 1].astype(F32) * (2 * cap)
        place.append(jnp.where(slot < cap - 0.5, base + slot, -9999.0))

    loads[2].wait()
    loads[3].wait()
    x_in = tok_ref[...].astype(F32)
    normed, _ = normalize(x_in)
    h_first = (normed * g1_ref[...]).astype(BF)
    loads[4].wait()
    qkv_ref[...] = nn(h_first, wqkv_ref[...]).astype(BF)
    stores = [move(qkv_ref, qkv_h, out_sem.at[1])]
    if micro > 0:
        held[6][...] = h_first
        stores.append(move(held[6], outs[6], out_sem.at[6 + FILLS]))

    groups = HEADS // FORE_HEADS
    wide = FORE_HEADS * HEAD
    def image(i, carry):
        at = pl.ds(pl.multiple_of(i * SEQ, 16), SEQ)
        for g in range(groups):
            query = spread_heads(head_block(qkv_ref, at, 0, g, FORE_HEADS, width))
            key = head_block(qkv_ref, at, 1, g, FORE_HEADS, width)
            value = head_block(qkv_ref, at, 2, g, FORE_HEADS, width)
            scores = nt(key, query) * (HEAD**-0.5)
            peak = jnp.max(scores, axis=0, keepdims=True)
            expo = jnp.exp(scores - peak)
            denom = jnp.sum(expo, axis=0, keepdims=True)
            probs_low = (expo * (1.0 / denom)).astype(BF)
            if micro == 0:
                level_ref[pl.ds(i * groups + g, 1), :] = peak + jnp.log(denom)
            else:
                each = BACK_HEADS // FORE_HEADS
                line = (i * (HEADS // BACK_HEADS) + g // each) * SEQ
                column = g % each * FORE_HEADS * SEQ
                to = pl.ds(pl.multiple_of(line, 16), SEQ)
                level_ref[to, column : column + FORE_HEADS * SEQ] = probs_low
            mixed = gather_heads(tn(probs_low, value))
            mixed_ref[at, g * wide : (g + 1) * wide] = mixed.astype(BF)
        return carry

    lax.fori_loop(0, images, image, 0, unroll=micro == 0)

    stores.append(move(mixed_ref, mixed_h, out_sem.at[2]))
    stores.append(move(level_ref, level_h, out_sem.at[4]))

    for n in range(5, 9):
        loads[n].wait()
    x_mid = tok_ref[...].astype(F32) + nn(mixed_ref[...], wo_ref[...])
    x1_ref[...] = x_mid
    stores.append(move(x1_ref, x1_h, out_sem.at[3]))
    normed, _ = normalize(x_mid)
    h_second = (normed * g2_ref[...]).astype(BF)
    all_s[:rows, :] = h_second
    logits = nt(router_ref[...], h_second)
    picked = [jnp.sum(on[k] * logits, axis=0, keepdims=True) for k in range(2)]
    top = jnp.maximum(picked[0], picked[1])
    expo = [jnp.exp(v - top) for v in picked]
    total = expo[0] + expo[1]
    gates = [v / total for v in expo]
    stack = jnp.concatenate(
        gates + place + [picks.astype(F32)] + [jnp.zeros((2, rows), F32)], axis=0
    )
    meta = jnp.transpose(stack)
    meta_ref[...] = meta
    stores.append(move(meta_ref, meta_h, out_sem.at[5]))
    grad_out = cot_ref[...].astype(F32)
    all_s[rows : 2 * rows, :] = (meta[:, 0:1] * grad_out).astype(BF)
    all_s[2 * rows :, :] = (meta[:, 1:2] * grad_out).astype(BF)
    place = [v.astype(jnp.int32) for v in place]

    gone = jnp.full((1, 2 * rows), -1, jnp.int32)
    pos_a = jnp.concatenate([place[0], place[0] + cap, place[1] + cap], axis=1)
    pos_b = jnp.concatenate([place[1], gone], axis=1)
    step = send_ref.shape[0] // FILLS
    for c in range(FILLS):
        start = c * step
        row = iota((step, 3 * rows), 0) + start
        first = jnp.where((row == pos_a) | (row == pos_b), 1.0, 0.0).astype(BF)
        part = nn(first, all_s[...])
        send_ref[pl.ds(start, step), :] = part.astype(BF)
        at = pl.ds(start, step)
        stores.append(move(send_ref.at[at], send_h.at[at], out_sem.at[6 + c]))
    for copy in stores:
        copy.wait()


def move(source, target, sem):
    copy = pltpu.make_async_copy(source, target, sem)
    copy.start()
    return copy


def micro_spec(shape, micro):
    return pl.BlockSpec((1,) + tuple(shape[1:]), lambda i: (micro,) + (0,) * (len(shape) - 1))


def whole_spec(shape):
    return pl.BlockSpec(tuple(shape), lambda i: (0,) * len(shape))


def params(limit, **more):
    return pltpu.CompilerParams(vmem_limit_bytes=limit * MB, **more)


def fore(micro, cap, tokens, picks_t, ranks, wqkv, wo, g1, g2, router_t, cot):
    _, rows, width = tokens.shape
    experts = router_t.shape[0]
    out_shape = (
        jax.ShapeDtypeStruct((experts * 2 * cap, width), BF),
        jax.ShapeDtypeStruct((rows, 3 * width), BF),
        jax.ShapeDtypeStruct((rows, width), BF),
        jax.ShapeDtypeStruct((rows, width), F32),
        jax.ShapeDtypeStruct((rows // SEQ * HEADS // FORE_HEADS, FORE_HEADS * SEQ), F32),
        jax.ShapeDtypeStruct((rows, 8), F32),
    )
    if micro > 0:
        probs = jax.ShapeDtypeStruct((rows * HEADS // BACK_HEADS, BACK_HEADS * SEQ), BF)
        first = jax.ShapeDtypeStruct((rows, width), BF)
        out_shape = out_shape[:4] + (probs, out_shape[5], first)
    flops = 2 * rows * width * (4 * width + 3 * experts * 2 * cap + 4 * SEQ)
    return pl.pallas_call(
        functools.partial(fore_kernel, cap, micro),
        in_specs=[IN_HBM] * 9,
        out_specs=[IN_HBM] * len(out_shape),
        out_shape=out_shape,
        scratch_shapes=[
            pltpu.VMEM((rows, width), BF),
            pltpu.VMEM(picks_t.shape[1:], jnp.int32),
            pltpu.VMEM(ranks.shape[1:], jnp.int32),
            pltpu.VMEM(wqkv.shape, BF),
            pltpu.VMEM(wo.shape, BF),
            pltpu.VMEM(g1.shape, F32),
            pltpu.VMEM(g2.shape, F32),
            pltpu.VMEM(router_t.shape, BF),
            pltpu.VMEM((rows, width), BF),
        ]
        + [pltpu.VMEM(v.shape, v.dtype) for v in out_shape]
        + [pltpu.VMEM((3 * rows, width), BF)]
        + [pltpu.SemaphoreType.DMA((9,)), pltpu.SemaphoreType.DMA((7 + FILLS,))],
        compiler_params=params(FORE_MB),
        cost_estimate=pl.CostEstimate(flops=4 * flops, bytes_accessed=8 * MB, transcendentals=0),
        name="fore",
    )(tokens, picks_t, ranks, wqkv, wo, g1, g2, router_t, cot)


def expert_kernel(cap, first, *refs):
    if first:
        recv_ref, up_ref, down_ref, ret_ref, dup_ref, ddown_ref = refs[:6]
    else:
        recv_ref, up_ref, down_ref, aup_ref, adown_ref, ret_ref, dup_ref, ddown_ref = refs[:8]
    h_s, g_s, out_s, row_s = refs[-4:]
    step = pl.program_id(0)
    steps = pl.num_programs(0)
    slots = h_s.shape[0]

    def position(shape, dim, start):
        slot = iota(shape, dim) + start
        block = ((slot.astype(F32) + 0.5) * (1.0 / cap)).astype(jnp.int32)
        return slot + block * cap

    part = slots // 4

    @pl.when(step == 0)
    def _():
        def take(c, carry):
            at = pl.ds(pl.multiple_of(c * part, 16), part)
            here = iota((part, 2 * slots), 1)
            there = position((part, 2 * slots), 0, c * part)
            pick = jnp.where(here == there, 1.0, 0.0).astype(BF)
            h_s[at, :] = nn(pick, recv_ref[...]).astype(BF)
            pick = jnp.where(here == there + cap, 1.0, 0.0).astype(BF)
            g_s[at, :] = nn(pick, recv_ref[...]).astype(BF)
            return carry

        lax.fori_loop(0, 4, take, 0)

    up = up_ref[0]
    down = down_ref[0]
    h = h_s[...]
    g = g_s[...]
    pre = nn(h, up)
    grad_act = nt(g, down)
    square = pre * pre
    tanh = jnp.tanh(GELU_C * pre * (1.0 + GELU_A * square))
    half = 0.5 + 0.5 * tanh
    act = (pre * half).astype(BF)
    slope = half + (0.5 * GELU_C) * pre * (1.0 - tanh * tanh) * (1.0 + 3.0 * GELU_A * square)
    grad_pre = (grad_act * slope).astype(BF)
    grad_up = tn(h, grad_pre)
    grad_down = tn(act, g)
    if not first:
        grad_up = grad_up + aup_ref[...]
        grad_down = grad_down + adown_ref[...]
    dup_ref[...] = grad_up.astype(dup_ref.dtype)
    ddown_ref[...] = grad_down.astype(ddown_ref.dtype)
    out = nn(act, down)
    row = nt(grad_pre, up)

    @pl.when(step == 0)
    def _():
        out_s[...] = out
        row_s[...] = row

    @pl.when(step > 0)
    def _():
        out_s[...] += out
        row_s[...] += row

    @pl.when(step == steps - 1)
    def _():
        def give(c, carry):
            at = pl.ds(pl.multiple_of(c * 2 * part, 16), 2 * part)
            here = iota((2 * part, slots), 0) + c * 2 * part
            there = position((2 * part, slots), 1, 0)
            pick = jnp.where(here == there, 1.0, 0.0).astype(BF)
            total = nn(pick, out_s[...].astype(BF))
            pick = jnp.where(here == there + cap, 1.0, 0.0).astype(BF)
            total = total + nn(pick, row_s[...].astype(BF))
            ret_ref[at, :] = total.astype(BF)
            return carry

        lax.fori_loop(0, 4, give, 0)


def expert(cap, recv, up, down, earlier):
    first = earlier is None
    total, width = recv.shape
    slots = total // 2
    hidden = up.shape[2]
    tile = 512
    dtype = F32 if first else BF
    up_block = pl.BlockSpec((width, tile), lambda i: (0, i))
    down_block = pl.BlockSpec((tile, width), lambda i: (i, 0))
    in_specs = [
        whole_spec(recv.shape),
        pl.BlockSpec((1, width, tile), lambda i: (0, 0, i)),
        pl.BlockSpec((1, tile, width), lambda i: (0, i, 0)),
    ]
    args = [recv, up, down]
    if not first:
        in_specs += [up_block, down_block]
        args += list(earlier)
    return pl.pallas_call(
        functools.partial(expert_kernel, cap, first),
        grid=(hidden // tile,),
        in_specs=in_specs,
        out_specs=[whole_spec(recv.shape), up_block, down_block],
        out_shape=(
            jax.ShapeDtypeStruct(recv.shape, BF),
            jax.ShapeDtypeStruct((width, hidden), dtype),
            jax.ShapeDtypeStruct((hidden, width), dtype),
        ),
        scratch_shapes=[
            pltpu.VMEM((slots, width), BF),
            pltpu.VMEM((slots, width), BF),
            pltpu.VMEM((slots, width), F32),
            pltpu.VMEM((slots, width), F32),
        ],
        compiler_params=params(EXPERT_MB),
        cost_estimate=pl.CostEstimate(
            flops=2 * 12 * slots * width * hidden, bytes_accessed=24 * MB, transcendentals=0
        ),
        name="expert",
    )(*args)


def back_kernel(last, micro, *refs):
    take = list(refs)

    def next_refs(count):
        taken, take[:] = take[:count], take[count:]
        return taken

    scal_ref, ret_ref = next_refs(2)
    sources = next_refs(BACK_INS)
    earlier_h = next_refs(4) if last else []
    block_h, dx1_h = next_refs(2)
    (dqkv_h,) = next_refs(1) if last else (None,)
    made_h = next_refs(4 if last else 3)
    held = next_refs(BACK_INS)
    (
        meta_ref,
        cot_ref,
        x1_ref,
        g2_ref,
        router_ref,
        mixed_ref,
        wo_ref,
        qkv_ref,
        level_ref,
        tok_ref,
        g1_ref,
        wqkv_ref,
    ) = held
    in_ref, out_ref, small_ref = next_refs(3)
    block_ref, dx1_ref, dqkv_ref, dmix_s, in_sem, out_sem = next_refs(6)
    if last:
        tail_s, pay_s = next_refs(2)
    sources = [h.at[micro] if h.shape[0] == MICRO else h for h in sources]
    pairs = list(zip(sources, held))
    if last:
        pairs += list(zip(earlier_h[:3], (in_ref, out_ref, small_ref)))
    loads = [move(a, b, in_sem.at[n]) for n, (a, b) in enumerate(pairs[:8])]
    stores = []
    total = ret_ref.shape[0]
    rows, width = x1_ref.shape
    experts = router_ref.shape[0]

    def store(source, target):
        stores.append(move(source, target, out_sem.at[len(stores)]))

    loads[0].wait()
    meta = meta_ref[...]
    gates = [meta[:, k : k + 1] for k in range(2)]
    place = [meta[:, 2 + k : 3 + k].astype(jnp.int32) for k in range(2)]
    picks = [meta[:, 4 + k : 5 + k].astype(jnp.int32) for k in range(2)]
    cap = total // (2 * experts)
    here = iota((rows, total), 1)
    ret = ret_ref[...]
    both = (here == place[0] + cap) | (here == place[1] + cap)
    grad_second = nn(jnp.where(both, 1.0, 0.0).astype(BF), ret)
    pair_out = [nn(jnp.where(here == place[k], 1.0, 0.0).astype(BF), ret) for k in range(2)]
    for n in range(1, 5):
        loads[n].wait()
    loads += [move(a, b, in_sem.at[8 + n]) for n, (a, b) in enumerate(pairs[8:])]
    grad_out = cot_ref[...].astype(F32)
    x_mid = x1_ref[...]
    result = x_mid
    grad_gate = []
    for k in range(2):
        result = result + gates[k] * pair_out[k]
        grad_gate.append(jnp.sum(grad_out * pair_out[k], axis=1, keepdims=True))
    block_ref[...] = result.astype(BF)
    store(block_ref, block_h.at[micro])
    mean_gate = gates[0] * grad_gate[0] + gates[1] * grad_gate[1]
    lane = iota((rows, experts), 1)
    grad_logits = jnp.zeros((rows, experts), F32)
    for k in range(2):
        grad_pick = gates[k] * (grad_gate[k] - mean_gate)
        grad_logits = grad_logits + jnp.where(lane == picks[k], grad_pick, 0.0)
    grad_logits = grad_logits.astype(BF)
    grad_second = grad_second + nn(grad_logits, router_ref[...])
    normed, factor = normalize(x_mid)
    h_second = (normed * g2_ref[...]).astype(BF)
    small = [
        tn(grad_logits, h_second),
        jnp.sum(grad_second * normed, axis=0, keepdims=True),
    ]
    grad_mid = grad_out + norm_back(grad_second * g2_ref[...], normed, factor)
    dx1_ref[...] = grad_mid
    if last:
        store(dx1_ref, dx1_h)
    for n in range(5, 9):
        loads[n].wait()
    grad_attn = grad_mid.astype(BF)
    out_grad = tn(mixed_ref[...], grad_attn)
    if last:
        slots = 2 * lax.axis_size("exp")
        half = slots // 2
        piece = width // half
        span = half * piece
        tail = SMALL * (experts // 16)

        def lay(s, b, block):
            mine = scal_ref[2] == b
            start = jnp.where(mine, 0, half)
            order = jnp.where(mine, scal_ref[0], scal_ref[1])
            for j in range(half):
                to = pl.multiple_of((start + (j ^ order)) * piece, piece)
                pay_s[s, pl.ds(to, piece), :] = block[j * piece : (j + 1) * piece].astype(BF)

        for copy in loads[13:15]:
            copy.wait()
        lay(1, 1, out_grad + out_ref[...].astype(F32))
        small[0] = small[0] + small_ref[0:experts, :]
        small[1] = small[1] + small_ref[experts : experts + 1, :]
        tail_s[:experts, :] = small[0].astype(BF)
    else:
        out_ref[...] = out_grad.astype(BF)
        small_ref[0:experts, :] = small[0]
        small_ref[experts : experts + 1, :] = small[1]
        small_ref[experts + 1 :, :] = jnp.zeros((small_ref.shape[0] - experts - 1, width), F32)
        store(out_ref, made_h[1])
        store(small_ref, made_h[2])
    dmix_s[...] = nt(grad_attn, wo_ref[...]).astype(BF)

    groups = HEADS // BACK_HEADS
    wide = BACK_HEADS * HEAD
    lines = BACK_HEADS // FORE_HEADS
    def image(i, carry):
        at = pl.ds(pl.multiple_of(i * SEQ, 16), SEQ)
        for g in range(groups):
            query = spread_heads(head_block(qkv_ref, at, 0, g, BACK_HEADS, width))
            key = head_block(qkv_ref, at, 1, g, BACK_HEADS, width)
            value = head_block(qkv_ref, at, 2, g, BACK_HEADS, width)
            grad_mixed = spread_heads(dmix_s[at, g * wide : (g + 1) * wide])
            if last:
                line = pl.multiple_of((i * groups + g) * SEQ, 16)
                probs_low = level_ref[pl.ds(line, SEQ), :]
                probs = probs_low.astype(F32)
            else:
                scores = nt(key, query) * (HEAD**-0.5)
                line = (i * groups + g) * lines
                level = [level_ref[pl.ds(line + n, 1), :] for n in range(lines)]
                probs = jnp.exp(scores - jnp.concatenate(level, axis=1))
                probs_low = probs.astype(BF)
            grad_probs = nt(value, grad_mixed)
            inner = jnp.sum(probs * grad_probs, axis=0, keepdims=True)
            grad_scores = (probs * (grad_probs - inner)).astype(BF)
            grad_value = nn(probs_low, grad_mixed)
            grad_key = nn(grad_scores, query) * (HEAD**-0.5)
            grad_query = gather_heads(tn(grad_scores, key)) * (HEAD**-0.5)
            for part, grad in enumerate((grad_query, grad_key, grad_value)):
                start = part * width + g * wide
                dqkv_ref[at, start : start + wide] = grad.astype(BF)
        return carry

    lax.fori_loop(0, rows // SEQ, image, 0, unroll=last)

    if last:
        store(dqkv_ref, dqkv_h)
    for n in range(9, 13 if last else 12):
        loads[n].wait()
    if last:
        h_first = tok_ref[...]
    else:
        normed, factor = normalize(tok_ref[...].astype(F32))
        h_first = (normed * g1_ref[...]).astype(BF)
    gain = jnp.zeros((width, 1), F32)
    for part in (2, 0, 1):
        columns = slice(part * width, (part + 1) * width)
        in_grad = tn(h_first, dqkv_ref[:, columns])
        if not last:
            in_ref[:, columns] = in_grad.astype(BF)
            continue
        in_grad = in_grad + in_ref[:, columns].astype(F32)
        gain = gain + jnp.sum(wqkv_ref[:, columns].astype(F32) * in_grad, axis=1, keepdims=True)
        lay(part // 2, part % 2, in_grad)
        if part != 0:
            s = part // 2
            store(pay_s.at[s, pl.ds(span, span)], made_h[s].at[pl.ds(0, span)])
            store(pay_s.at[s, pl.ds(0, span)], made_h[2 + s].at[pl.ds(0, span)])
    if last:
        eye = iota((width, width), 0) == iota((width, width), 1)
        gain = jnp.sum(jnp.where(eye, gain, 0.0), axis=0, keepdims=True) / g1_ref[...]
        fill = jnp.zeros((tail - experts - 2, width), F32)
        tail_s[experts:, :] = jnp.concatenate([small[1], gain, fill], axis=0).astype(BF)
        for target in (made_h[0], made_h[2]):
            store(tail_s, target.at[pl.ds(span, tail)])
    else:
        store(in_ref, made_h[0])
        grad_first = nt(dqkv_ref[...], wqkv_ref[...]) * g1_ref[...]
        dx1_ref[...] = dx1_ref[...] + norm_back(grad_first, normed, factor)
        store(dx1_ref, dx1_h.at[micro])
    for copy in stores:
        copy.wait()


BACK_INS = 12


def back(micro, scal, plan, ret, saved, tokens, cot, wqkv, wo, g1, g2, router_t, earlier):
    last = earlier is not None
    qkv, mixed, x1, level, meta, *more = saved
    _, rows, width = tokens.shape
    experts = router_t.shape[0]
    slots, piece, tail = plan
    ins = [meta, cot, x1, g2, router_t, mixed, wo, qkv, level, *(more or [tokens]), g1, wqkv]
    shapes = [
        jax.ShapeDtypeStruct(tokens.shape, BF),
        jax.ShapeDtypeStruct((rows, width), F32),
        jax.ShapeDtypeStruct((rows, 3 * width), BF),
    ]
    kept = list(shapes)
    if not last:
        shapes = [shapes[0], jax.ShapeDtypeStruct(tokens.shape, F32)]
    sums = [
        jax.ShapeDtypeStruct(wqkv.shape, BF),
        jax.ShapeDtypeStruct(wo.shape, BF),
        jax.ShapeDtypeStruct((experts + 8, width), F32),
    ]

    def hold(value):
        shape = value.shape[1:] if value.shape[0] == MICRO else value.shape
        return pltpu.VMEM(shape, value.dtype)

    scratch = [hold(a) for a in ins + sums + kept]
    scratch += [
        pltpu.VMEM((rows, width), BF),
        pltpu.SemaphoreType.DMA((16,)),
        pltpu.SemaphoreType.DMA((12,)),
    ]
    aliases = {}
    if last:
        block, *sums = earlier
        args = [scal, ret] + ins + sums + [block]
        aliases = {17: 0}
        span = slots // 2 * piece
        shapes += [jax.ShapeDtypeStruct((span + more, width), BF) for more in (tail, 0)] * 2
        scratch += [pltpu.VMEM((tail, width), BF), pltpu.VMEM((2, slots * piece, width), BF)]
    else:
        args = [scal, ret] + ins
        shapes += sums
    in_specs = [pl.BlockSpec(memory_space=pltpu.SMEM), IN_VMEM] + [IN_HBM] * (len(args) - 2)
    out_specs = [IN_HBM] * len(shapes)
    flops = 2 * rows * width * (3 * ret.shape[0] + 12 * width)
    return pl.pallas_call(
        functools.partial(back_kernel, last, micro),
        in_specs=in_specs,
        out_specs=out_specs,
        out_shape=shapes,
        scratch_shapes=scratch,
        input_output_aliases=aliases,
        compiler_params=params(LAST_MB if last else BACK_MB),
        cost_estimate=pl.CostEstimate(flops=5 * flops, bytes_accessed=20 * MB, transcendentals=0),
        name="back",
    )(*args)


def finish_kernel(dqkv_ref, dx1_ref, tok_ref, wqkv_ref, g1_ref, *refs):
    grad_first = nt(dqkv_ref[...], wqkv_ref[...])
    normed, factor = normalize(tok_ref[0].astype(F32))
    refs[-1][0] = dx1_ref[...] + norm_back(grad_first * g1_ref[...], normed, factor)


def finish(micro, dqkv, dx1, tokens, wqkv, g1, earlier):
    _, rows, width = tokens.shape
    each = rows // 2
    both = pl.BlockSpec((1, each, width), lambda i: (micro, i, 0))
    in_specs = [
        pl.BlockSpec((each, 3 * width), lambda i: (i, 0)),
        pl.BlockSpec((each, width), lambda i: (i, 0)),
        both,
        whole_spec(wqkv.shape),
        whole_spec(g1.shape),
    ]
    args = [dqkv, dx1, tokens, wqkv, g1, earlier]
    in_specs.append(IN_HBM)
    return pl.pallas_call(
        finish_kernel,
        grid=(2,),
        in_specs=in_specs,
        out_specs=both,
        out_shape=jax.ShapeDtypeStruct(tokens.shape, F32),
        input_output_aliases={5: 0},
        compiler_params=params(FINISH_MB),
        cost_estimate=pl.CostEstimate(
            flops=2 * rows * width * 3 * width, bytes_accessed=6 * MB, transcendentals=0
        ),
        name="finish",
    )(*args)


def local(kernel, shapes, args, scalars=0, scratch=()):
    specs = [pl.BlockSpec(memory_space=pltpu.SMEM)] * scalars
    specs += [pl.BlockSpec(memory_space=pltpu.VMEM)] * (len(args) - scalars)
    size = sum(a.size * 4 for a in args)
    return pl.pallas_call(
        kernel,
        in_specs=specs,
        out_specs=[pl.BlockSpec(memory_space=pltpu.VMEM)] * len(shapes),
        out_shape=shapes,
        scratch_shapes=list(scratch),
        compiler_params=params(32),
        cost_estimate=pl.CostEstimate(flops=1000, bytes_accessed=size, transcendentals=0),
    )(*args)


def halve(keep, arrived, count, piece):
    rows, width = keep.shape
    half = count // 2 * piece
    tail = rows - 2 * half

    def kernel(keep_ref, arrived_ref, send_out, keep_out):
        total = (keep_ref[...].astype(F32) + arrived_ref[...].astype(F32)).astype(BF)
        keep_out[:half, :] = total[:half]
        if tail:
            keep_out[half:, :] = total[2 * half :]
        send_out[...] = total[half:]

    shape = jax.ShapeDtypeStruct((half + tail, width), BF)
    return local(kernel, [shape] * 2, [keep, arrived])


def join(first, second):
    rows, width = first.shape

    def kernel(a, b, out):
        out[:rows, :] = a[...]
        out[rows:, :] = b[...]

    (made,) = local(kernel, [jax.ShapeDtypeStruct((2 * rows, width), BF)], [first, second])
    return made


def reduce_all(sends, keeps, scal, plan, width, experts, beside):
    slots, piece, tail = plan
    size = lax.axis_size("exp")
    bits = size.bit_length() - 1
    orders = halving_orders(size)
    low, high = 1 << (bits - 2), 1 << (bits - 1)
    groups = [low, high, low | high]

    def swap(value, step):
        pairs = []
        for core in range(2):
            mask = 1 << orders[core][step]
            pairs += [(core * size + i, core * size + (i ^ mask)) for i in range(size)]
        return lax.ppermute(value, ("grp", "exp"), pairs)

    def swap_far(value, mask):
        return lax.ppermute(value, "exp", [(i, i ^ mask) for i in range(size)])

    def swap_core(value):
        return lax.ppermute(value, "grp", [(0, 1), (1, 0)])

    arrived = [swap_core(v) for v in sends]
    count = slots // 2
    steps = bits - 2
    for step in range(steps):
        made = [halve(keeps[s], arrived[s], count, piece) for s in range(2)]
        count //= 2
        arrived = [swap(made[s][0], step) for s in range(2)]
        keeps = [v[1] for v in made]

    share = tail // 4
    span = 2 * piece + share

    def quarter(scal_ref, *refs):
        small_s = refs[8]
        for s in range(2):
            total = refs[s][...].astype(F32) + refs[2 + s][...].astype(F32)
            for j in range(4):
                block = total[j * piece : (j + 1) * piece]
                refs[4 + j][s * piece : (s + 1) * piece, :] = block.astype(BF)
            if s == 0:
                small_s[...] = total[4 * piece :]
        for j in range(4):
            part = pl.multiple_of((scal_ref[3] ^ j) * share, share)
            refs[4 + j][2 * piece :, :] = small_s[pl.ds(part, share), :].astype(BF)

    shape = jax.ShapeDtypeStruct((span, width), BF)
    made = local(
        quarter,
        [shape] * 4,
        [scal] + list(keeps) + list(arrived),
        scalars=1,
        scratch=[pltpu.VMEM((tail, width), F32)],
    )
    arrived = [swap_far(made[1 + j], groups[j]) for j in range(3)]
    extra = beside()
    *arrived, extra = lax.optimization_barrier((*arrived, extra))

    def add_up(a, b, c, d, mine_ref):
        total = (a[...].astype(F32) + b[...].astype(F32)) + (c[...].astype(F32) + d[...].astype(F32))
        mine_ref[...] = total.astype(BF)

    (mine,) = local(add_up, [shape], [made[0]] + arrived)

    others = [swap_far(mine, groups[j]) for j in range(3)]

    def lay(scal_ref, a, b, c, d, one_ref, two_ref, small_ref):
        for j, ref in enumerate((a, b, c, d)):
            one_ref[j * piece : (j + 1) * piece, :] = ref[:piece, :]
            two_ref[j * piece : (j + 1) * piece, :] = ref[piece : 2 * piece, :]
            part = pl.multiple_of((scal_ref[3] ^ j) * share, share)
            small_ref[pl.ds(part, share), :] = ref[2 * piece :, :].astype(F32)

    shape = jax.ShapeDtypeStruct((4 * piece, width), BF)
    *have, small = local(
        lay,
        [shape] * 2 + [jax.ShapeDtypeStruct((tail, width), F32)],
        [scal, mine] + others,
        scalars=1,
    )
    vectors = (small[experts + 1], small[experts], small[:experts].T)
    for step in reversed(range(steps)):
        arrived = [swap(have[s], step) for s in range(2)]
        if step == 0:
            arrived[1], vectors = lax.optimization_barrier((arrived[1], vectors))
        have = [join(have[s], arrived[s]) for s in range(2)]
    other = [swap_core(v) for v in have]
    each = slots // 2

    def deal(halves, mine, *refs):
        scal_ref, refs = refs[0], refs[1:]
        in_h, out_h, block_s, sems = refs[-4:]
        core = scal_ref[2]
        part = core if mine else 1 - core
        order = scal_ref[0] if mine else scal_ref[1]
        copies = []
        for n, s in enumerate(halves):
            for pos in range(each):
                to = pl.multiple_of((pos ^ order) * piece, piece)
                block = refs[n][pos * piece : (pos + 1) * piece, :].astype(F32)
                block_s[n, pl.ds(to, piece), :] = block
            if s == 0:
                columns = pl.ds(pl.multiple_of(part * width, width), width)
                copies.append(move(block_s.at[n], in_h.at[:, columns], sems.at[0]))
            else:

                @pl.when(part == 0)
                def _():
                    move(block_s.at[n], in_h.at[:, pl.ds(2 * width, width)], sems.at[1]).wait()

                @pl.when(part == 1)
                def _():
                    move(block_s.at[n], out_h, sems.at[1]).wait()

        for copy in copies:
            copy.wait()

    def dealt(halves, values, grads):
        mine = grads is None
        grads = [] if mine else list(grads)
        count = len(values)
        return pl.pallas_call(
            functools.partial(deal, halves, mine),
            in_specs=[pl.BlockSpec(memory_space=pltpu.SMEM)]
            + [IN_VMEM] * count
            + [IN_HBM] * len(grads),
            out_specs=[IN_HBM, IN_HBM],
            out_shape=(
                jax.ShapeDtypeStruct((width, 3 * width), F32),
                jax.ShapeDtypeStruct((width, width), F32),
            ),
            input_output_aliases={} if mine else {1 + count: 0, 2 + count: 1},
            scratch_shapes=[
                pltpu.VMEM((count, width, width), F32),
                pltpu.SemaphoreType.DMA((2,)),
            ],
            compiler_params=params(16),
            cost_estimate=pl.CostEstimate(flops=1000, bytes_accessed=4 * MB, transcendentals=0),
            name="deal",
        )(scal, *values, *grads)

    grads = dealt((0, 1), have, None)
    in_grad, out_grad = dealt((0, 1), other, grads)
    return in_grad, out_grad, *vectors, extra


def halving_orders(size):
    bits = size.bit_length() - 1
    first = list(range(bits - 2))
    second = [first[b ^ 1] if (b ^ 1) < len(first) else b for b in first]
    return first, second


def places(size):
    bits = size.bit_length() - 1
    core = lax.axis_index("grp")
    me = lax.axis_index("exp")
    last = me >> (bits - 2)
    made = []
    for order in halving_orders(size):
        value = jnp.zeros_like(me)
        for b in order:
            value = value * 2 + ((me >> b) & 1)
        made.append(value * 4 + last)
    own = jnp.where(core == 0, made[0], made[1])
    other = jnp.where(core == 0, made[1], made[0])
    return jnp.stack([own, other, core, last]).astype(jnp.int32)


def shards(
    tokens,
    expert_picks,
    priority_ranks,
    attn_input,
    attn_output,
    first_gain,
    second_gain,
    router_weight,
    expert_up,
    expert_down,
    cotangent,
):
    size = lax.axis_size("exp")
    experts = router_weight.shape[1]
    rows, width = tokens.shape[1:]
    cap = max(2, rows // size)
    total = experts * 2 * cap
    slots = 2 * size
    plan = (slots, 2 * width // slots, SMALL * (experts // 16))
    scal = places(size)
    picks_t = jnp.transpose(expert_picks, (0, 2, 1))
    router_t = router_weight.T
    g1 = first_gain.reshape(1, width)
    g2 = second_gain.reshape(1, width)

    def exchange(value):
        value = value.reshape(experts, 2 * cap, width)
        value = lax.all_to_all(value, "exp", split_axis=0, concat_axis=0, tiled=True)
        return value.reshape(total, width)

    saved, sent = [], []
    for micro in range(MICRO):
        made = fore(
            micro,
            cap,
            tokens,
            picks_t,
            priority_ranks,
            attn_input,
            attn_output,
            g1,
            g2,
            router_t,
            cotangent,
        )
        sent.append(made[0])
        saved.append(made[1:])
    arrived = [exchange(v) for v in sent]
    answer0, up0, down0 = expert(cap, arrived[0], expert_up, expert_down, None)
    answer1, up1, down1 = expert(cap, arrived[1], expert_up, expert_down, (up0, down0))
    ret = [exchange(v) for v in (answer0, answer1)]
    up_other = lax.ppermute(up1, "grp", [(0, 1), (1, 0)])
    down_other = lax.ppermute(down1, "grp", [(0, 1), (1, 0)])

    weights = (attn_input, attn_output, g1, g2, router_t)
    block, grad0, *sums = back(
        0, scal, plan, ret[0], saved[0], tokens, cotangent, *weights, None
    )
    halves = lax.optimization_barrier((up1, up_other, down1, down_other, sums[2]))
    up_sum = halves[0].astype(F32) + halves[1].astype(F32)
    down_sum = halves[2].astype(F32) + halves[3].astype(F32)
    up_sum, down_sum, sums[2] = lax.optimization_barrier((up_sum, down_sum, halves[4]))
    block, dx1, dqkv1, *pay = back(
        1, scal, plan, ret[1], saved[1], tokens, cotangent, *weights, (block, *sums)
    )

    def beside():
        return finish(1, dqkv1, dx1, tokens, attn_input, g1, grad0)

    *dense, tokens_grad = reduce_all(pay[:2], pay[2:], scal, plan, width, experts, beside)
    return (block, tokens_grad, *dense, up_sum[None], down_sum[None])


def solution(mesh):
    split = P(None, ("grp", "exp"), None)
    owned = P("exp", None, None)
    in_specs = (split,) * 3 + (P(),) * 5 + (owned, owned, split)
    out_specs = (split, split) + (P(),) * 5 + (owned, owned)
    return jax.shard_map(shards, mesh=mesh, in_specs=in_specs, out_specs=out_specs, check_vma=False)
```

```python
import functools

import jax
import jax.numpy as jnp
from jax import lax
from jax.experimental import pallas as pl
from jax.experimental.pallas import tpu as pltpu
from jax.sharding import PartitionSpec as P

HEADS = 8
HEAD = 64
SEQ = 144
MICRO = 2
EPS = 1e-06
FORE_HEADS = 2
BACK_HEADS = 4
GELU_C = 0.7978845608028654
GELU_A = 0.044715
SMALL = 32

BF = jnp.bfloat16
F32 = jnp.float32
MB = 1 << 20
FORE_MB = 60
EXPERT_MB = 48
BACK_MB = 60
FINISH_MB = 60
LAST_MB = 50
FILLS = 4
IN_VMEM = pl.BlockSpec(memory_space=pltpu.VMEM)
IN_HBM = pl.BlockSpec(memory_space=pltpu.HBM)


def nn(a, b):
    return lax.dot_general(a, b, (((1,), (0,)), ((), ())), preferred_element_type=F32)


def nt(a, b):
    return lax.dot_general(a, b, (((1,), (1,)), ((), ())), preferred_element_type=F32)


def tn(a, b):
    return lax.dot_general(a, b, (((0,), (0,)), ((), ())), preferred_element_type=F32)


def normalize(values):
    center = values - jnp.mean(values, axis=-1, keepdims=True)
    factor = lax.rsqrt(jnp.mean(center * center, axis=-1, keepdims=True) + EPS)
    return center * factor, factor


def norm_back(grad_normed, normed, factor):
    return factor * (
        grad_normed
        - jnp.mean(grad_normed, axis=-1, keepdims=True)
        - normed * jnp.mean(grad_normed * normed, axis=-1, keepdims=True)
    )


def iota(shape, dim):
    return lax.broadcasted_iota(jnp.int32, shape, dim)


def spread_heads(block):
    head = iota(block.shape, 1) // HEAD
    zero = jnp.zeros_like(block)
    count = block.shape[1] // HEAD
    return jnp.concatenate([jnp.where(head == h, block, zero) for h in range(count)], axis=0)


def gather_heads(full):
    count = full.shape[1] // HEAD
    rows = full.shape[0] // count
    head = iota((rows, full.shape[1]), 1) // HEAD
    total = jnp.where(head == 0, full[:rows], 0.0)
    for h in range(1, count):
        total = total + jnp.where(head == h, full[h * rows : (h + 1) * rows], 0.0)
    return total


def head_block(ref, rows, part, group, count, width):
    start = part * width + group * count * HEAD
    return ref[rows, start : start + count * HEAD]


def fore_kernel(cap, micro, *refs):
    tok_h, pick_h, rank_h, wqkv_h, wo_h, g1_h, g2_h, router_h, cot_h = refs[:9]
    count = 6 if micro == 0 else 7
    outs, refs = refs[9 : 9 + count], refs[9 + count :]
    send_h, qkv_h, mixed_h, x1_h, level_h, meta_h = outs[:6]
    tok_ref, pick_ref, rank_ref, wqkv_ref, wo_ref, g1_ref, g2_ref, router_ref, cot_ref = refs[:9]
    held, refs = refs[9 : 9 + count], refs[9 + count :]
    send_ref, qkv_ref, mixed_ref, x1_ref, level_ref, meta_ref = held[:6]
    all_s, in_sem, out_sem = refs
    rows, width = x1_ref.shape
    experts = router_ref.shape[0]
    images = rows // SEQ
    pairs = (
        (pick_h.at[micro], pick_ref),
        (rank_h.at[micro], rank_ref),
        (tok_h.at[micro], tok_ref),
        (g1_h, g1_ref),
        (wqkv_h, wqkv_ref),
        (wo_h, wo_ref),
        (g2_h, g2_ref),
        (router_h, router_ref),
        (cot_h.at[micro], cot_ref),
    )
    loads = [move(a, b, in_sem.at[n]) for n, (a, b) in enumerate(pairs)]

    loads[0].wait()
    loads[1].wait()
    rank_row = rank_ref[...].astype(F32)
    eye = iota((rows, rows), 0) == iota((rows, rows), 1)
    rank_col = jnp.sum(jnp.where(eye, rank_row, 0.0), axis=1, keepdims=True)
    less = jnp.where(rank_col < rank_row, 1.0, 0.0).astype(BF)
    picks = pick_ref[...]
    expert = iota((experts, rows), 0)
    on = [jnp.where(expert == picks[k : k + 1], 1.0, 0.0) for k in range(2)]
    before = [nn(on[k].astype(BF), less) for k in range(2)]
    before[1] = before[1] + jnp.sum(on[0], axis=1, keepdims=True)
    place = []
    for k in range(2):
        slot = jnp.sum(on[k] * before[k], axis=0, keepdims=True)
        base = picks[k : k + 1].astype(F32) * (2 * cap)
        place.append(jnp.where(slot < cap - 0.5, base + slot, -9999.0))

    loads[2].wait()
    loads[3].wait()
    x_in = tok_ref[...].astype(F32)
    normed, _ = normalize(x_in)
    h_first = (normed * g1_ref[...]).astype(BF)
    loads[4].wait()
    qkv_ref[...] = nn(h_first, wqkv_ref[...]).astype(BF)
    stores = [move(qkv_ref, qkv_h, out_sem.at[1])]
    if micro > 0:
        held[6][...] = h_first
        stores.append(move(held[6], outs[6], out_sem.at[6 + FILLS]))

    groups = HEADS // FORE_HEADS
    wide = FORE_HEADS * HEAD
    def image(i, carry):
        at = pl.ds(pl.multiple_of(i * SEQ, 16), SEQ)
        for g in range(groups):
            query = spread_heads(head_block(qkv_ref, at, 0, g, FORE_HEADS, width))
            key = head_block(qkv_ref, at, 1, g, FORE_HEADS, width)
            value = head_block(qkv_ref, at, 2, g, FORE_HEADS, width)
            scores = nt(key, query) * (HEAD**-0.5)
            peak = jnp.max(scores, axis=0, keepdims=True)
            expo = jnp.exp(scores - peak)
            denom = jnp.sum(expo, axis=0, keepdims=True)
            probs_low = (expo * (1.0 / denom)).astype(BF)
            if micro == 0:
                level_ref[pl.ds(i * groups + g, 1), :] = peak + jnp.log(denom)
            else:
                each = BACK_HEADS // FORE_HEADS
                line = (i * (HEADS // BACK_HEADS) + g // each) * SEQ
                column = g % each * FORE_HEADS * SEQ
                to = pl.ds(pl.multiple_of(line, 16), SEQ)
                level_ref[to, column : column + FORE_HEADS * SEQ] = probs_low
            mixed = gather_heads(tn(probs_low, value))
            mixed_ref[at, g * wide : (g + 1) * wide] = mixed.astype(BF)
        return carry

    lax.fori_loop(0, images, image, 0, unroll=micro == 0)

    stores.append(move(mixed_ref, mixed_h, out_sem.at[2]))
    stores.append(move(level_ref, level_h, out_sem.at[4]))

    for n in range(5, 9):
        loads[n].wait()
    x_mid = tok_ref[...].astype(F32) + nn(mixed_ref[...], wo_ref[...])
    x1_ref[...] = x_mid
    stores.append(move(x1_ref, x1_h, out_sem.at[3]))
    normed, _ = normalize(x_mid)
    h_second = (normed * g2_ref[...]).astype(BF)
    all_s[:rows, :] = h_second
    logits = nt(router_ref[...], h_second)
    picked = [jnp.sum(on[k] * logits, axis=0, keepdims=True) for k in range(2)]
    top = jnp.maximum(picked[0], picked[1])
    expo = [jnp.exp(v - top) for v in picked]
    total = expo[0] + expo[1]
    gates = [v / total for v in expo]
    stack = jnp.concatenate(
        gates + place + [picks.astype(F32)] + [jnp.zeros((2, rows), F32)], axis=0
    )
    meta = jnp.transpose(stack)
    meta_ref[...] = meta
    stores.append(move(meta_ref, meta_h, out_sem.at[5]))
    grad_out = cot_ref[...].astype(F32)
    all_s[rows : 2 * rows, :] = (meta[:, 0:1] * grad_out).astype(BF)
    all_s[2 * rows :, :] = (meta[:, 1:2] * grad_out).astype(BF)
    place = [v.astype(jnp.int32) for v in place]

    gone = jnp.full((1, 2 * rows), -1, jnp.int32)
    pos_a = jnp.concatenate([place[0], place[0] + cap, place[1] + cap], axis=1)
    pos_b = jnp.concatenate([place[1], gone], axis=1)
    step = send_ref.shape[0] // FILLS
    for c in range(FILLS):
        start = c * step
        row = iota((step, 3 * rows), 0) + start
        first = jnp.where((row == pos_a) | (row == pos_b), 1.0, 0.0).astype(BF)
        part = nn(first, all_s[...])
        send_ref[pl.ds(start, step), :] = part.astype(BF)
        at = pl.ds(start, step)
        stores.append(move(send_ref.at[at], send_h.at[at], out_sem.at[6 + c]))
    for copy in stores:
        copy.wait()


def move(source, target, sem):
    copy = pltpu.make_async_copy(source, target, sem)
    copy.start()
    return copy


def micro_spec(shape, micro):
    return pl.BlockSpec((1,) + tuple(shape[1:]), lambda i: (micro,) + (0,) * (len(shape) - 1))


def whole_spec(shape):
    return pl.BlockSpec(tuple(shape), lambda i: (0,) * len(shape))


def params(limit, **more):
    return pltpu.CompilerParams(vmem_limit_bytes=limit * MB, **more)


def fore(micro, cap, tokens, picks_t, ranks, wqkv, wo, g1, g2, router_t, cot):
    _, rows, width = tokens.shape
    experts = router_t.shape[0]
    out_shape = (
        jax.ShapeDtypeStruct((experts * 2 * cap, width), BF),
        jax.ShapeDtypeStruct((rows, 3 * width), BF),
        jax.ShapeDtypeStruct((rows, width), BF),
        jax.ShapeDtypeStruct((rows, width), F32),
        jax.ShapeDtypeStruct((rows // SEQ * HEADS // FORE_HEADS, FORE_HEADS * SEQ), F32),
        jax.ShapeDtypeStruct((rows, 8), F32),
    )
    if micro > 0:
        probs = jax.ShapeDtypeStruct((rows * HEADS // BACK_HEADS, BACK_HEADS * SEQ), BF)
        first = jax.ShapeDtypeStruct((rows, width), BF)
        out_shape = out_shape[:4] + (probs, out_shape[5], first)
    flops = 2 * rows * width * (4 * width + 3 * experts * 2 * cap + 4 * SEQ)
    return pl.pallas_call(
        functools.partial(fore_kernel, cap, micro),
        in_specs=[IN_HBM] * 9,
        out_specs=[IN_HBM] * len(out_shape),
        out_shape=out_shape,
        scratch_shapes=[
            pltpu.VMEM((rows, width), BF),
            pltpu.VMEM(picks_t.shape[1:], jnp.int32),
            pltpu.VMEM(ranks.shape[1:], jnp.int32),
            pltpu.VMEM(wqkv.shape, BF),
            pltpu.VMEM(wo.shape, BF),
            pltpu.VMEM(g1.shape, F32),
            pltpu.VMEM(g2.shape, F32),
            pltpu.VMEM(router_t.shape, BF),
            pltpu.VMEM((rows, width), BF),
        ]
        + [pltpu.VMEM(v.shape, v.dtype) for v in out_shape]
        + [pltpu.VMEM((3 * rows, width), BF)]
        + [pltpu.SemaphoreType.DMA((9,)), pltpu.SemaphoreType.DMA((7 + FILLS,))],
        compiler_params=params(FORE_MB),
        cost_estimate=pl.CostEstimate(flops=4 * flops, bytes_accessed=8 * MB, transcendentals=0),
        name="fore",
    )(tokens, picks_t, ranks, wqkv, wo, g1, g2, router_t, cot)


def expert_kernel(cap, first, *refs):
    if first:
        recv_ref, up_ref, down_ref, ret_ref, dup_ref, ddown_ref = refs[:6]
    else:
        recv_ref, up_ref, down_ref, aup_ref, adown_ref, ret_ref, dup_ref, ddown_ref = refs[:8]
    h_s, g_s, out_s, row_s = refs[-4:]
    step = pl.program_id(0)
    steps = pl.num_programs(0)
    slots = h_s.shape[0]

    def position(shape, dim, start):
        slot = iota(shape, dim) + start
        block = ((slot.astype(F32) + 0.5) * (1.0 / cap)).astype(jnp.int32)
        return slot + block * cap

    part = slots // 4

    @pl.when(step == 0)
    def _():
        def take(c, carry):
            at = pl.ds(pl.multiple_of(c * part, 16), part)
            here = iota((part, 2 * slots), 1)
            there = position((part, 2 * slots), 0, c * part)
            pick = jnp.where(here == there, 1.0, 0.0).astype(BF)
            h_s[at, :] = nn(pick, recv_ref[...]).astype(BF)
            pick = jnp.where(here == there + cap, 1.0, 0.0).astype(BF)
            g_s[at, :] = nn(pick, recv_ref[...]).astype(BF)
            return carry

        lax.fori_loop(0, 4, take, 0)

    up = up_ref[0]
    down = down_ref[0]
    h = h_s[...]
    g = g_s[...]
    pre = nn(h, up)
    grad_act = nt(g, down)
    square = pre * pre
    tanh = jnp.tanh(GELU_C * pre * (1.0 + GELU_A * square))
    half = 0.5 + 0.5 * tanh
    act = (pre * half).astype(BF)
    slope = half + (0.5 * GELU_C) * pre * (1.0 - tanh * tanh) * (1.0 + 3.0 * GELU_A * square)
    grad_pre = (grad_act * slope).astype(BF)
    grad_up = tn(h, grad_pre)
    grad_down = tn(act, g)
    if not first:
        grad_up = grad_up + aup_ref[...]
        grad_down = grad_down + adown_ref[...]
    dup_ref[...] = grad_up.astype(dup_ref.dtype)
    ddown_ref[...] = grad_down.astype(ddown_ref.dtype)
    out = nn(act, down)
    row = nt(grad_pre, up)

    @pl.when(step == 0)
    def _():
        out_s[...] = out
        row_s[...] = row

    @pl.when(step > 0)
    def _():
        out_s[...] += out
        row_s[...] += row

    @pl.when(step == steps - 1)
    def _():
        def give(c, carry):
            at = pl.ds(pl.multiple_of(c * 2 * part, 16), 2 * part)
            here = iota((2 * part, slots), 0) + c * 2 * part
            there = position((2 * part, slots), 1, 0)
            pick = jnp.where(here == there, 1.0, 0.0).astype(BF)
            total = nn(pick, out_s[...].astype(BF))
            pick = jnp.where(here == there + cap, 1.0, 0.0).astype(BF)
            total = total + nn(pick, row_s[...].astype(BF))
            ret_ref[at, :] = total.astype(BF)
            return carry

        lax.fori_loop(0, 4, give, 0)


def expert(cap, recv, up, down, earlier):
    first = earlier is None
    total, width = recv.shape
    slots = total // 2
    hidden = up.shape[2]
    tile = 512
    dtype = F32 if first else BF
    up_block = pl.BlockSpec((width, tile), lambda i: (0, i))
    down_block = pl.BlockSpec((tile, width), lambda i: (i, 0))
    in_specs = [
        whole_spec(recv.shape),
        pl.BlockSpec((1, width, tile), lambda i: (0, 0, i)),
        pl.BlockSpec((1, tile, width), lambda i: (0, i, 0)),
    ]
    args = [recv, up, down]
    if not first:
        in_specs += [up_block, down_block]
        args += list(earlier)
    return pl.pallas_call(
        functools.partial(expert_kernel, cap, first),
        grid=(hidden // tile,),
        in_specs=in_specs,
        out_specs=[whole_spec(recv.shape), up_block, down_block],
        out_shape=(
            jax.ShapeDtypeStruct(recv.shape, BF),
            jax.ShapeDtypeStruct((width, hidden), dtype),
            jax.ShapeDtypeStruct((hidden, width), dtype),
        ),
        scratch_shapes=[
            pltpu.VMEM((slots, width), BF),
            pltpu.VMEM((slots, width), BF),
            pltpu.VMEM((slots, width), F32),
            pltpu.VMEM((slots, width), F32),
        ],
        compiler_params=params(EXPERT_MB),
        cost_estimate=pl.CostEstimate(
            flops=2 * 12 * slots * width * hidden, bytes_accessed=24 * MB, transcendentals=0
        ),
        name="expert",
    )(*args)


def back_kernel(last, micro, *refs):
    take = list(refs)

    def next_refs(count):
        taken, take[:] = take[:count], take[count:]
        return taken

    scal_ref, ret_ref = next_refs(2)
    sources = next_refs(BACK_INS)
    earlier_h = next_refs(4) if last else []
    block_h, dx1_h = next_refs(2)
    (dqkv_h,) = next_refs(1) if last else (None,)
    made_h = next_refs(4 if last else 3)
    held = next_refs(BACK_INS)
    (
        meta_ref,
        cot_ref,
        x1_ref,
        g2_ref,
        router_ref,
        mixed_ref,
        wo_ref,
        qkv_ref,
        level_ref,
        tok_ref,
        g1_ref,
        wqkv_ref,
    ) = held
    in_ref, out_ref, small_ref = next_refs(3)
    block_ref, dx1_ref, dqkv_ref, dmix_s, in_sem, out_sem = next_refs(6)
    if last:
        tail_s, pay_s = next_refs(2)
    sources = [h.at[micro] if h.shape[0] == MICRO else h for h in sources]
    pairs = list(zip(sources, held))
    if last:
        pairs += list(zip(earlier_h[:3], (in_ref, out_ref, small_ref)))
    loads = [move(a, b, in_sem.at[n]) for n, (a, b) in enumerate(pairs[:8])]
    stores = []
    total = ret_ref.shape[0]
    rows, width = x1_ref.shape
    experts = router_ref.shape[0]

    def store(source, target):
        stores.append(move(source, target, out_sem.at[len(stores)]))

    loads[0].wait()
    meta = meta_ref[...]
    gates = [meta[:, k : k + 1] for k in range(2)]
    place = [meta[:, 2 + k : 3 + k].astype(jnp.int32) for k in range(2)]
    picks = [meta[:, 4 + k : 5 + k].astype(jnp.int32) for k in range(2)]
    cap = total // (2 * experts)
    here = iota((rows, total), 1)
    ret = ret_ref[...]
    both = (here == place[0] + cap) | (here == place[1] + cap)
    hot = [jnp.where(m, 1.0, 0.0).astype(BF) for m in (both, here == place[0], here == place[1])]
    stacked = nn(jnp.concatenate(hot, axis=0), ret)
    grad_second = stacked[:rows]
    pair_out = [stacked[rows : 2 * rows], stacked[2 * rows :]]
    for n in range(1, 5):
        loads[n].wait()
    loads += [move(a, b, in_sem.at[8 + n]) for n, (a, b) in enumerate(pairs[8:])]
    grad_out = cot_ref[...].astype(F32)
    x_mid = x1_ref[...]
    result = x_mid
    grad_gate = []
    for k in range(2):
        result = result + gates[k] * pair_out[k]
        grad_gate.append(jnp.sum(grad_out * pair_out[k], axis=1, keepdims=True))
    block_ref[...] = result.astype(BF)
    store(block_ref, block_h.at[micro])
    mean_gate = gates[0] * grad_gate[0] + gates[1] * grad_gate[1]
    lane = iota((rows, experts), 1)
    grad_logits = jnp.zeros((rows, experts), F32)
    for k in range(2):
        grad_pick = gates[k] * (grad_gate[k] - mean_gate)
        grad_logits = grad_logits + jnp.where(lane == picks[k], grad_pick, 0.0)
    grad_logits = grad_logits.astype(BF)
    grad_second = grad_second + nn(grad_logits, router_ref[...])
    normed, factor = normalize(x_mid)
    h_second = (normed * g2_ref[...]).astype(BF)
    small = [
        tn(grad_logits, h_second),
        jnp.sum(grad_second * normed, axis=0, keepdims=True),
    ]
    grad_mid = grad_out + norm_back(grad_second * g2_ref[...], normed, factor)
    dx1_ref[...] = grad_mid
    if last:
        store(dx1_ref, dx1_h)
    for n in range(5, 9):
        loads[n].wait()
    grad_attn = grad_mid.astype(BF)
    out_grad = tn(mixed_ref[...], grad_attn)
    if last:
        slots = 2 * lax.axis_size("exp")
        half = slots // 2
        piece = width // half
        span = half * piece
        tail = SMALL * (experts // 16)

        def lay(s, b, block):
            mine = scal_ref[2] == b
            start = jnp.where(mine, 0, half)
            order = jnp.where(mine, scal_ref[0], scal_ref[1])
            for j in range(half):
                to = pl.multiple_of((start + (j ^ order)) * piece, piece)
                pay_s[s, pl.ds(to, piece), :] = block[j * piece : (j + 1) * piece].astype(BF)

        for copy in loads[13:15]:
            copy.wait()
        lay(1, 1, out_grad + out_ref[...].astype(F32))
        small[0] = small[0] + small_ref[0:experts, :]
        small[1] = small[1] + small_ref[experts : experts + 1, :]
        tail_s[:experts, :] = small[0].astype(BF)
    else:
        out_ref[...] = out_grad.astype(BF)
        small_ref[0:experts, :] = small[0]
        small_ref[experts : experts + 1, :] = small[1]
        small_ref[experts + 1 :, :] = jnp.zeros((small_ref.shape[0] - experts - 1, width), F32)
        store(out_ref, made_h[1])
        store(small_ref, made_h[2])
    dmix_s[...] = nt(grad_attn, wo_ref[...]).astype(BF)

    groups = HEADS // BACK_HEADS
    wide = BACK_HEADS * HEAD
    lines = BACK_HEADS // FORE_HEADS
    def image(i, carry):
        at = pl.ds(pl.multiple_of(i * SEQ, 16), SEQ)
        for g in range(groups):
            query = spread_heads(head_block(qkv_ref, at, 0, g, BACK_HEADS, width))
            key = head_block(qkv_ref, at, 1, g, BACK_HEADS, width)
            value = head_block(qkv_ref, at, 2, g, BACK_HEADS, width)
            grad_mixed = spread_heads(dmix_s[at, g * wide : (g + 1) * wide])
            if last:
                line = pl.multiple_of((i * groups + g) * SEQ, 16)
                probs_low = level_ref[pl.ds(line, SEQ), :]
                probs = probs_low.astype(F32)
            else:
                scores = nt(key, query) * (HEAD**-0.5)
                line = (i * groups + g) * lines
                level = [level_ref[pl.ds(line + n, 1), :] for n in range(lines)]
                probs = jnp.exp(scores - jnp.concatenate(level, axis=1))
                probs_low = probs.astype(BF)
            grad_probs = nt(value, grad_mixed)
            inner = jnp.sum(probs * grad_probs, axis=0, keepdims=True)
            grad_scores = (probs * (grad_probs - inner)).astype(BF)
            grad_value = nn(probs_low, grad_mixed)
            grad_key = nn(grad_scores, query) * (HEAD**-0.5)
            grad_query = gather_heads(tn(grad_scores, key)) * (HEAD**-0.5)
            for part, grad in enumerate((grad_query, grad_key, grad_value)):
                start = part * width + g * wide
                dqkv_ref[at, start : start + wide] = grad.astype(BF)
        return carry

    lax.fori_loop(0, rows // SEQ, image, 0, unroll=last)

    if last:
        store(dqkv_ref, dqkv_h)
    for n in range(9, 13 if last else 12):
        loads[n].wait()
    if last:
        h_first = tok_ref[...]
    else:
        normed, factor = normalize(tok_ref[...].astype(F32))
        h_first = (normed * g1_ref[...]).astype(BF)
    gain = jnp.zeros((width, 1), F32)
    for part in (2, 0, 1):
        columns = slice(part * width, (part + 1) * width)
        in_grad = tn(h_first, dqkv_ref[:, columns])
        if not last:
            in_ref[:, columns] = in_grad.astype(BF)
            continue
        in_grad = in_grad + in_ref[:, columns].astype(F32)
        gain = gain + jnp.sum(wqkv_ref[:, columns].astype(F32) * in_grad, axis=1, keepdims=True)
        lay(part // 2, part % 2, in_grad)
        if part != 0:
            s = part // 2
            store(pay_s.at[s, pl.ds(span, span)], made_h[s].at[pl.ds(0, span)])
            store(pay_s.at[s, pl.ds(0, span)], made_h[2 + s].at[pl.ds(0, span)])
    if last:
        eye = iota((width, width), 0) == iota((width, width), 1)
        gain = jnp.sum(jnp.where(eye, gain, 0.0), axis=0, keepdims=True) / g1_ref[...]
        fill = jnp.zeros((tail - experts - 2, width), F32)
        tail_s[experts:, :] = jnp.concatenate([small[1], gain, fill], axis=0).astype(BF)
        for target in (made_h[0], made_h[2]):
            store(tail_s, target.at[pl.ds(span, tail)])
    else:
        store(in_ref, made_h[0])
        grad_first = nt(dqkv_ref[...], wqkv_ref[...]) * g1_ref[...]
        dx1_ref[...] = dx1_ref[...] + norm_back(grad_first, normed, factor)
        store(dx1_ref, dx1_h.at[micro])
    for copy in stores:
        copy.wait()


BACK_INS = 12


def back(micro, scal, plan, ret, saved, tokens, cot, wqkv, wo, g1, g2, router_t, earlier):
    last = earlier is not None
    qkv, mixed, x1, level, meta, *more = saved
    _, rows, width = tokens.shape
    experts = router_t.shape[0]
    slots, piece, tail = plan
    ins = [meta, cot, x1, g2, router_t, mixed, wo, qkv, level, *(more or [tokens]), g1, wqkv]
    shapes = [
        jax.ShapeDtypeStruct(tokens.shape, BF),
        jax.ShapeDtypeStruct((rows, width), F32),
        jax.ShapeDtypeStruct((rows, 3 * width), BF),
    ]
    kept = list(shapes)
    if not last:
        shapes = [shapes[0], jax.ShapeDtypeStruct(tokens.shape, F32)]
    sums = [
        jax.ShapeDtypeStruct(wqkv.shape, BF),
        jax.ShapeDtypeStruct(wo.shape, BF),
        jax.ShapeDtypeStruct((experts + 8, width), F32),
    ]

    def hold(value):
        shape = value.shape[1:] if value.shape[0] == MICRO else value.shape
        return pltpu.VMEM(shape, value.dtype)

    scratch = [hold(a) for a in ins + sums + kept]
    scratch += [
        pltpu.VMEM((rows, width), BF),
        pltpu.SemaphoreType.DMA((16,)),
        pltpu.SemaphoreType.DMA((12,)),
    ]
    aliases = {}
    if last:
        block, *sums = earlier
        args = [scal, ret] + ins + sums + [block]
        aliases = {17: 0}
        span = slots // 2 * piece
        shapes += [jax.ShapeDtypeStruct((span + more, width), BF) for more in (tail, 0)] * 2
        scratch += [pltpu.VMEM((tail, width), BF), pltpu.VMEM((2, slots * piece, width), BF)]
    else:
        args = [scal, ret] + ins
        shapes += sums
    in_specs = [pl.BlockSpec(memory_space=pltpu.SMEM), IN_VMEM] + [IN_HBM] * (len(args) - 2)
    out_specs = [IN_HBM] * len(shapes)
    flops = 2 * rows * width * (3 * ret.shape[0] + 12 * width)
    return pl.pallas_call(
        functools.partial(back_kernel, last, micro),
        in_specs=in_specs,
        out_specs=out_specs,
        out_shape=shapes,
        scratch_shapes=scratch,
        input_output_aliases=aliases,
        compiler_params=params(LAST_MB if last else BACK_MB),
        cost_estimate=pl.CostEstimate(flops=5 * flops, bytes_accessed=20 * MB, transcendentals=0),
        name="back",
    )(*args)


def finish_kernel(dqkv_ref, dx1_ref, tok_ref, wqkv_ref, g1_ref, *refs):
    grad_first = nt(dqkv_ref[...], wqkv_ref[...])
    normed, factor = normalize(tok_ref[0].astype(F32))
    refs[-1][0] = dx1_ref[...] + norm_back(grad_first * g1_ref[...], normed, factor)


def finish(micro, dqkv, dx1, tokens, wqkv, g1, earlier):
    _, rows, width = tokens.shape
    each = rows // 2
    both = pl.BlockSpec((1, each, width), lambda i: (micro, i, 0))
    in_specs = [
        pl.BlockSpec((each, 3 * width), lambda i: (i, 0)),
        pl.BlockSpec((each, width), lambda i: (i, 0)),
        both,
        whole_spec(wqkv.shape),
        whole_spec(g1.shape),
    ]
    args = [dqkv, dx1, tokens, wqkv, g1, earlier]
    in_specs.append(IN_HBM)
    return pl.pallas_call(
        finish_kernel,
        grid=(2,),
        in_specs=in_specs,
        out_specs=both,
        out_shape=jax.ShapeDtypeStruct(tokens.shape, F32),
        input_output_aliases={5: 0},
        compiler_params=params(FINISH_MB),
        cost_estimate=pl.CostEstimate(
            flops=2 * rows * width * 3 * width, bytes_accessed=6 * MB, transcendentals=0
        ),
        name="finish",
    )(*args)


def local(kernel, shapes, args, scalars=0, scratch=()):
    specs = [pl.BlockSpec(memory_space=pltpu.SMEM)] * scalars
    specs += [pl.BlockSpec(memory_space=pltpu.VMEM)] * (len(args) - scalars)
    size = sum(a.size * 4 for a in args)
    return pl.pallas_call(
        kernel,
        in_specs=specs,
        out_specs=[pl.BlockSpec(memory_space=pltpu.VMEM)] * len(shapes),
        out_shape=shapes,
        scratch_shapes=list(scratch),
        compiler_params=params(32),
        cost_estimate=pl.CostEstimate(flops=1000, bytes_accessed=size, transcendentals=0),
    )(*args)


def halve(keep, arrived, count, piece):
    rows, width = keep.shape
    half = count // 2 * piece
    tail = rows - 2 * half

    def kernel(keep_ref, arrived_ref, send_out, keep_out):
        total = (keep_ref[...].astype(F32) + arrived_ref[...].astype(F32)).astype(BF)
        keep_out[:half, :] = total[:half]
        if tail:
            keep_out[half:, :] = total[2 * half :]
        send_out[...] = total[half:]

    shape = jax.ShapeDtypeStruct((half + tail, width), BF)
    return local(kernel, [shape] * 2, [keep, arrived])


def join(first, second):
    rows, width = first.shape

    def kernel(a, b, out):
        out[:rows, :] = a[...]
        out[rows:, :] = b[...]

    (made,) = local(kernel, [jax.ShapeDtypeStruct((2 * rows, width), BF)], [first, second])
    return made


def reduce_all(sends, keeps, scal, plan, width, experts, beside):
    slots, piece, tail = plan
    size = lax.axis_size("exp")
    bits = size.bit_length() - 1
    orders = halving_orders(size)
    low, high = 1 << (bits - 2), 1 << (bits - 1)
    groups = [low, high, low | high]

    def swap(value, step):
        pairs = []
        for core in range(2):
            mask = 1 << orders[core][step]
            pairs += [(core * size + i, core * size + (i ^ mask)) for i in range(size)]
        return lax.ppermute(value, ("grp", "exp"), pairs)

    def swap_far(value, mask):
        return lax.ppermute(value, "exp", [(i, i ^ mask) for i in range(size)])

    def swap_core(value):
        return lax.ppermute(value, "grp", [(0, 1), (1, 0)])

    arrived = [swap_core(v) for v in sends]
    count = slots // 2
    steps = bits - 2
    for step in range(steps):
        made = [halve(keeps[s], arrived[s], count, piece) for s in range(2)]
        count //= 2
        arrived = [swap(made[s][0], step) for s in range(2)]
        keeps = [v[1] for v in made]

    share = tail // 4
    span = 2 * piece + share

    def quarter(scal_ref, *refs):
        small_s = refs[8]
        for s in range(2):
            total = refs[s][...].astype(F32) + refs[2 + s][...].astype(F32)
            for j in range(4):
                block = total[j * piece : (j + 1) * piece]
                refs[4 + j][s * piece : (s + 1) * piece, :] = block.astype(BF)
            if s == 0:
                small_s[...] = total[4 * piece :]
        for j in range(4):
            part = pl.multiple_of((scal_ref[3] ^ j) * share, share)
            refs[4 + j][2 * piece :, :] = small_s[pl.ds(part, share), :].astype(BF)

    shape = jax.ShapeDtypeStruct((span, width), BF)
    made = local(
        quarter,
        [shape] * 4,
        [scal] + list(keeps) + list(arrived),
        scalars=1,
        scratch=[pltpu.VMEM((tail, width), F32)],
    )
    arrived = [swap_far(made[1 + j], groups[j]) for j in range(3)]
    extra = beside()
    *arrived, extra = lax.optimization_barrier((*arrived, extra))

    def add_up(a, b, c, d, mine_ref):
        total = (a[...].astype(F32) + b[...].astype(F32)) + (c[...].astype(F32) + d[...].astype(F32))
        mine_ref[...] = total.astype(BF)

    (mine,) = local(add_up, [shape], [made[0]] + arrived)

    others = [swap_far(mine, groups[j]) for j in range(3)]

    def lay(scal_ref, a, b, c, d, one_ref, two_ref, small_ref):
        for j, ref in enumerate((a, b, c, d)):
            one_ref[j * piece : (j + 1) * piece, :] = ref[:piece, :]
            two_ref[j * piece : (j + 1) * piece, :] = ref[piece : 2 * piece, :]
            part = pl.multiple_of((scal_ref[3] ^ j) * share, share)
            small_ref[pl.ds(part, share), :] = ref[2 * piece :, :].astype(F32)

    shape = jax.ShapeDtypeStruct((4 * piece, width), BF)
    *have, small = local(
        lay,
        [shape] * 2 + [jax.ShapeDtypeStruct((tail, width), F32)],
        [scal, mine] + others,
        scalars=1,
    )
    vectors = (small[experts + 1], small[experts], small[:experts].T)
    for step in reversed(range(steps)):
        arrived = [swap(have[s], step) for s in range(2)]
        if step == 0:
            arrived[1], vectors = lax.optimization_barrier((arrived[1], vectors))
        have = [join(have[s], arrived[s]) for s in range(2)]
    other = [swap_core(v) for v in have]
    each = slots // 2

    def deal(halves, mine, *refs):
        scal_ref, refs = refs[0], refs[1:]
        in_h, out_h, block_s, sems = refs[-4:]
        core = scal_ref[2]
        part = core if mine else 1 - core
        order = scal_ref[0] if mine else scal_ref[1]
        copies = []
        for n, s in enumerate(halves):
            for pos in range(each):
                to = pl.multiple_of((pos ^ order) * piece, piece)
                block = refs[n][pos * piece : (pos + 1) * piece, :].astype(F32)
                block_s[n, pl.ds(to, piece), :] = block
            if s == 0:
                columns = pl.ds(pl.multiple_of(part * width, width), width)
                copies.append(move(block_s.at[n], in_h.at[:, columns], sems.at[0]))
            else:

                @pl.when(part == 0)
                def _():
                    move(block_s.at[n], in_h.at[:, pl.ds(2 * width, width)], sems.at[1]).wait()

                @pl.when(part == 1)
                def _():
                    move(block_s.at[n], out_h, sems.at[1]).wait()

        for copy in copies:
            copy.wait()

    def dealt(halves, values, grads):
        mine = grads is None
        grads = [] if mine else list(grads)
        count = len(values)
        return pl.pallas_call(
            functools.partial(deal, halves, mine),
            in_specs=[pl.BlockSpec(memory_space=pltpu.SMEM)]
            + [IN_VMEM] * count
            + [IN_HBM] * len(grads),
            out_specs=[IN_HBM, IN_HBM],
            out_shape=(
                jax.ShapeDtypeStruct((width, 3 * width), F32),
                jax.ShapeDtypeStruct((width, width), F32),
            ),
            input_output_aliases={} if mine else {1 + count: 0, 2 + count: 1},
            scratch_shapes=[
                pltpu.VMEM((count, width, width), F32),
                pltpu.SemaphoreType.DMA((2,)),
            ],
            compiler_params=params(16),
            cost_estimate=pl.CostEstimate(flops=1000, bytes_accessed=4 * MB, transcendentals=0),
            name="deal",
        )(scal, *values, *grads)

    grads = dealt((0, 1), have, None)
    in_grad, out_grad = dealt((0, 1), other, grads)
    return in_grad, out_grad, *vectors, extra


def halving_orders(size):
    bits = size.bit_length() - 1
    first = list(range(bits - 2))
    second = [first[b ^ 1] if (b ^ 1) < len(first) else b for b in first]
    return first, second


def places(size):
    bits = size.bit_length() - 1
    core = lax.axis_index("grp")
    me = lax.axis_index("exp")
    last = me >> (bits - 2)
    made = []
    for order in halving_orders(size):
        value = jnp.zeros_like(me)
        for b in order:
            value = value * 2 + ((me >> b) & 1)
        made.append(value * 4 + last)
    own = jnp.where(core == 0, made[0], made[1])
    other = jnp.where(core == 0, made[1], made[0])
    return jnp.stack([own, other, core, last]).astype(jnp.int32)


def shards(
    tokens,
    expert_picks,
    priority_ranks,
    attn_input,
    attn_output,
    first_gain,
    second_gain,
    router_weight,
    expert_up,
    expert_down,
    cotangent,
):
    size = lax.axis_size("exp")
    experts = router_weight.shape[1]
    rows, width = tokens.shape[1:]
    cap = max(2, rows // size)
    total = experts * 2 * cap
    slots = 2 * size
    plan = (slots, 2 * width // slots, SMALL * (experts // 16))
    scal = places(size)
    picks_t = jnp.transpose(expert_picks, (0, 2, 1))
    router_t = router_weight.T
    g1 = first_gain.reshape(1, width)
    g2 = second_gain.reshape(1, width)

    def exchange(value):
        value = value.reshape(experts, 2 * cap, width)
        value = lax.all_to_all(value, "exp", split_axis=0, concat_axis=0, tiled=True)
        return value.reshape(total, width)

    saved, sent = [], []
    for micro in range(MICRO):
        made = fore(
            micro,
            cap,
            tokens,
            picks_t,
            priority_ranks,
            attn_input,
            attn_output,
            g1,
            g2,
            router_t,
            cotangent,
        )
        sent.append(made[0])
        saved.append(made[1:])
    arrived = [exchange(v) for v in sent]
    answer0, up0, down0 = expert(cap, arrived[0], expert_up, expert_down, None)
    answer1, up1, down1 = expert(cap, arrived[1], expert_up, expert_down, (up0, down0))
    ret = [exchange(v) for v in (answer0, answer1)]
    up_other = lax.ppermute(up1, "grp", [(0, 1), (1, 0)])
    down_other = lax.ppermute(down1, "grp", [(0, 1), (1, 0)])

    weights = (attn_input, attn_output, g1, g2, router_t)
    block, grad0, *sums = back(
        0, scal, plan, ret[0], saved[0], tokens, cotangent, *weights, None
    )
    halves = lax.optimization_barrier((up1, up_other, down1, down_other, sums[2]))
    up_sum = halves[0].astype(F32) + halves[1].astype(F32)
    down_sum = halves[2].astype(F32) + halves[3].astype(F32)
    up_sum, down_sum, sums[2] = lax.optimization_barrier((up_sum, down_sum, halves[4]))
    block, dx1, dqkv1, *pay = back(
        1, scal, plan, ret[1], saved[1], tokens, cotangent, *weights, (block, *sums)
    )

    def beside():
        return finish(1, dqkv1, dx1, tokens, attn_input, g1, grad0)

    *dense, tokens_grad = reduce_all(pay[:2], pay[2:], scal, plan, width, experts, beside)
    return (block, tokens_grad, *dense, up_sum[None], down_sum[None])


def solution(mesh):
    split = P(None, ("grp", "exp"), None)
    owned = P("exp", None, None)
    in_specs = (split,) * 3 + (P(),) * 5 + (owned, owned, split)
    out_specs = (split, split) + (P(),) * 5 + (owned, owned)
    return jax.shard_map(shards, mesh=mesh, in_specs=in_specs, out_specs=out_specs, check_vma=False)
```

```python
import functools

import jax
import jax.numpy as jnp
from jax import lax
from jax.experimental import pallas as pl
from jax.experimental.pallas import tpu as pltpu
from jax.sharding import PartitionSpec as P

HEADS = 8
HEAD = 64
SEQ = 144
MICRO = 2
EPS = 1e-06
FORE_HEADS = 2
BACK_HEADS = 4
GELU_C = 0.7978845608028654
GELU_A = 0.044715
SMALL = 32

BF = jnp.bfloat16
F32 = jnp.float32
MB = 1 << 20
FORE_MB = 60
EXPERT_MB = 48
BACK_MB = 60
FINISH_MB = 60
LAST_MB = 50
FILLS = 4
IN_VMEM = pl.BlockSpec(memory_space=pltpu.VMEM)
IN_HBM = pl.BlockSpec(memory_space=pltpu.HBM)


def nn(a, b):
    return lax.dot_general(a, b, (((1,), (0,)), ((), ())), preferred_element_type=F32)


def nt(a, b):
    return lax.dot_general(a, b, (((1,), (1,)), ((), ())), preferred_element_type=F32)


def tn(a, b):
    return lax.dot_general(a, b, (((0,), (0,)), ((), ())), preferred_element_type=F32)


def normalize(values):
    center = values - jnp.mean(values, axis=-1, keepdims=True)
    factor = lax.rsqrt(jnp.mean(center * center, axis=-1, keepdims=True) + EPS)
    return center * factor, factor


def norm_back(grad_normed, normed, factor):
    return factor * (
        grad_normed
        - jnp.mean(grad_normed, axis=-1, keepdims=True)
        - normed * jnp.mean(grad_normed * normed, axis=-1, keepdims=True)
    )


def iota(shape, dim):
    return lax.broadcasted_iota(jnp.int32, shape, dim)


def spread_heads(block):
    head = iota(block.shape, 1) // HEAD
    zero = jnp.zeros_like(block)
    count = block.shape[1] // HEAD
    return jnp.concatenate([jnp.where(head == h, block, zero) for h in range(count)], axis=0)


def gather_heads(full):
    count = full.shape[1] // HEAD
    rows = full.shape[0] // count
    head = iota((rows, full.shape[1]), 1) // HEAD
    total = jnp.where(head == 0, full[:rows], 0.0)
    for h in range(1, count):
        total = total + jnp.where(head == h, full[h * rows : (h + 1) * rows], 0.0)
    return total


def head_block(ref, rows, part, group, count, width):
    start = part * width + group * count * HEAD
    return ref[rows, start : start + count * HEAD]


def fore_kernel(cap, micro, *refs):
    tok_h, pick_h, rank_h, wqkv_h, wo_h, g1_h, g2_h, router_h, cot_h = refs[:9]
    count = 6 if micro == 0 else 7
    outs, refs = refs[9 : 9 + count], refs[9 + count :]
    send_h, qkv_h, mixed_h, x1_h, level_h, meta_h = outs[:6]
    tok_ref, pick_ref, rank_ref, wqkv_ref, wo_ref, g1_ref, g2_ref, router_ref, cot_ref = refs[:9]
    held, refs = refs[9 : 9 + count], refs[9 + count :]
    send_ref, qkv_ref, mixed_ref, x1_ref, level_ref, meta_ref = held[:6]
    all_s, in_sem, out_sem = refs
    rows, width = x1_ref.shape
    experts = router_ref.shape[0]
    images = rows // SEQ
    pairs = (
        (pick_h.at[micro], pick_ref),
        (rank_h.at[micro], rank_ref),
        (tok_h.at[micro], tok_ref),
        (g1_h, g1_ref),
        (wqkv_h, wqkv_ref),
        (wo_h, wo_ref),
        (g2_h, g2_ref),
        (router_h, router_ref),
        (cot_h.at[micro], cot_ref),
    )
    loads = [move(a, b, in_sem.at[n]) for n, (a, b) in enumerate(pairs)]

    loads[0].wait()
    loads[1].wait()
    rank_row = rank_ref[...].astype(F32)
    eye = iota((rows, rows), 0) == iota((rows, rows), 1)
    rank_col = jnp.sum(jnp.where(eye, rank_row, 0.0), axis=1, keepdims=True)
    less = jnp.where(rank_col < rank_row, 1.0, 0.0).astype(BF)
    picks = pick_ref[...]
    expert = iota((experts, rows), 0)
    on = [jnp.where(expert == picks[k : k + 1], 1.0, 0.0) for k in range(2)]
    before = [nn(on[k].astype(BF), less) for k in range(2)]
    before[1] = before[1] + jnp.sum(on[0], axis=1, keepdims=True)
    place = []
    for k in range(2):
        slot = jnp.sum(on[k] * before[k], axis=0, keepdims=True)
        base = picks[k : k + 1].astype(F32) * (2 * cap)
        place.append(jnp.where(slot < cap - 0.5, base + slot, -9999.0))

    loads[2].wait()
    loads[3].wait()
    x_in = tok_ref[...].astype(F32)
    normed, _ = normalize(x_in)
    h_first = (normed * g1_ref[...]).astype(BF)
    loads[4].wait()
    qkv_ref[...] = nn(h_first, wqkv_ref[...]).astype(BF)
    stores = [move(qkv_ref, qkv_h, out_sem.at[1])]
    if micro > 0:
        held[6][...] = h_first
        stores.append(move(held[6], outs[6], out_sem.at[6 + FILLS]))

    groups = HEADS // FORE_HEADS
    wide = FORE_HEADS * HEAD
    def image(i, carry):
        at = pl.ds(pl.multiple_of(i * SEQ, 16), SEQ)
        for g in range(groups):
            query = spread_heads(head_block(qkv_ref, at, 0, g, FORE_HEADS, width))
            key = head_block(qkv_ref, at, 1, g, FORE_HEADS, width)
            value = head_block(qkv_ref, at, 2, g, FORE_HEADS, width)
            scores = nt(key, query) * (HEAD**-0.5)
            peak = jnp.max(scores, axis=0, keepdims=True)
            expo = jnp.exp(scores - peak)
            denom = jnp.sum(expo, axis=0, keepdims=True)
            probs_low = (expo * (1.0 / denom)).astype(BF)
            if micro == 0:
                level_ref[pl.ds(i * groups + g, 1), :] = peak + jnp.log(denom)
            else:
                each = BACK_HEADS // FORE_HEADS
                line = (i * (HEADS // BACK_HEADS) + g // each) * SEQ
                column = g % each * FORE_HEADS * SEQ
                to = pl.ds(pl.multiple_of(line, 16), SEQ)
                level_ref[to, column : column + FORE_HEADS * SEQ] = probs_low
            mixed = gather_heads(tn(probs_low, value))
            mixed_ref[at, g * wide : (g + 1) * wide] = mixed.astype(BF)
        return carry

    lax.fori_loop(0, images, image, 0, unroll=micro == 0)

    stores.append(move(mixed_ref, mixed_h, out_sem.at[2]))
    stores.append(move(level_ref, level_h, out_sem.at[4]))

    for n in range(5, 9):
        loads[n].wait()
    x_mid = tok_ref[...].astype(F32) + nn(mixed_ref[...], wo_ref[...])
    x1_ref[...] = x_mid
    stores.append(move(x1_ref, x1_h, out_sem.at[3]))
    normed, _ = normalize(x_mid)
    h_second = (normed * g2_ref[...]).astype(BF)
    all_s[:rows, :] = h_second
    logits = nt(router_ref[...], h_second)
    picked = [jnp.sum(on[k] * logits, axis=0, keepdims=True) for k in range(2)]
    top = jnp.maximum(picked[0], picked[1])
    expo = [jnp.exp(v - top) for v in picked]
    total = expo[0] + expo[1]
    gates = [v / total for v in expo]
    stack = jnp.concatenate(
        gates + place + [picks.astype(F32)] + [jnp.zeros((2, rows), F32)], axis=0
    )
    meta = jnp.transpose(stack)
    meta_ref[...] = meta
    stores.append(move(meta_ref, meta_h, out_sem.at[5]))
    grad_out = cot_ref[...].astype(F32)
    all_s[rows : 2 * rows, :] = (meta[:, 0:1] * grad_out).astype(BF)
    all_s[2 * rows :, :] = (meta[:, 1:2] * grad_out).astype(BF)
    place = [v.astype(jnp.int32) for v in place]

    gone = jnp.full((1, 2 * rows), -1, jnp.int32)
    pos_a = jnp.concatenate([place[0], place[0] + cap, place[1] + cap], axis=1)
    pos_b = jnp.concatenate([place[1], gone], axis=1)
    step = send_ref.shape[0] // FILLS
    for c in range(FILLS):
        start = c * step
        row = iota((step, 3 * rows), 0) + start
        first = jnp.where((row == pos_a) | (row == pos_b), 1.0, 0.0).astype(BF)
        part = nn(first, all_s[...])
        send_ref[pl.ds(start, step), :] = part.astype(BF)
        at = pl.ds(start, step)
        stores.append(move(send_ref.at[at], send_h.at[at], out_sem.at[6 + c]))
    for copy in stores:
        copy.wait()


def move(source, target, sem):
    copy = pltpu.make_async_copy(source, target, sem)
    copy.start()
    return copy


def micro_spec(shape, micro):
    return pl.BlockSpec((1,) + tuple(shape[1:]), lambda i: (micro,) + (0,) * (len(shape) - 1))


def whole_spec(shape):
    return pl.BlockSpec(tuple(shape), lambda i: (0,) * len(shape))


def params(limit, **more):
    return pltpu.CompilerParams(vmem_limit_bytes=limit * MB, **more)


def fore(micro, cap, tokens, picks_t, ranks, wqkv, wo, g1, g2, router_t, cot):
    _, rows, width = tokens.shape
    experts = router_t.shape[0]
    out_shape = (
        jax.ShapeDtypeStruct((experts * 2 * cap, width), BF),
        jax.ShapeDtypeStruct((rows, 3 * width), BF),
        jax.ShapeDtypeStruct((rows, width), BF),
        jax.ShapeDtypeStruct((rows, width), F32),
        jax.ShapeDtypeStruct((rows // SEQ * HEADS // FORE_HEADS, FORE_HEADS * SEQ), F32),
        jax.ShapeDtypeStruct((rows, 8), F32),
    )
    if micro > 0:
        probs = jax.ShapeDtypeStruct((rows * HEADS // BACK_HEADS, BACK_HEADS * SEQ), BF)
        first = jax.ShapeDtypeStruct((rows, width), BF)
        out_shape = out_shape[:4] + (probs, out_shape[5], first)
    flops = 2 * rows * width * (4 * width + 3 * experts * 2 * cap + 4 * SEQ)
    return pl.pallas_call(
        functools.partial(fore_kernel, cap, micro),
        in_specs=[IN_HBM] * 9,
        out_specs=[IN_HBM] * len(out_shape),
        out_shape=out_shape,
        scratch_shapes=[
            pltpu.VMEM((rows, width), BF),
            pltpu.VMEM(picks_t.shape[1:], jnp.int32),
            pltpu.VMEM(ranks.shape[1:], jnp.int32),
            pltpu.VMEM(wqkv.shape, BF),
            pltpu.VMEM(wo.shape, BF),
            pltpu.VMEM(g1.shape, F32),
            pltpu.VMEM(g2.shape, F32),
            pltpu.VMEM(router_t.shape, BF),
            pltpu.VMEM((rows, width), BF),
        ]
        + [pltpu.VMEM(v.shape, v.dtype) for v in out_shape]
        + [pltpu.VMEM((3 * rows, width), BF)]
        + [pltpu.SemaphoreType.DMA((9,)), pltpu.SemaphoreType.DMA((7 + FILLS,))],
        compiler_params=params(FORE_MB),
        cost_estimate=pl.CostEstimate(flops=4 * flops, bytes_accessed=8 * MB, transcendentals=0),
        name="fore",
    )(tokens, picks_t, ranks, wqkv, wo, g1, g2, router_t, cot)


def expert_kernel(cap, first, *refs):
    if first:
        recv_ref, up_ref, down_ref, ret_ref, dup_ref, ddown_ref = refs[:6]
    else:
        recv_ref, up_ref, down_ref, aup_ref, adown_ref, ret_ref, dup_ref, ddown_ref = refs[:8]
    h_s, g_s, out_s, row_s = refs[-4:]
    step = pl.program_id(0)
    steps = pl.num_programs(0)
    slots = h_s.shape[0]

    def position(shape, dim, start):
        slot = iota(shape, dim) + start
        block = ((slot.astype(F32) + 0.5) * (1.0 / cap)).astype(jnp.int32)
        return slot + block * cap

    part = slots // 4

    @pl.when(step == 0)
    def _():
        def take(c, carry):
            at = pl.ds(pl.multiple_of(c * part, 16), part)
            here = iota((part, 2 * slots), 1)
            there = position((part, 2 * slots), 0, c * part)
            pick = jnp.where(here == there, 1.0, 0.0).astype(BF)
            h_s[at, :] = nn(pick, recv_ref[...]).astype(BF)
            pick = jnp.where(here == there + cap, 1.0, 0.0).astype(BF)
            g_s[at, :] = nn(pick, recv_ref[...]).astype(BF)
            return carry

        lax.fori_loop(0, 4, take, 0)

    up = up_ref[0]
    down = down_ref[0]
    h = h_s[...]
    g = g_s[...]
    pre = nn(h, up)
    grad_act = nt(g, down)
    square = pre * pre
    tanh = jnp.tanh(GELU_C * pre * (1.0 + GELU_A * square))
    half = 0.5 + 0.5 * tanh
    act = (pre * half).astype(BF)
    slope = half + (0.5 * GELU_C) * pre * (1.0 - tanh * tanh) * (1.0 + 3.0 * GELU_A * square)
    grad_pre = (grad_act * slope).astype(BF)
    grad_up = tn(h, grad_pre)
    grad_down = tn(act, g)
    if not first:
        grad_up = grad_up + aup_ref[...]
        grad_down = grad_down + adown_ref[...]
    dup_ref[...] = grad_up.astype(dup_ref.dtype)
    ddown_ref[...] = grad_down.astype(ddown_ref.dtype)
    out = nn(act, down)
    row = nt(grad_pre, up)

    @pl.when(step == 0)
    def _():
        out_s[...] = out
        row_s[...] = row

    @pl.when(step > 0)
    def _():
        out_s[...] += out
        row_s[...] += row

    @pl.when(step == steps - 1)
    def _():
        def give(c, carry):
            at = pl.ds(pl.multiple_of(c * 2 * part, 16), 2 * part)
            here = iota((2 * part, slots), 0) + c * 2 * part
            there = position((2 * part, slots), 1, 0)
            pick = jnp.where(here == there, 1.0, 0.0).astype(BF)
            total = nn(pick, out_s[...].astype(BF))
            pick = jnp.where(here == there + cap, 1.0, 0.0).astype(BF)
            total = total + nn(pick, row_s[...].astype(BF))
            ret_ref[at, :] = total.astype(BF)
            return carry

        lax.fori_loop(0, 4, give, 0)


def expert(cap, recv, up, down, earlier):
    first = earlier is None
    total, width = recv.shape
    slots = total // 2
    hidden = up.shape[2]
    tile = 512
    dtype = F32 if first else BF
    up_block = pl.BlockSpec((width, tile), lambda i: (0, i))
    down_block = pl.BlockSpec((tile, width), lambda i: (i, 0))
    in_specs = [
        whole_spec(recv.shape),
        pl.BlockSpec((1, width, tile), lambda i: (0, 0, i)),
        pl.BlockSpec((1, tile, width), lambda i: (0, i, 0)),
    ]
    args = [recv, up, down]
    if not first:
        in_specs += [up_block, down_block]
        args += list(earlier)
    return pl.pallas_call(
        functools.partial(expert_kernel, cap, first),
        grid=(hidden // tile,),
        in_specs=in_specs,
        out_specs=[whole_spec(recv.shape), up_block, down_block],
        out_shape=(
            jax.ShapeDtypeStruct(recv.shape, BF),
            jax.ShapeDtypeStruct((width, hidden), dtype),
            jax.ShapeDtypeStruct((hidden, width), dtype),
        ),
        scratch_shapes=[
            pltpu.VMEM((slots, width), BF),
            pltpu.VMEM((slots, width), BF),
            pltpu.VMEM((slots, width), F32),
            pltpu.VMEM((slots, width), F32),
        ],
        compiler_params=params(EXPERT_MB),
        cost_estimate=pl.CostEstimate(
            flops=2 * 12 * slots * width * hidden, bytes_accessed=24 * MB, transcendentals=0
        ),
        name="expert",
    )(*args)


def back_kernel(last, micro, *refs):
    take = list(refs)

    def next_refs(count):
        taken, take[:] = take[:count], take[count:]
        return taken

    scal_ref, ret_ref = next_refs(2)
    sources = next_refs(BACK_INS)
    earlier_h = next_refs(4) if last else []
    block_h, dx1_h = next_refs(2)
    (dqkv_h,) = next_refs(1) if last else (None,)
    made_h = next_refs(4 if last else 3)
    held = next_refs(BACK_INS)
    (
        meta_ref,
        cot_ref,
        x1_ref,
        g2_ref,
        router_ref,
        mixed_ref,
        wo_ref,
        qkv_ref,
        level_ref,
        tok_ref,
        g1_ref,
        wqkv_ref,
    ) = held
    in_ref, out_ref, small_ref = next_refs(3)
    block_ref, dx1_ref, dqkv_ref, dmix_s, in_sem, out_sem = next_refs(6)
    if last:
        tail_s, pay_s = next_refs(2)
    sources = [h.at[micro] if h.shape[0] == MICRO else h for h in sources]
    pairs = list(zip(sources, held))
    if last:
        pairs += list(zip(earlier_h[:3], (in_ref, out_ref, small_ref)))
    loads = [move(a, b, in_sem.at[n]) for n, (a, b) in enumerate(pairs[:8])]
    stores = []
    total = ret_ref.shape[0]
    rows, width = x1_ref.shape
    experts = router_ref.shape[0]

    def store(source, target):
        stores.append(move(source, target, out_sem.at[len(stores)]))

    loads[0].wait()
    meta = meta_ref[...]
    gates = [meta[:, k : k + 1] for k in range(2)]
    place = [meta[:, 2 + k : 3 + k].astype(jnp.int32) for k in range(2)]
    picks = [meta[:, 4 + k : 5 + k].astype(jnp.int32) for k in range(2)]
    cap = total // (2 * experts)
    here = iota((rows, total), 1)
    ret = ret_ref[...]
    both = (here == place[0] + cap) | (here == place[1] + cap)
    hot = [jnp.where(m, 1.0, 0.0).astype(BF) for m in (both, here == place[0], here == place[1])]
    stacked = nn(jnp.concatenate(hot, axis=0), ret)
    grad_second = stacked[:rows]
    pair_out = [stacked[rows : 2 * rows], stacked[2 * rows :]]
    for n in range(1, 5):
        loads[n].wait()
    loads += [move(a, b, in_sem.at[8 + n]) for n, (a, b) in enumerate(pairs[8:])]
    grad_out = cot_ref[...].astype(F32)
    x_mid = x1_ref[...]
    result = x_mid
    grad_gate = []
    for k in range(2):
        result = result + gates[k] * pair_out[k]
        grad_gate.append(jnp.sum(grad_out * pair_out[k], axis=1, keepdims=True))
    block_ref[...] = result.astype(BF)
    store(block_ref, block_h.at[micro])
    mean_gate = gates[0] * grad_gate[0] + gates[1] * grad_gate[1]
    lane = iota((rows, experts), 1)
    grad_logits = jnp.zeros((rows, experts), F32)
    for k in range(2):
        grad_pick = gates[k] * (grad_gate[k] - mean_gate)
        grad_logits = grad_logits + jnp.where(lane == picks[k], grad_pick, 0.0)
    grad_logits = grad_logits.astype(BF)
    grad_second = grad_second + nn(grad_logits, router_ref[...])
    normed, factor = normalize(x_mid)
    h_second = (normed * g2_ref[...]).astype(BF)
    small = [
        tn(grad_logits, h_second),
        jnp.sum(grad_second * normed, axis=0, keepdims=True),
    ]
    grad_mid = grad_out + norm_back(grad_second * g2_ref[...], normed, factor)
    dx1_ref[...] = grad_mid
    if last:
        store(dx1_ref, dx1_h)
    for n in range(5, 9):
        loads[n].wait()
    grad_attn = grad_mid.astype(BF)
    out_grad = tn(mixed_ref[...], grad_attn)
    if last:
        slots = 2 * lax.axis_size("exp")
        half = slots // 2
        piece = width // half
        span = half * piece
        tail = SMALL * (experts // 16)

        def lay(s, b, block):
            mine = scal_ref[2] == b
            start = jnp.where(mine, 0, half)
            order = jnp.where(mine, scal_ref[0], scal_ref[1])
            for j in range(half):
                to = pl.multiple_of((start + (j ^ order)) * piece, piece)
                pay_s[s, pl.ds(to, piece), :] = block[j * piece : (j + 1) * piece].astype(BF)

        for copy in loads[13:15]:
            copy.wait()
        lay(1, 1, out_grad + out_ref[...].astype(F32))
        small[0] = small[0] + small_ref[0:experts, :]
        small[1] = small[1] + small_ref[experts : experts + 1, :]
        tail_s[:experts, :] = small[0].astype(BF)
    else:
        out_ref[...] = out_grad.astype(BF)
        small_ref[0:experts, :] = small[0]
        small_ref[experts : experts + 1, :] = small[1]
        small_ref[experts + 1 :, :] = jnp.zeros((small_ref.shape[0] - experts - 1, width), F32)
        store(out_ref, made_h[1])
        store(small_ref, made_h[2])
    dmix_s[...] = nt(grad_attn, wo_ref[...]).astype(BF)

    groups = HEADS // BACK_HEADS
    wide = BACK_HEADS * HEAD
    lines = BACK_HEADS // FORE_HEADS
    def image(i, carry):
        at = pl.ds(pl.multiple_of(i * SEQ, 16), SEQ)
        for g in range(groups):
            query = spread_heads(head_block(qkv_ref, at, 0, g, BACK_HEADS, width))
            key = head_block(qkv_ref, at, 1, g, BACK_HEADS, width)
            value = head_block(qkv_ref, at, 2, g, BACK_HEADS, width)
            grad_mixed = spread_heads(dmix_s[at, g * wide : (g + 1) * wide])
            if last:
                line = pl.multiple_of((i * groups + g) * SEQ, 16)
                probs_low = level_ref[pl.ds(line, SEQ), :]
                probs = probs_low.astype(F32)
            else:
                scores = nt(key, query) * (HEAD**-0.5)
                line = (i * groups + g) * lines
                level = [level_ref[pl.ds(line + n, 1), :] for n in range(lines)]
                probs = jnp.exp(scores - jnp.concatenate(level, axis=1))
                probs_low = probs.astype(BF)
            grad_probs = nt(value, grad_mixed)
            inner = jnp.sum(probs * grad_probs, axis=0, keepdims=True)
            grad_scores = (probs * (grad_probs - inner)).astype(BF)
            grad_value = nn(probs_low, grad_mixed)
            grad_key = nn(grad_scores, query) * (HEAD**-0.5)
            grad_query = gather_heads(tn(grad_scores, key)) * (HEAD**-0.5)
            for part, grad in enumerate((grad_query, grad_key, grad_value)):
                start = part * width + g * wide
                dqkv_ref[at, start : start + wide] = grad.astype(BF)
        return carry

    lax.fori_loop(0, rows // SEQ, image, 0, unroll=last)

    if last:
        store(dqkv_ref, dqkv_h)
    for n in range(9, 13 if last else 12):
        loads[n].wait()
    if last:
        h_first = tok_ref[...]
    else:
        normed, factor = normalize(tok_ref[...].astype(F32))
        h_first = (normed * g1_ref[...]).astype(BF)
    gain = jnp.zeros((width, 1), F32)
    for part in (2, 0, 1):
        columns = slice(part * width, (part + 1) * width)
        in_grad = tn(h_first, dqkv_ref[:, columns])
        if not last:
            in_ref[:, columns] = in_grad.astype(BF)
            continue
        in_grad = in_grad + in_ref[:, columns].astype(F32)
        gain = gain + jnp.sum(wqkv_ref[:, columns].astype(F32) * in_grad, axis=1, keepdims=True)
        lay(part // 2, part % 2, in_grad)
        if part != 0:
            s = part // 2
            store(pay_s.at[s, pl.ds(span, span)], made_h[s].at[pl.ds(0, span)])
            store(pay_s.at[s, pl.ds(0, span)], made_h[2 + s].at[pl.ds(0, span)])
    if last:
        eye = iota((width, width), 0) == iota((width, width), 1)
        gain = jnp.sum(jnp.where(eye, gain, 0.0), axis=0, keepdims=True) / g1_ref[...]
        fill = jnp.zeros((tail - experts - 2, width), F32)
        tail_s[experts:, :] = jnp.concatenate([small[1], gain, fill], axis=0).astype(BF)
        for target in (made_h[0], made_h[2]):
            store(tail_s, target.at[pl.ds(span, tail)])
    else:
        store(in_ref, made_h[0])
        grad_first = nt(dqkv_ref[...], wqkv_ref[...]) * g1_ref[...]
        dx1_ref[...] = dx1_ref[...] + norm_back(grad_first, normed, factor)
        store(dx1_ref, dx1_h.at[micro])
    for copy in stores:
        copy.wait()


BACK_INS = 12


def back(micro, scal, plan, ret, saved, tokens, cot, wqkv, wo, g1, g2, router_t, earlier):
    last = earlier is not None
    qkv, mixed, x1, level, meta, *more = saved
    _, rows, width = tokens.shape
    experts = router_t.shape[0]
    slots, piece, tail = plan
    ins = [meta, cot, x1, g2, router_t, mixed, wo, qkv, level, *(more or [tokens]), g1, wqkv]
    shapes = [
        jax.ShapeDtypeStruct(tokens.shape, BF),
        jax.ShapeDtypeStruct((rows, width), F32),
        jax.ShapeDtypeStruct((rows, 3 * width), BF),
    ]
    kept = list(shapes)
    if not last:
        shapes = [shapes[0], jax.ShapeDtypeStruct(tokens.shape, F32)]
    sums = [
        jax.ShapeDtypeStruct(wqkv.shape, BF),
        jax.ShapeDtypeStruct(wo.shape, BF),
        jax.ShapeDtypeStruct((experts + 8, width), F32),
    ]

    def hold(value):
        shape = value.shape[1:] if value.shape[0] == MICRO else value.shape
        return pltpu.VMEM(shape, value.dtype)

    scratch = [hold(a) for a in ins + sums + kept]
    scratch += [
        pltpu.VMEM((rows, width), BF),
        pltpu.SemaphoreType.DMA((16,)),
        pltpu.SemaphoreType.DMA((12,)),
    ]
    aliases = {}
    if last:
        block, *sums = earlier
        args = [scal, ret] + ins + sums + [block]
        aliases = {17: 0}
        span = slots // 2 * piece
        shapes += [jax.ShapeDtypeStruct((span + more, width), BF) for more in (tail, 0)] * 2
        scratch += [pltpu.VMEM((tail, width), BF), pltpu.VMEM((2, slots * piece, width), BF)]
    else:
        args = [scal, ret] + ins
        shapes += sums
    in_specs = [pl.BlockSpec(memory_space=pltpu.SMEM), IN_VMEM] + [IN_HBM] * (len(args) - 2)
    out_specs = [IN_HBM] * len(shapes)
    flops = 2 * rows * width * (3 * ret.shape[0] + 12 * width)
    return pl.pallas_call(
        functools.partial(back_kernel, last, micro),
        in_specs=in_specs,
        out_specs=out_specs,
        out_shape=shapes,
        scratch_shapes=scratch,
        input_output_aliases=aliases,
        compiler_params=params(LAST_MB if last else BACK_MB),
        cost_estimate=pl.CostEstimate(flops=5 * flops, bytes_accessed=20 * MB, transcendentals=0),
        name="back",
    )(*args)


def finish_kernel(dqkv_ref, dx1_ref, tok_ref, wqkv_ref, g1_ref, *refs):
    grad_first = nt(dqkv_ref[...], wqkv_ref[...])
    normed, factor = normalize(tok_ref[0].astype(F32))
    refs[-1][0] = dx1_ref[...] + norm_back(grad_first * g1_ref[...], normed, factor)


def finish(micro, dqkv, dx1, tokens, wqkv, g1, earlier):
    _, rows, width = tokens.shape
    each = rows // 2
    both = pl.BlockSpec((1, each, width), lambda i: (micro, i, 0))
    in_specs = [
        pl.BlockSpec((each, 3 * width), lambda i: (i, 0)),
        pl.BlockSpec((each, width), lambda i: (i, 0)),
        both,
        whole_spec(wqkv.shape),
        whole_spec(g1.shape),
    ]
    args = [dqkv, dx1, tokens, wqkv, g1, earlier]
    in_specs.append(IN_HBM)
    return pl.pallas_call(
        finish_kernel,
        grid=(2,),
        in_specs=in_specs,
        out_specs=both,
        out_shape=jax.ShapeDtypeStruct(tokens.shape, F32),
        input_output_aliases={5: 0},
        compiler_params=params(FINISH_MB),
        cost_estimate=pl.CostEstimate(
            flops=2 * rows * width * 3 * width, bytes_accessed=6 * MB, transcendentals=0
        ),
        name="finish",
    )(*args)


def local(kernel, shapes, args, scalars=0, scratch=()):
    specs = [pl.BlockSpec(memory_space=pltpu.SMEM)] * scalars
    specs += [pl.BlockSpec(memory_space=pltpu.VMEM)] * (len(args) - scalars)
    size = sum(a.size * 4 for a in args)
    return pl.pallas_call(
        kernel,
        in_specs=specs,
        out_specs=[pl.BlockSpec(memory_space=pltpu.VMEM)] * len(shapes),
        out_shape=shapes,
        scratch_shapes=list(scratch),
        compiler_params=params(32),
        cost_estimate=pl.CostEstimate(flops=1000, bytes_accessed=size, transcendentals=0),
    )(*args)


def halve(keep, arrived, count, piece):
    rows, width = keep.shape
    half = count // 2 * piece
    tail = rows - 2 * half

    def kernel(keep_ref, arrived_ref, send_out, keep_out):
        total = (keep_ref[...].astype(F32) + arrived_ref[...].astype(F32)).astype(BF)
        keep_out[:half, :] = total[:half]
        if tail:
            keep_out[half:, :] = total[2 * half :]
        send_out[...] = total[half:]

    shape = jax.ShapeDtypeStruct((half + tail, width), BF)
    return local(kernel, [shape] * 2, [keep, arrived])


def join(first, second):
    rows, width = first.shape

    def kernel(a, b, out):
        out[:rows, :] = a[...]
        out[rows:, :] = b[...]

    (made,) = local(kernel, [jax.ShapeDtypeStruct((2 * rows, width), BF)], [first, second])
    return made


def reduce_all(sends, keeps, scal, plan, width, experts, beside):
    slots, piece, tail = plan
    size = lax.axis_size("exp")
    bits = size.bit_length() - 1
    orders = halving_orders(size)
    low, high = 1 << (bits - 2), 1 << (bits - 1)
    groups = [low, high, low | high]

    def swap(value, step):
        pairs = []
        for core in range(2):
            mask = 1 << orders[core][step]
            pairs += [(core * size + i, core * size + (i ^ mask)) for i in range(size)]
        return lax.ppermute(value, ("grp", "exp"), pairs)

    def swap_far(value, mask):
        return lax.ppermute(value, "exp", [(i, i ^ mask) for i in range(size)])

    def swap_core(value):
        return lax.ppermute(value, "grp", [(0, 1), (1, 0)])

    arrived = [swap_core(v) for v in sends]
    count = slots // 2
    steps = bits - 2
    for step in range(steps):
        made = [halve(keeps[s], arrived[s], count, piece) for s in range(2)]
        count //= 2
        arrived = [swap(made[s][0], step) for s in range(2)]
        keeps = [v[1] for v in made]

    share = tail // 4
    span = 2 * piece + share

    def quarter(scal_ref, *refs):
        small_s = refs[8]
        for s in range(2):
            total = refs[s][...].astype(F32) + refs[2 + s][...].astype(F32)
            for j in range(4):
                block = total[j * piece : (j + 1) * piece]
                refs[4 + j][s * piece : (s + 1) * piece, :] = block.astype(BF)
            if s == 0:
                small_s[...] = total[4 * piece :]
        for j in range(4):
            part = pl.multiple_of((scal_ref[3] ^ j) * share, share)
            refs[4 + j][2 * piece :, :] = small_s[pl.ds(part, share), :].astype(BF)

    shape = jax.ShapeDtypeStruct((span, width), BF)
    made = local(
        quarter,
        [shape] * 4,
        [scal] + list(keeps) + list(arrived),
        scalars=1,
        scratch=[pltpu.VMEM((tail, width), F32)],
    )
    arrived = [swap_far(made[1 + j], groups[j]) for j in range(3)]
    extra = beside()
    *arrived, extra = lax.optimization_barrier((*arrived, extra))

    def add_up(a, b, c, d, mine_ref):
        total = (a[...].astype(F32) + b[...].astype(F32)) + (c[...].astype(F32) + d[...].astype(F32))
        mine_ref[...] = total.astype(BF)

    (mine,) = local(add_up, [shape], [made[0]] + arrived)

    others = [swap_far(mine, groups[j]) for j in range(3)]

    def lay(scal_ref, a, b, c, d, one_ref, two_ref, small_ref):
        for j, ref in enumerate((a, b, c, d)):
            one_ref[j * piece : (j + 1) * piece, :] = ref[:piece, :]
            two_ref[j * piece : (j + 1) * piece, :] = ref[piece : 2 * piece, :]
            part = pl.multiple_of((scal_ref[3] ^ j) * share, share)
            small_ref[pl.ds(part, share), :] = ref[2 * piece :, :].astype(F32)

    shape = jax.ShapeDtypeStruct((4 * piece, width), BF)
    *have, small = local(
        lay,
        [shape] * 2 + [jax.ShapeDtypeStruct((tail, width), F32)],
        [scal, mine] + others,
        scalars=1,
    )
    vectors = (small[experts + 1], small[experts], small[:experts].T)
    for step in reversed(range(1, steps)):
        arrived = [swap(have[s], step) for s in range(2)]
        have = [join(have[s], arrived[s]) for s in range(2)]
    count = slots // 4
    rows = count * piece

    def deal(first, whose, *refs):
        scal_ref, refs = refs[0], refs[1:]
        in_h, out_h, block_s, sems = refs[-4:]
        core = scal_ref[2]
        copies, later = [], []
        for n, (s, other) in enumerate(whose):
            order = scal_ref[other]
            part = 1 - core if other else core
            for pos in range(count):
                to = pl.multiple_of(((pos ^ order) % count) * piece, piece)
                block = refs[n][pos * piece : (pos + 1) * piece, :].astype(F32)
                block_s[n, pl.ds(to, piece), :] = block
            half = (order // count + (0 if first else 1)) % 2
            at = pl.ds(pl.multiple_of(half * rows, rows), rows)
            if s == 0:
                columns = pl.ds(pl.multiple_of(part * width, width), width)
                copies.append(move(block_s.at[n], in_h.at[at, columns], sems.at[n]))
            else:
                later.append((n, part, at))
        for n, part, at in later:

            @pl.when(part == 0)
            def _():
                target = in_h.at[at, pl.ds(2 * width, width)]
                move(block_s.at[n], target, sems.at[n]).wait()

            @pl.when(part == 1)
            def _():
                move(block_s.at[n], out_h.at[at], sems.at[n]).wait()

        for copy in copies:
            copy.wait()

    def dealt(first, whose, values, grads):
        number = len(values)
        grads = [] if grads is None else list(grads)
        return pl.pallas_call(
            functools.partial(deal, first, whose),
            in_specs=[pl.BlockSpec(memory_space=pltpu.SMEM)]
            + [IN_VMEM] * number
            + [IN_HBM] * len(grads),
            out_specs=[IN_HBM, IN_HBM],
            out_shape=(
                jax.ShapeDtypeStruct((width, 3 * width), F32),
                jax.ShapeDtypeStruct((width, width), F32),
            ),
            input_output_aliases={1 + number: 0, 2 + number: 1} if grads else {},
            scratch_shapes=[
                pltpu.VMEM((number, rows, width), F32),
                pltpu.SemaphoreType.DMA((number,)),
            ],
            compiler_params=params(16),
            cost_estimate=pl.CostEstimate(flops=1000, bytes_accessed=4 * MB, transcendentals=0),
            name="deal",
        )(scal, *values, *grads)

    arrived = [swap(have[s], 0) for s in range(2)]
    near = [swap_core(v) for v in have]
    grads = dealt(True, ((0, 0), (1, 0), (0, 1), (1, 1)), [*have, *near], None)
    arrived[1], vectors, grads = lax.optimization_barrier((arrived[1], vectors, grads))
    far = [swap_core(v) for v in arrived]
    grads = dealt(False, ((0, 0), (1, 0)), arrived, grads)
    in_grad, out_grad = dealt(False, ((0, 1), (1, 1)), far, grads)
    return in_grad, out_grad, *vectors, extra


def halving_orders(size):
    bits = size.bit_length() - 1
    first = list(range(bits - 2))
    second = [first[b ^ 1] if (b ^ 1) < len(first) else b for b in first]
    return first, second


def places(size):
    bits = size.bit_length() - 1
    core = lax.axis_index("grp")
    me = lax.axis_index("exp")
    last = me >> (bits - 2)
    made = []
    for order in halving_orders(size):
        value = jnp.zeros_like(me)
        for b in order:
            value = value * 2 + ((me >> b) & 1)
        made.append(value * 4 + last)
    own = jnp.where(core == 0, made[0], made[1])
    other = jnp.where(core == 0, made[1], made[0])
    return jnp.stack([own, other, core, last]).astype(jnp.int32)


def shards(
    tokens,
    expert_picks,
    priority_ranks,
    attn_input,
    attn_output,
    first_gain,
    second_gain,
    router_weight,
    expert_up,
    expert_down,
    cotangent,
):
    size = lax.axis_size("exp")
    experts = router_weight.shape[1]
    rows, width = tokens.shape[1:]
    cap = max(2, rows // size)
    total = experts * 2 * cap
    slots = 2 * size
    plan = (slots, 2 * width // slots, SMALL * (experts // 16))
    scal = places(size)
    picks_t = jnp.transpose(expert_picks, (0, 2, 1))
    router_t = router_weight.T
    g1 = first_gain.reshape(1, width)
    g2 = second_gain.reshape(1, width)

    def exchange(value):
        value = value.reshape(experts, 2 * cap, width)
        value = lax.all_to_all(value, "exp", split_axis=0, concat_axis=0, tiled=True)
        return value.reshape(total, width)

    saved, sent = [], []
    for micro in range(MICRO):
        made = fore(
            micro,
            cap,
            tokens,
            picks_t,
            priority_ranks,
            attn_input,
            attn_output,
            g1,
            g2,
            router_t,
            cotangent,
        )
        sent.append(made[0])
        saved.append(made[1:])
    arrived = [exchange(v) for v in sent]
    answer0, up0, down0 = expert(cap, arrived[0], expert_up, expert_down, None)
    answer1, up1, down1 = expert(cap, arrived[1], expert_up, expert_down, (up0, down0))
    ret = [exchange(v) for v in (answer0, answer1)]
    up_other = lax.ppermute(up1, "grp", [(0, 1), (1, 0)])
    down_other = lax.ppermute(down1, "grp", [(0, 1), (1, 0)])

    weights = (attn_input, attn_output, g1, g2, router_t)
    block, grad0, *sums = back(
        0, scal, plan, ret[0], saved[0], tokens, cotangent, *weights, None
    )
    halves = lax.optimization_barrier((up1, up_other, down1, down_other, sums[2]))
    up_sum = halves[0].astype(F32) + halves[1].astype(F32)
    down_sum = halves[2].astype(F32) + halves[3].astype(F32)
    up_sum, down_sum, sums[2] = lax.optimization_barrier((up_sum, down_sum, halves[4]))
    block, dx1, dqkv1, *pay = back(
        1, scal, plan, ret[1], saved[1], tokens, cotangent, *weights, (block, *sums)
    )

    def beside():
        return finish(1, dqkv1, dx1, tokens, attn_input, g1, grad0)

    *dense, tokens_grad = reduce_all(pay[:2], pay[2:], scal, plan, width, experts, beside)
    return (block, tokens_grad, *dense, up_sum[None], down_sum[None])


def solution(mesh):
    split = P(None, ("grp", "exp"), None)
    owned = P("exp", None, None)
    in_specs = (split,) * 3 + (P(),) * 5 + (owned, owned, split)
    out_specs = (split, split) + (P(),) * 5 + (owned, owned)
    return jax.shard_map(shards, mesh=mesh, in_specs=in_specs, out_specs=out_specs, check_vma=False)
```

```python
import functools

import jax
import jax.numpy as jnp
from jax import lax
from jax.experimental import pallas as pl
from jax.experimental.pallas import tpu as pltpu
from jax.sharding import PartitionSpec as P

HEADS = 8
HEAD = 64
SEQ = 144
MICRO = 2
EPS = 1e-06
FORE_HEADS = 2
BACK_HEADS = 4
GELU_C = 0.7978845608028654
GELU_A = 0.044715
SMALL = 32

BF = jnp.bfloat16
F32 = jnp.float32
MB = 1 << 20
FORE_MB = 60
EXPERT_MB = 48
BACK_MB = 60
FINISH_MB = 60
LAST_MB = 50
FILLS = 4
IN_VMEM = pl.BlockSpec(memory_space=pltpu.VMEM)
IN_HBM = pl.BlockSpec(memory_space=pltpu.HBM)


def nn(a, b):
    return lax.dot_general(a, b, (((1,), (0,)), ((), ())), preferred_element_type=F32)


def nt(a, b):
    return lax.dot_general(a, b, (((1,), (1,)), ((), ())), preferred_element_type=F32)


def tn(a, b):
    return lax.dot_general(a, b, (((0,), (0,)), ((), ())), preferred_element_type=F32)


def normalize(values):
    center = values - jnp.mean(values, axis=-1, keepdims=True)
    factor = lax.rsqrt(jnp.mean(center * center, axis=-1, keepdims=True) + EPS)
    return center * factor, factor


def norm_back(grad_normed, normed, factor):
    return factor * (
        grad_normed
        - jnp.mean(grad_normed, axis=-1, keepdims=True)
        - normed * jnp.mean(grad_normed * normed, axis=-1, keepdims=True)
    )


def iota(shape, dim):
    return lax.broadcasted_iota(jnp.int32, shape, dim)


def spread_heads(block):
    head = iota(block.shape, 1) // HEAD
    zero = jnp.zeros_like(block)
    count = block.shape[1] // HEAD
    return jnp.concatenate([jnp.where(head == h, block, zero) for h in range(count)], axis=0)


def gather_heads(full):
    count = full.shape[1] // HEAD
    rows = full.shape[0] // count
    head = iota((rows, full.shape[1]), 1) // HEAD
    total = jnp.where(head == 0, full[:rows], 0.0)
    for h in range(1, count):
        total = total + jnp.where(head == h, full[h * rows : (h + 1) * rows], 0.0)
    return total


def head_block(ref, rows, part, group, count, width):
    start = part * width + group * count * HEAD
    return ref[rows, start : start + count * HEAD]


def fore_kernel(cap, micro, *refs):
    tok_h, pick_h, rank_h, wqkv_h, wo_h, g1_h, g2_h, router_h, cot_h = refs[:9]
    count = 6 if micro == 0 else 7
    outs, refs = refs[9 : 9 + count], refs[9 + count :]
    send_h, qkv_h, mixed_h, x1_h, level_h, meta_h = outs[:6]
    tok_ref, pick_ref, rank_ref, wqkv_ref, wo_ref, g1_ref, g2_ref, router_ref, cot_ref = refs[:9]
    held, refs = refs[9 : 9 + count], refs[9 + count :]
    send_ref, qkv_ref, mixed_ref, x1_ref, level_ref, meta_ref = held[:6]
    all_s, in_sem, out_sem = refs
    rows, width = x1_ref.shape
    experts = router_ref.shape[0]
    images = rows // SEQ
    pairs = (
        (pick_h.at[micro], pick_ref),
        (rank_h.at[micro], rank_ref),
        (tok_h.at[micro], tok_ref),
        (g1_h, g1_ref),
        (wqkv_h, wqkv_ref),
        (wo_h, wo_ref),
        (g2_h, g2_ref),
        (router_h, router_ref),
        (cot_h.at[micro], cot_ref),
    )
    loads = [move(a, b, in_sem.at[n]) for n, (a, b) in enumerate(pairs)]

    loads[0].wait()
    loads[1].wait()
    rank_row = rank_ref[...].astype(F32)
    eye = iota((rows, rows), 0) == iota((rows, rows), 1)
    rank_col = jnp.sum(jnp.where(eye, rank_row, 0.0), axis=1, keepdims=True)
    less = jnp.where(rank_col < rank_row, 1.0, 0.0).astype(BF)
    picks = pick_ref[...]
    expert = iota((experts, rows), 0)
    on = [jnp.where(expert == picks[k : k + 1], 1.0, 0.0) for k in range(2)]
    before = [nn(on[k].astype(BF), less) for k in range(2)]
    before[1] = before[1] + jnp.sum(on[0], axis=1, keepdims=True)
    place = []
    for k in range(2):
        slot = jnp.sum(on[k] * before[k], axis=0, keepdims=True)
        base = picks[k : k + 1].astype(F32) * (2 * cap)
        place.append(jnp.where(slot < cap - 0.5, base + slot, -9999.0))

    loads[2].wait()
    loads[3].wait()
    x_in = tok_ref[...].astype(F32)
    normed, _ = normalize(x_in)
    h_first = (normed * g1_ref[...]).astype(BF)
    loads[4].wait()
    qkv_ref[...] = nn(h_first, wqkv_ref[...]).astype(BF)
    stores = [move(qkv_ref, qkv_h, out_sem.at[1])]
    if micro > 0:
        held[6][...] = h_first
        stores.append(move(held[6], outs[6], out_sem.at[6 + FILLS]))

    groups = HEADS // FORE_HEADS
    wide = FORE_HEADS * HEAD
    def image(i, carry):
        at = pl.ds(pl.multiple_of(i * SEQ, 16), SEQ)
        for g in range(groups):
            query = spread_heads(head_block(qkv_ref, at, 0, g, FORE_HEADS, width))
            key = head_block(qkv_ref, at, 1, g, FORE_HEADS, width)
            value = head_block(qkv_ref, at, 2, g, FORE_HEADS, width)
            scores = nt(key, query) * (HEAD**-0.5)
            peak = jnp.max(scores, axis=0, keepdims=True)
            expo = jnp.exp(scores - peak)
            denom = jnp.sum(expo, axis=0, keepdims=True)
            probs_low = (expo * (1.0 / denom)).astype(BF)
            if micro == 0:
                level_ref[pl.ds(i * groups + g, 1), :] = peak + jnp.log(denom)
            else:
                each = BACK_HEADS // FORE_HEADS
                line = (i * (HEADS // BACK_HEADS) + g // each) * SEQ
                column = g % each * FORE_HEADS * SEQ
                to = pl.ds(pl.multiple_of(line, 16), SEQ)
                level_ref[to, column : column + FORE_HEADS * SEQ] = probs_low
            mixed = gather_heads(tn(probs_low, value))
            mixed_ref[at, g * wide : (g + 1) * wide] = mixed.astype(BF)
        return carry

    lax.fori_loop(0, images, image, 0, unroll=micro == 0)

    stores.append(move(mixed_ref, mixed_h, out_sem.at[2]))
    stores.append(move(level_ref, level_h, out_sem.at[4]))

    for n in range(5, 9):
        loads[n].wait()
    x_mid = tok_ref[...].astype(F32) + nn(mixed_ref[...], wo_ref[...])
    x1_ref[...] = x_mid
    stores.append(move(x1_ref, x1_h, out_sem.at[3]))
    normed, _ = normalize(x_mid)
    h_second = (normed * g2_ref[...]).astype(BF)
    all_s[:rows, :] = h_second
    logits = nt(router_ref[...], h_second)
    picked = [jnp.sum(on[k] * logits, axis=0, keepdims=True) for k in range(2)]
    top = jnp.maximum(picked[0], picked[1])
    expo = [jnp.exp(v - top) for v in picked]
    total = expo[0] + expo[1]
    gates = [v / total for v in expo]
    stack = jnp.concatenate(
        gates + place + [picks.astype(F32)] + [jnp.zeros((2, rows), F32)], axis=0
    )
    meta = jnp.transpose(stack)
    meta_ref[...] = meta
    stores.append(move(meta_ref, meta_h, out_sem.at[5]))
    grad_out = cot_ref[...].astype(F32)
    all_s[rows : 2 * rows, :] = (meta[:, 0:1] * grad_out).astype(BF)
    all_s[2 * rows :, :] = (meta[:, 1:2] * grad_out).astype(BF)
    place = [v.astype(jnp.int32) for v in place]

    gone = jnp.full((1, 2 * rows), -1, jnp.int32)
    pos_a = jnp.concatenate([place[0], place[0] + cap, place[1] + cap], axis=1)
    pos_b = jnp.concatenate([place[1], gone], axis=1)
    step = send_ref.shape[0] // FILLS
    for c in range(FILLS):
        start = c * step
        row = iota((step, 3 * rows), 0) + start
        first = jnp.where((row == pos_a) | (row == pos_b), 1.0, 0.0).astype(BF)
        part = nn(first, all_s[...])
        send_ref[pl.ds(start, step), :] = part.astype(BF)
        at = pl.ds(start, step)
        stores.append(move(send_ref.at[at], send_h.at[at], out_sem.at[6 + c]))
    for copy in stores:
        copy.wait()


def move(source, target, sem):
    copy = pltpu.make_async_copy(source, target, sem)
    copy.start()
    return copy


def micro_spec(shape, micro):
    return pl.BlockSpec((1,) + tuple(shape[1:]), lambda i: (micro,) + (0,) * (len(shape) - 1))


def whole_spec(shape):
    return pl.BlockSpec(tuple(shape), lambda i: (0,) * len(shape))


def params(limit, **more):
    return pltpu.CompilerParams(vmem_limit_bytes=limit * MB, **more)


def fore(micro, cap, tokens, picks_t, ranks, wqkv, wo, g1, g2, router_t, cot):
    _, rows, width = tokens.shape
    experts = router_t.shape[0]
    out_shape = (
        jax.ShapeDtypeStruct((experts * 2 * cap, width), BF),
        jax.ShapeDtypeStruct((rows, 3 * width), BF),
        jax.ShapeDtypeStruct((rows, width), BF),
        jax.ShapeDtypeStruct((rows, width), F32),
        jax.ShapeDtypeStruct((rows // SEQ * HEADS // FORE_HEADS, FORE_HEADS * SEQ), F32),
        jax.ShapeDtypeStruct((rows, 8), F32),
    )
    if micro > 0:
        probs = jax.ShapeDtypeStruct((rows * HEADS // BACK_HEADS, BACK_HEADS * SEQ), BF)
        first = jax.ShapeDtypeStruct((rows, width), BF)
        out_shape = out_shape[:4] + (probs, out_shape[5], first)
    flops = 2 * rows * width * (4 * width + 3 * experts * 2 * cap + 4 * SEQ)
    return pl.pallas_call(
        functools.partial(fore_kernel, cap, micro),
        in_specs=[IN_HBM] * 9,
        out_specs=[IN_HBM] * len(out_shape),
        out_shape=out_shape,
        scratch_shapes=[
            pltpu.VMEM((rows, width), BF),
            pltpu.VMEM(picks_t.shape[1:], jnp.int32),
            pltpu.VMEM(ranks.shape[1:], jnp.int32),
            pltpu.VMEM(wqkv.shape, BF),
            pltpu.VMEM(wo.shape, BF),
            pltpu.VMEM(g1.shape, F32),
            pltpu.VMEM(g2.shape, F32),
            pltpu.VMEM(router_t.shape, BF),
            pltpu.VMEM((rows, width), BF),
        ]
        + [pltpu.VMEM(v.shape, v.dtype) for v in out_shape]
        + [pltpu.VMEM((3 * rows, width), BF)]
        + [pltpu.SemaphoreType.DMA((9,)), pltpu.SemaphoreType.DMA((7 + FILLS,))],
        compiler_params=params(FORE_MB),
        cost_estimate=pl.CostEstimate(flops=4 * flops, bytes_accessed=8 * MB, transcendentals=0),
        name="fore",
    )(tokens, picks_t, ranks, wqkv, wo, g1, g2, router_t, cot)


def expert_kernel(cap, first, *refs):
    if first:
        recv_ref, up_ref, down_ref, ret_ref, dup_ref, ddown_ref = refs[:6]
    else:
        recv_ref, up_ref, down_ref, aup_ref, adown_ref, ret_ref, dup_ref, ddown_ref = refs[:8]
    h_s, g_s, out_s, row_s = refs[-4:]
    step = pl.program_id(0)
    steps = pl.num_programs(0)
    slots = h_s.shape[0]

    def position(shape, dim, start):
        slot = iota(shape, dim) + start
        block = ((slot.astype(F32) + 0.5) * (1.0 / cap)).astype(jnp.int32)
        return slot + block * cap

    part = slots // 4

    @pl.when(step == 0)
    def _():
        def take(c, carry):
            at = pl.ds(pl.multiple_of(c * part, 16), part)
            here = iota((part, 2 * slots), 1)
            there = position((part, 2 * slots), 0, c * part)
            pick = jnp.where(here == there, 1.0, 0.0).astype(BF)
            h_s[at, :] = nn(pick, recv_ref[...]).astype(BF)
            pick = jnp.where(here == there + cap, 1.0, 0.0).astype(BF)
            g_s[at, :] = nn(pick, recv_ref[...]).astype(BF)
            return carry

        lax.fori_loop(0, 4, take, 0)

    up = up_ref[0]
    down = down_ref[0]
    h = h_s[...]
    g = g_s[...]
    pre = nn(h, up)
    grad_act = nt(g, down)
    square = pre * pre
    tanh = jnp.tanh(GELU_C * pre * (1.0 + GELU_A * square))
    half = 0.5 + 0.5 * tanh
    act = (pre * half).astype(BF)
    slope = half + (0.5 * GELU_C) * pre * (1.0 - tanh * tanh) * (1.0 + 3.0 * GELU_A * square)
    grad_pre = (grad_act * slope).astype(BF)
    grad_up = tn(h, grad_pre)
    grad_down = tn(act, g)
    if not first:
        grad_up = grad_up + aup_ref[...]
        grad_down = grad_down + adown_ref[...]
    dup_ref[...] = grad_up.astype(dup_ref.dtype)
    ddown_ref[...] = grad_down.astype(ddown_ref.dtype)
    out = nn(act, down)
    row = nt(grad_pre, up)

    @pl.when(step == 0)
    def _():
        out_s[...] = out
        row_s[...] = row

    @pl.when(step > 0)
    def _():
        out_s[...] += out
        row_s[...] += row

    @pl.when(step == steps - 1)
    def _():
        def give(c, carry):
            at = pl.ds(pl.multiple_of(c * 2 * part, 16), 2 * part)
            here = iota((2 * part, slots), 0) + c * 2 * part
            there = position((2 * part, slots), 1, 0)
            pick = jnp.where(here == there, 1.0, 0.0).astype(BF)
            total = nn(pick, out_s[...].astype(BF))
            pick = jnp.where(here == there + cap, 1.0, 0.0).astype(BF)
            total = total + nn(pick, row_s[...].astype(BF))
            ret_ref[at, :] = total.astype(BF)
            return carry

        lax.fori_loop(0, 4, give, 0)


def expert(cap, recv, up, down, earlier):
    first = earlier is None
    total, width = recv.shape
    slots = total // 2
    hidden = up.shape[2]
    tile = 512
    dtype = F32 if first else BF
    up_block = pl.BlockSpec((width, tile), lambda i: (0, i))
    down_block = pl.BlockSpec((tile, width), lambda i: (i, 0))
    in_specs = [
        whole_spec(recv.shape),
        pl.BlockSpec((1, width, tile), lambda i: (0, 0, i)),
        pl.BlockSpec((1, tile, width), lambda i: (0, i, 0)),
    ]
    args = [recv, up, down]
    if not first:
        in_specs += [up_block, down_block]
        args += list(earlier)
    return pl.pallas_call(
        functools.partial(expert_kernel, cap, first),
        grid=(hidden // tile,),
        in_specs=in_specs,
        out_specs=[whole_spec(recv.shape), up_block, down_block],
        out_shape=(
            jax.ShapeDtypeStruct(recv.shape, BF),
            jax.ShapeDtypeStruct((width, hidden), dtype),
            jax.ShapeDtypeStruct((hidden, width), dtype),
        ),
        scratch_shapes=[
            pltpu.VMEM((slots, width), BF),
            pltpu.VMEM((slots, width), BF),
            pltpu.VMEM((slots, width), F32),
            pltpu.VMEM((slots, width), F32),
        ],
        compiler_params=params(EXPERT_MB),
        cost_estimate=pl.CostEstimate(
            flops=2 * 12 * slots * width * hidden, bytes_accessed=24 * MB, transcendentals=0
        ),
        name="expert",
    )(*args)


def back_kernel(last, micro, *refs):
    take = list(refs)

    def next_refs(count):
        taken, take[:] = take[:count], take[count:]
        return taken

    scal_ref, ret_ref = next_refs(2)
    sources = next_refs(BACK_INS)
    earlier_h = next_refs(4) if last else []
    block_h, dx1_h = next_refs(2)
    (dqkv_h,) = next_refs(1) if last else (None,)
    made_h = next_refs(4 if last else 3)
    held = next_refs(BACK_INS)
    (
        meta_ref,
        cot_ref,
        x1_ref,
        g2_ref,
        router_ref,
        mixed_ref,
        wo_ref,
        qkv_ref,
        level_ref,
        tok_ref,
        g1_ref,
        wqkv_ref,
    ) = held
    in_ref, out_ref, small_ref = next_refs(3)
    block_ref, dx1_ref, dqkv_ref, dmix_s, in_sem, out_sem = next_refs(6)
    if last:
        tail_s, pay_s = next_refs(2)
    sources = [h.at[micro] if h.shape[0] == MICRO else h for h in sources]
    pairs = list(zip(sources, held))
    if last:
        pairs += list(zip(earlier_h[:3], (in_ref, out_ref, small_ref)))
    loads = [move(a, b, in_sem.at[n]) for n, (a, b) in enumerate(pairs[:8])]
    stores = []
    total = ret_ref.shape[0]
    rows, width = x1_ref.shape
    experts = router_ref.shape[0]

    def store(source, target):
        stores.append(move(source, target, out_sem.at[len(stores)]))

    loads[0].wait()
    meta = meta_ref[...]
    gates = [meta[:, k : k + 1] for k in range(2)]
    place = [meta[:, 2 + k : 3 + k].astype(jnp.int32) for k in range(2)]
    picks = [meta[:, 4 + k : 5 + k].astype(jnp.int32) for k in range(2)]
    cap = total // (2 * experts)
    here = iota((rows, total), 1)
    ret = ret_ref[...]
    both = (here == place[0] + cap) | (here == place[1] + cap)
    hot = [jnp.where(m, 1.0, 0.0).astype(BF) for m in (both, here == place[0], here == place[1])]
    stacked = nn(jnp.concatenate(hot, axis=0), ret)
    grad_second = stacked[:rows]
    pair_out = [stacked[rows : 2 * rows], stacked[2 * rows :]]
    for n in range(1, 5):
        loads[n].wait()
    loads += [move(a, b, in_sem.at[8 + n]) for n, (a, b) in enumerate(pairs[8:])]
    grad_out = cot_ref[...].astype(F32)
    x_mid = x1_ref[...]
    result = x_mid
    grad_gate = []
    for k in range(2):
        result = result + gates[k] * pair_out[k]
        grad_gate.append(jnp.sum(grad_out * pair_out[k], axis=1, keepdims=True))
    block_ref[...] = result.astype(BF)
    store(block_ref, block_h.at[micro])
    mean_gate = gates[0] * grad_gate[0] + gates[1] * grad_gate[1]
    lane = iota((rows, experts), 1)
    grad_logits = jnp.zeros((rows, experts), F32)
    for k in range(2):
        grad_pick = gates[k] * (grad_gate[k] - mean_gate)
        grad_logits = grad_logits + jnp.where(lane == picks[k], grad_pick, 0.0)
    grad_logits = grad_logits.astype(BF)
    grad_second = grad_second + nn(grad_logits, router_ref[...])
    normed, factor = normalize(x_mid)
    h_second = (normed * g2_ref[...]).astype(BF)
    small = [
        tn(grad_logits, h_second),
        jnp.sum(grad_second * normed, axis=0, keepdims=True),
    ]
    grad_mid = grad_out + norm_back(grad_second * g2_ref[...], normed, factor)
    dx1_ref[...] = grad_mid
    if last:
        store(dx1_ref, dx1_h)
    for n in range(5, 9):
        loads[n].wait()
    grad_attn = grad_mid.astype(BF)
    out_grad = tn(mixed_ref[...], grad_attn)
    if last:
        slots = 2 * lax.axis_size("exp")
        half = slots // 2
        piece = width // half
        span = half * piece
        tail = SMALL * (experts // 16)

        def lay(s, b, block):
            mine = scal_ref[2] == b
            start = jnp.where(mine, 0, half)
            order = jnp.where(mine, scal_ref[0], scal_ref[1])
            for j in range(half):
                to = pl.multiple_of((start + (j ^ order)) * piece, piece)
                pay_s[s, pl.ds(to, piece), :] = block[j * piece : (j + 1) * piece].astype(BF)

        for copy in loads[13:15]:
            copy.wait()
        lay(1, 1, out_grad + out_ref[...].astype(F32))
        small[0] = small[0] + small_ref[0:experts, :]
        small[1] = small[1] + small_ref[experts : experts + 1, :]
        tail_s[:experts, :] = small[0].astype(BF)
    else:
        out_ref[...] = out_grad.astype(BF)
        small_ref[0:experts, :] = small[0]
        small_ref[experts : experts + 1, :] = small[1]
        small_ref[experts + 1 :, :] = jnp.zeros((small_ref.shape[0] - experts - 1, width), F32)
        store(out_ref, made_h[1])
        store(small_ref, made_h[2])
    dmix_s[...] = nt(grad_attn, wo_ref[...]).astype(BF)

    groups = HEADS // BACK_HEADS
    wide = BACK_HEADS * HEAD
    lines = BACK_HEADS // FORE_HEADS
    def image(i, carry):
        at = pl.ds(pl.multiple_of(i * SEQ, 16), SEQ)
        for g in range(groups):
            query = spread_heads(head_block(qkv_ref, at, 0, g, BACK_HEADS, width))
            key = head_block(qkv_ref, at, 1, g, BACK_HEADS, width)
            value = head_block(qkv_ref, at, 2, g, BACK_HEADS, width)
            grad_mixed = spread_heads(dmix_s[at, g * wide : (g + 1) * wide])
            if last:
                line = pl.multiple_of((i * groups + g) * SEQ, 16)
                probs_low = level_ref[pl.ds(line, SEQ), :]
                probs = probs_low.astype(F32)
            else:
                scores = nt(key, query) * (HEAD**-0.5)
                line = (i * groups + g) * lines
                level = [level_ref[pl.ds(line + n, 1), :] for n in range(lines)]
                probs = jnp.exp(scores - jnp.concatenate(level, axis=1))
                probs_low = probs.astype(BF)
            grad_probs = nt(value, grad_mixed)
            inner = jnp.sum(probs * grad_probs, axis=0, keepdims=True)
            grad_scores = (probs * (grad_probs - inner)).astype(BF)
            grad_value = nn(probs_low, grad_mixed)
            grad_key = nn(grad_scores, query) * (HEAD**-0.5)
            grad_query = gather_heads(tn(grad_scores, key)) * (HEAD**-0.5)
            for part, grad in enumerate((grad_query, grad_key, grad_value)):
                start = part * width + g * wide
                dqkv_ref[at, start : start + wide] = grad.astype(BF)
        return carry

    lax.fori_loop(0, rows // SEQ, image, 0, unroll=last)

    if last:
        store(dqkv_ref, dqkv_h)
    for n in range(9, 13 if last else 12):
        loads[n].wait()
    if last:
        h_first = tok_ref[...]
    else:
        normed, factor = normalize(tok_ref[...].astype(F32))
        h_first = (normed * g1_ref[...]).astype(BF)
    gain = jnp.zeros((width, 1), F32)
    for part in (2, 0, 1):
        columns = slice(part * width, (part + 1) * width)
        in_grad = tn(h_first, dqkv_ref[:, columns])
        if not last:
            in_ref[:, columns] = in_grad.astype(BF)
            continue
        in_grad = in_grad + in_ref[:, columns].astype(F32)
        gain = gain + jnp.sum(wqkv_ref[:, columns].astype(F32) * in_grad, axis=1, keepdims=True)
        lay(part // 2, part % 2, in_grad)
        if part != 0:
            s = part // 2
            store(pay_s.at[s, pl.ds(span, span)], made_h[s].at[pl.ds(0, span)])
            store(pay_s.at[s, pl.ds(0, span)], made_h[2 + s].at[pl.ds(0, span)])
    if last:
        eye = iota((width, width), 0) == iota((width, width), 1)
        gain = jnp.sum(jnp.where(eye, gain, 0.0), axis=0, keepdims=True) / g1_ref[...]
        fill = jnp.zeros((tail - experts - 2, width), F32)
        tail_s[experts:, :] = jnp.concatenate([small[1], gain, fill], axis=0).astype(BF)
        for target in (made_h[0], made_h[2]):
            store(tail_s, target.at[pl.ds(span, tail)])
    else:
        store(in_ref, made_h[0])
        grad_first = nt(dqkv_ref[...], wqkv_ref[...]) * g1_ref[...]
        dx1_ref[...] = dx1_ref[...] + norm_back(grad_first, normed, factor)
        store(dx1_ref, dx1_h.at[micro])
    for copy in stores:
        copy.wait()


BACK_INS = 12


def back(micro, scal, plan, ret, saved, tokens, cot, wqkv, wo, g1, g2, router_t, earlier):
    last = earlier is not None
    qkv, mixed, x1, level, meta, *more = saved
    _, rows, width = tokens.shape
    experts = router_t.shape[0]
    slots, piece, tail = plan
    ins = [meta, cot, x1, g2, router_t, mixed, wo, qkv, level, *(more or [tokens]), g1, wqkv]
    shapes = [
        jax.ShapeDtypeStruct(tokens.shape, BF),
        jax.ShapeDtypeStruct((rows, width), F32),
        jax.ShapeDtypeStruct((rows, 3 * width), BF),
    ]
    kept = list(shapes)
    if not last:
        shapes = [shapes[0], jax.ShapeDtypeStruct(tokens.shape, F32)]
    sums = [
        jax.ShapeDtypeStruct(wqkv.shape, BF),
        jax.ShapeDtypeStruct(wo.shape, BF),
        jax.ShapeDtypeStruct((experts + 8, width), F32),
    ]

    def hold(value):
        shape = value.shape[1:] if value.shape[0] == MICRO else value.shape
        return pltpu.VMEM(shape, value.dtype)

    scratch = [hold(a) for a in ins + sums + kept]
    scratch += [
        pltpu.VMEM((rows, width), BF),
        pltpu.SemaphoreType.DMA((16,)),
        pltpu.SemaphoreType.DMA((12,)),
    ]
    aliases = {}
    if last:
        block, *sums = earlier
        args = [scal, ret] + ins + sums + [block]
        aliases = {17: 0}
        span = slots // 2 * piece
        shapes += [jax.ShapeDtypeStruct((span + more, width), BF) for more in (tail, 0)] * 2
        scratch += [pltpu.VMEM((tail, width), BF), pltpu.VMEM((2, slots * piece, width), BF)]
    else:
        args = [scal, ret] + ins
        shapes += sums
    in_specs = [pl.BlockSpec(memory_space=pltpu.SMEM), IN_VMEM] + [IN_HBM] * (len(args) - 2)
    out_specs = [IN_HBM] * len(shapes)
    flops = 2 * rows * width * (3 * ret.shape[0] + 12 * width)
    return pl.pallas_call(
        functools.partial(back_kernel, last, micro),
        in_specs=in_specs,
        out_specs=out_specs,
        out_shape=shapes,
        scratch_shapes=scratch,
        input_output_aliases=aliases,
        compiler_params=params(LAST_MB if last else BACK_MB),
        cost_estimate=pl.CostEstimate(flops=5 * flops, bytes_accessed=20 * MB, transcendentals=0),
        name="back",
    )(*args)


def finish_kernel(dqkv_ref, dx1_ref, tok_ref, wqkv_ref, g1_ref, *refs):
    grad_first = nt(dqkv_ref[...], wqkv_ref[...])
    normed, factor = normalize(tok_ref[0].astype(F32))
    refs[-1][0] = dx1_ref[...] + norm_back(grad_first * g1_ref[...], normed, factor)


def finish(micro, dqkv, dx1, tokens, wqkv, g1, earlier):
    _, rows, width = tokens.shape
    each = rows // 2
    both = pl.BlockSpec((1, each, width), lambda i: (micro, i, 0))
    in_specs = [
        pl.BlockSpec((each, 3 * width), lambda i: (i, 0)),
        pl.BlockSpec((each, width), lambda i: (i, 0)),
        both,
        whole_spec(wqkv.shape),
        whole_spec(g1.shape),
    ]
    args = [dqkv, dx1, tokens, wqkv, g1, earlier]
    in_specs.append(IN_HBM)
    return pl.pallas_call(
        finish_kernel,
        grid=(2,),
        in_specs=in_specs,
        out_specs=both,
        out_shape=jax.ShapeDtypeStruct(tokens.shape, F32),
        input_output_aliases={5: 0},
        compiler_params=params(FINISH_MB),
        cost_estimate=pl.CostEstimate(
            flops=2 * rows * width * 3 * width, bytes_accessed=6 * MB, transcendentals=0
        ),
        name="finish",
    )(*args)


def local(kernel, shapes, args, scalars=0, scratch=()):
    specs = [pl.BlockSpec(memory_space=pltpu.SMEM)] * scalars
    specs += [pl.BlockSpec(memory_space=pltpu.VMEM)] * (len(args) - scalars)
    size = sum(a.size * 4 for a in args)
    return pl.pallas_call(
        kernel,
        in_specs=specs,
        out_specs=[pl.BlockSpec(memory_space=pltpu.VMEM)] * len(shapes),
        out_shape=shapes,
        scratch_shapes=list(scratch),
        compiler_params=params(32),
        cost_estimate=pl.CostEstimate(flops=1000, bytes_accessed=size, transcendentals=0),
    )(*args)


def halve(keep, arrived, count, piece):
    rows, width = keep.shape
    half = count // 2 * piece
    tail = rows - 2 * half

    def kernel(keep_ref, arrived_ref, send_out, keep_out):
        total = (keep_ref[...].astype(F32) + arrived_ref[...].astype(F32)).astype(BF)
        keep_out[:half, :] = total[:half]
        if tail:
            keep_out[half:, :] = total[2 * half :]
        send_out[...] = total[half:]

    shape = jax.ShapeDtypeStruct((half + tail, width), BF)
    return local(kernel, [shape] * 2, [keep, arrived])


def join(first, second):
    rows, width = first.shape

    def kernel(a, b, out):
        out[:rows, :] = a[...]
        out[rows:, :] = b[...]

    (made,) = local(kernel, [jax.ShapeDtypeStruct((2 * rows, width), BF)], [first, second])
    return made


def reduce_all(sends, keeps, scal, plan, width, experts, beside):
    slots, piece, tail = plan
    size = lax.axis_size("exp")
    bits = size.bit_length() - 1
    orders = halving_orders(size)
    low, high = 1 << (bits - 2), 1 << (bits - 1)
    groups = [low, high, low | high]

    def swap(value, step):
        pairs = []
        for core in range(2):
            mask = 1 << orders[core][step]
            pairs += [(core * size + i, core * size + (i ^ mask)) for i in range(size)]
        return lax.ppermute(value, ("grp", "exp"), pairs)

    def swap_far(value, mask):
        return lax.ppermute(value, "exp", [(i, i ^ mask) for i in range(size)])

    def swap_core(value):
        return lax.ppermute(value, "grp", [(0, 1), (1, 0)])

    arrived = [swap_core(v) for v in sends]
    count = slots // 2
    steps = bits - 2
    for step in range(steps):
        made = [halve(keeps[s], arrived[s], count, piece) for s in range(2)]
        count //= 2
        arrived = [swap(made[s][0], step) for s in range(2)]
        keeps = [v[1] for v in made]
        if step == 0:
            extra = beside()
            arrived[0], extra = lax.optimization_barrier((arrived[0], extra))

    share = tail // 4
    span = 2 * piece + share

    def quarter(scal_ref, *refs):
        small_s = refs[8]
        for s in range(2):
            total = refs[s][...].astype(F32) + refs[2 + s][...].astype(F32)
            for j in range(4):
                block = total[j * piece : (j + 1) * piece]
                refs[4 + j][s * piece : (s + 1) * piece, :] = block.astype(BF)
            if s == 0:
                small_s[...] = total[4 * piece :]
        for j in range(4):
            part = pl.multiple_of((scal_ref[3] ^ j) * share, share)
            refs[4 + j][2 * piece :, :] = small_s[pl.ds(part, share), :].astype(BF)

    shape = jax.ShapeDtypeStruct((span, width), BF)
    made = local(
        quarter,
        [shape] * 4,
        [scal] + list(keeps) + list(arrived),
        scalars=1,
        scratch=[pltpu.VMEM((tail, width), F32)],
    )
    arrived = [swap_far(made[1 + j], groups[j]) for j in range(3)]

    def add_up(a, b, c, d, mine_ref):
        total = (a[...].astype(F32) + b[...].astype(F32)) + (c[...].astype(F32) + d[...].astype(F32))
        mine_ref[...] = total.astype(BF)

    (mine,) = local(add_up, [shape], [made[0]] + arrived)

    others = [swap_far(mine, groups[j]) for j in range(3)]

    def lay(scal_ref, a, b, c, d, one_ref, two_ref, small_ref):
        for j, ref in enumerate((a, b, c, d)):
            one_ref[j * piece : (j + 1) * piece, :] = ref[:piece, :]
            two_ref[j * piece : (j + 1) * piece, :] = ref[piece : 2 * piece, :]
            part = pl.multiple_of((scal_ref[3] ^ j) * share, share)
            small_ref[pl.ds(part, share), :] = ref[2 * piece :, :].astype(F32)

    shape = jax.ShapeDtypeStruct((4 * piece, width), BF)
    *have, small = local(
        lay,
        [shape] * 2 + [jax.ShapeDtypeStruct((tail, width), F32)],
        [scal, mine] + others,
        scalars=1,
    )
    vectors = (small[experts + 1], small[experts], small[:experts].T)
    for step in reversed(range(1, steps)):
        arrived = [swap(have[s], step) for s in range(2)]
        have = [join(have[s], arrived[s]) for s in range(2)]
    count = slots // 4
    rows = count * piece

    def deal(first, whose, *refs):
        scal_ref, refs = refs[0], refs[1:]
        in_h, out_h, block_s, sems = refs[-4:]
        core = scal_ref[2]
        copies, later = [], []
        for n, (s, other) in enumerate(whose):
            order = scal_ref[other]
            part = 1 - core if other else core
            for pos in range(count):
                to = pl.multiple_of(((pos ^ order) % count) * piece, piece)
                block = refs[n][pos * piece : (pos + 1) * piece, :].astype(F32)
                block_s[n, pl.ds(to, piece), :] = block
            half = (order // count + (0 if first else 1)) % 2
            at = pl.ds(pl.multiple_of(half * rows, rows), rows)
            if s == 0:
                columns = pl.ds(pl.multiple_of(part * width, width), width)
                copies.append(move(block_s.at[n], in_h.at[at, columns], sems.at[n]))
            else:
                later.append((n, part, at))
        for n, part, at in later:

            @pl.when(part == 0)
            def _():
                target = in_h.at[at, pl.ds(2 * width, width)]
                move(block_s.at[n], target, sems.at[n]).wait()

            @pl.when(part == 1)
            def _():
                move(block_s.at[n], out_h.at[at], sems.at[n]).wait()

        for copy in copies:
            copy.wait()

    def dealt(first, whose, values, grads):
        number = len(values)
        grads = [] if grads is None else list(grads)
        return pl.pallas_call(
            functools.partial(deal, first, whose),
            in_specs=[pl.BlockSpec(memory_space=pltpu.SMEM)]
            + [IN_VMEM] * number
            + [IN_HBM] * len(grads),
            out_specs=[IN_HBM, IN_HBM],
            out_shape=(
                jax.ShapeDtypeStruct((width, 3 * width), F32),
                jax.ShapeDtypeStruct((width, width), F32),
            ),
            input_output_aliases={1 + number: 0, 2 + number: 1} if grads else {},
            scratch_shapes=[
                pltpu.VMEM((number, rows, width), F32),
                pltpu.SemaphoreType.DMA((number,)),
            ],
            compiler_params=params(16),
            cost_estimate=pl.CostEstimate(flops=1000, bytes_accessed=4 * MB, transcendentals=0),
            name="deal",
        )(scal, *values, *grads)

    arrived = [swap(have[s], 0) for s in range(2)]
    near = [swap_core(v) for v in have]
    grads = dealt(True, ((0, 0), (1, 0), (0, 1), (1, 1)), [*have, *near], None)
    arrived[1], vectors, grads = lax.optimization_barrier((arrived[1], vectors, grads))
    far = [swap_core(v) for v in arrived]
    grads = dealt(False, ((0, 0), (1, 0)), arrived, grads)
    in_grad, out_grad = dealt(False, ((0, 1), (1, 1)), far, grads)
    return in_grad, out_grad, *vectors, extra


def halving_orders(size):
    bits = size.bit_length() - 1
    first = list(range(bits - 2))
    second = [first[b ^ 1] if (b ^ 1) < len(first) else b for b in first]
    return first, second


def places(size):
    bits = size.bit_length() - 1
    core = lax.axis_index("grp")
    me = lax.axis_index("exp")
    last = me >> (bits - 2)
    made = []
    for order in halving_orders(size):
        value = jnp.zeros_like(me)
        for b in order:
            value = value * 2 + ((me >> b) & 1)
        made.append(value * 4 + last)
    own = jnp.where(core == 0, made[0], made[1])
    other = jnp.where(core == 0, made[1], made[0])
    return jnp.stack([own, other, core, last]).astype(jnp.int32)


def shards(
    tokens,
    expert_picks,
    priority_ranks,
    attn_input,
    attn_output,
    first_gain,
    second_gain,
    router_weight,
    expert_up,
    expert_down,
    cotangent,
):
    size = lax.axis_size("exp")
    experts = router_weight.shape[1]
    rows, width = tokens.shape[1:]
    cap = max(2, rows // size)
    total = experts * 2 * cap
    slots = 2 * size
    plan = (slots, 2 * width // slots, SMALL * (experts // 16))
    scal = places(size)
    picks_t = jnp.transpose(expert_picks, (0, 2, 1))
    router_t = router_weight.T
    g1 = first_gain.reshape(1, width)
    g2 = second_gain.reshape(1, width)

    def exchange(value):
        value = value.reshape(experts, 2 * cap, width)
        value = lax.all_to_all(value, "exp", split_axis=0, concat_axis=0, tiled=True)
        return value.reshape(total, width)

    saved, sent = [], []
    for micro in range(MICRO):
        made = fore(
            micro,
            cap,
            tokens,
            picks_t,
            priority_ranks,
            attn_input,
            attn_output,
            g1,
            g2,
            router_t,
            cotangent,
        )
        sent.append(made[0])
        saved.append(made[1:])
    arrived = [exchange(v) for v in sent]
    answer0, up0, down0 = expert(cap, arrived[0], expert_up, expert_down, None)
    answer1, up1, down1 = expert(cap, arrived[1], expert_up, expert_down, (up0, down0))
    ret = [exchange(v) for v in (answer0, answer1)]
    up_other = lax.ppermute(up1, "grp", [(0, 1), (1, 0)])
    down_other = lax.ppermute(down1, "grp", [(0, 1), (1, 0)])

    weights = (attn_input, attn_output, g1, g2, router_t)
    block, grad0, *sums = back(
        0, scal, plan, ret[0], saved[0], tokens, cotangent, *weights, None
    )
    halves = lax.optimization_barrier((up1, up_other, down1, down_other, sums[2]))
    up_sum = halves[0].astype(F32) + halves[1].astype(F32)
    down_sum = halves[2].astype(F32) + halves[3].astype(F32)
    up_sum, down_sum, sums[2] = lax.optimization_barrier((up_sum, down_sum, halves[4]))
    block, dx1, dqkv1, *pay = back(
        1, scal, plan, ret[1], saved[1], tokens, cotangent, *weights, (block, *sums)
    )

    def beside():
        return finish(1, dqkv1, dx1, tokens, attn_input, g1, grad0)

    *dense, tokens_grad = reduce_all(pay[:2], pay[2:], scal, plan, width, experts, beside)
    return (block, tokens_grad, *dense, up_sum[None], down_sum[None])


def solution(mesh):
    split = P(None, ("grp", "exp"), None)
    owned = P("exp", None, None)
    in_specs = (split,) * 3 + (P(),) * 5 + (owned, owned, split)
    out_specs = (split, split) + (P(),) * 5 + (owned, owned)
    return jax.shard_map(shards, mesh=mesh, in_specs=in_specs, out_specs=out_specs, check_vma=False)
```

```python
import functools

import jax
import jax.numpy as jnp
from jax import lax
from jax.experimental import pallas as pl
from jax.experimental.pallas import tpu as pltpu
from jax.sharding import PartitionSpec as P

HEADS = 8
HEAD = 64
SEQ = 144
MICRO = 2
EPS = 1e-06
FORE_HEADS = 2
BACK_HEADS = 4
GELU_C = 0.7978845608028654
GELU_A = 0.044715
SMALL = 32

BF = jnp.bfloat16
F32 = jnp.float32
MB = 1 << 20
FORE_MB = 60
EXPERT_MB = 48
BACK_MB = 60
FINISH_MB = 60
LAST_MB = 50
FILLS = 4
IN_VMEM = pl.BlockSpec(memory_space=pltpu.VMEM)
IN_HBM = pl.BlockSpec(memory_space=pltpu.HBM)


def nn(a, b):
    return lax.dot_general(a, b, (((1,), (0,)), ((), ())), preferred_element_type=F32)


def nt(a, b):
    return lax.dot_general(a, b, (((1,), (1,)), ((), ())), preferred_element_type=F32)


def tn(a, b):
    return lax.dot_general(a, b, (((0,), (0,)), ((), ())), preferred_element_type=F32)


def normalize(values):
    center = values - jnp.mean(values, axis=-1, keepdims=True)
    factor = lax.rsqrt(jnp.mean(center * center, axis=-1, keepdims=True) + EPS)
    return center * factor, factor


def norm_back(grad_normed, normed, factor):
    return factor * (
        grad_normed
        - jnp.mean(grad_normed, axis=-1, keepdims=True)
        - normed * jnp.mean(grad_normed * normed, axis=-1, keepdims=True)
    )


def iota(shape, dim):
    return lax.broadcasted_iota(jnp.int32, shape, dim)


def spread_heads(block):
    head = iota(block.shape, 1) // HEAD
    zero = jnp.zeros_like(block)
    count = block.shape[1] // HEAD
    return jnp.concatenate([jnp.where(head == h, block, zero) for h in range(count)], axis=0)


def gather_heads(full):
    count = full.shape[1] // HEAD
    rows = full.shape[0] // count
    head = iota((rows, full.shape[1]), 1) // HEAD
    total = jnp.where(head == 0, full[:rows], 0.0)
    for h in range(1, count):
        total = total + jnp.where(head == h, full[h * rows : (h + 1) * rows], 0.0)
    return total


def head_block(ref, rows, part, group, count, width):
    start = part * width + group * count * HEAD
    return ref[rows, start : start + count * HEAD]


def fore_kernel(cap, micro, *refs):
    tok_h, pick_h, rank_h, wqkv_h, wo_h, g1_h, g2_h, router_h, cot_h = refs[:9]
    count = 6 if micro == 0 else 7
    outs, refs = refs[9 : 9 + count], refs[9 + count :]
    send_h, qkv_h, mixed_h, x1_h, level_h, meta_h = outs[:6]
    tok_ref, pick_ref, rank_ref, wqkv_ref, wo_ref, g1_ref, g2_ref, router_ref, cot_ref = refs[:9]
    held, refs = refs[9 : 9 + count], refs[9 + count :]
    send_ref, qkv_ref, mixed_ref, x1_ref, level_ref, meta_ref = held[:6]
    all_s, in_sem, out_sem = refs
    rows, width = x1_ref.shape
    experts = router_ref.shape[0]
    images = rows // SEQ
    pairs = (
        (pick_h.at[micro], pick_ref),
        (rank_h.at[micro], rank_ref),
        (tok_h.at[micro], tok_ref),
        (g1_h, g1_ref),
        (wqkv_h, wqkv_ref),
        (wo_h, wo_ref),
        (g2_h, g2_ref),
        (router_h, router_ref),
        (cot_h.at[micro], cot_ref),
    )
    loads = [move(a, b, in_sem.at[n]) for n, (a, b) in enumerate(pairs)]

    loads[0].wait()
    loads[1].wait()
    rank_row = rank_ref[...].astype(F32)
    eye = iota((rows, rows), 0) == iota((rows, rows), 1)
    rank_col = jnp.sum(jnp.where(eye, rank_row, 0.0), axis=1, keepdims=True)
    less = jnp.where(rank_col < rank_row, 1.0, 0.0).astype(BF)
    picks = pick_ref[...]
    expert = iota((experts, rows), 0)
    on = [jnp.where(expert == picks[k : k + 1], 1.0, 0.0) for k in range(2)]
    before = [nn(on[k].astype(BF), less) for k in range(2)]
    before[1] = before[1] + jnp.sum(on[0], axis=1, keepdims=True)
    place = []
    for k in range(2):
        slot = jnp.sum(on[k] * before[k], axis=0, keepdims=True)
        base = picks[k : k + 1].astype(F32) * (2 * cap)
        place.append(jnp.where(slot < cap - 0.5, base + slot, -9999.0))

    loads[2].wait()
    loads[3].wait()
    x_in = tok_ref[...].astype(F32)
    normed, _ = normalize(x_in)
    h_first = (normed * g1_ref[...]).astype(BF)
    loads[4].wait()
    qkv_ref[...] = nn(h_first, wqkv_ref[...]).astype(BF)
    stores = [move(qkv_ref, qkv_h, out_sem.at[1])]
    if micro > 0:
        held[6][...] = h_first
        stores.append(move(held[6], outs[6], out_sem.at[6 + FILLS]))

    groups = HEADS // FORE_HEADS
    wide = FORE_HEADS * HEAD
    def image(i, carry):
        at = pl.ds(pl.multiple_of(i * SEQ, 16), SEQ)
        for g in range(groups):
            query = spread_heads(head_block(qkv_ref, at, 0, g, FORE_HEADS, width))
            key = head_block(qkv_ref, at, 1, g, FORE_HEADS, width)
            value = head_block(qkv_ref, at, 2, g, FORE_HEADS, width)
            scores = nt(key, query) * (HEAD**-0.5)
            peak = jnp.max(scores, axis=0, keepdims=True)
            expo = jnp.exp(scores - peak)
            denom = jnp.sum(expo, axis=0, keepdims=True)
            probs_low = (expo * (1.0 / denom)).astype(BF)
            if micro == 0:
                level_ref[pl.ds(i * groups + g, 1), :] = peak + jnp.log(denom)
            else:
                each = BACK_HEADS // FORE_HEADS
                line = (i * (HEADS // BACK_HEADS) + g // each) * SEQ
                column = g % each * FORE_HEADS * SEQ
                to = pl.ds(pl.multiple_of(line, 16), SEQ)
                level_ref[to, column : column + FORE_HEADS * SEQ] = probs_low
            mixed = gather_heads(tn(probs_low, value))
            mixed_ref[at, g * wide : (g + 1) * wide] = mixed.astype(BF)
        return carry

    lax.fori_loop(0, images, image, 0, unroll=micro == 0)

    stores.append(move(mixed_ref, mixed_h, out_sem.at[2]))
    stores.append(move(level_ref, level_h, out_sem.at[4]))

    for n in range(5, 9):
        loads[n].wait()
    x_mid = tok_ref[...].astype(F32) + nn(mixed_ref[...], wo_ref[...])
    x1_ref[...] = x_mid
    stores.append(move(x1_ref, x1_h, out_sem.at[3]))
    normed, _ = normalize(x_mid)
    h_second = (normed * g2_ref[...]).astype(BF)
    all_s[:rows, :] = h_second
    logits = nt(router_ref[...], h_second)
    picked = [jnp.sum(on[k] * logits, axis=0, keepdims=True) for k in range(2)]
    top = jnp.maximum(picked[0], picked[1])
    expo = [jnp.exp(v - top) for v in picked]
    total = expo[0] + expo[1]
    gates = [v / total for v in expo]
    stack = jnp.concatenate(
        gates + place + [picks.astype(F32)] + [jnp.zeros((2, rows), F32)], axis=0
    )
    meta = jnp.transpose(stack)
    meta_ref[...] = meta
    stores.append(move(meta_ref, meta_h, out_sem.at[5]))
    grad_out = cot_ref[...].astype(F32)
    all_s[rows : 2 * rows, :] = (meta[:, 0:1] * grad_out).astype(BF)
    all_s[2 * rows :, :] = (meta[:, 1:2] * grad_out).astype(BF)
    place = [v.astype(jnp.int32) for v in place]

    gone = jnp.full((1, 2 * rows), -1, jnp.int32)
    pos_a = jnp.concatenate([place[0], place[0] + cap, place[1] + cap], axis=1)
    pos_b = jnp.concatenate([place[1], gone], axis=1)
    step = send_ref.shape[0] // FILLS
    for c in range(FILLS):
        start = c * step
        row = iota((step, 3 * rows), 0) + start
        first = jnp.where((row == pos_a) | (row == pos_b), 1.0, 0.0).astype(BF)
        part = nn(first, all_s[...])
        send_ref[pl.ds(start, step), :] = part.astype(BF)
        at = pl.ds(start, step)
        stores.append(move(send_ref.at[at], send_h.at[at], out_sem.at[6 + c]))
    for copy in stores:
        copy.wait()


def move(source, target, sem):
    copy = pltpu.make_async_copy(source, target, sem)
    copy.start()
    return copy


def micro_spec(shape, micro):
    return pl.BlockSpec((1,) + tuple(shape[1:]), lambda i: (micro,) + (0,) * (len(shape) - 1))


def whole_spec(shape):
    return pl.BlockSpec(tuple(shape), lambda i: (0,) * len(shape))


def params(limit, **more):
    return pltpu.CompilerParams(vmem_limit_bytes=limit * MB, **more)


def fore(micro, cap, tokens, picks_t, ranks, wqkv, wo, g1, g2, router_t, cot):
    _, rows, width = tokens.shape
    experts = router_t.shape[0]
    out_shape = (
        jax.ShapeDtypeStruct((experts * 2 * cap, width), BF),
        jax.ShapeDtypeStruct((rows, 3 * width), BF),
        jax.ShapeDtypeStruct((rows, width), BF),
        jax.ShapeDtypeStruct((rows, width), F32),
        jax.ShapeDtypeStruct((rows // SEQ * HEADS // FORE_HEADS, FORE_HEADS * SEQ), F32),
        jax.ShapeDtypeStruct((rows, 8), F32),
    )
    if micro > 0:
        probs = jax.ShapeDtypeStruct((rows * HEADS // BACK_HEADS, BACK_HEADS * SEQ), BF)
        first = jax.ShapeDtypeStruct((rows, width), BF)
        out_shape = out_shape[:4] + (probs, out_shape[5], first)
    flops = 2 * rows * width * (4 * width + 3 * experts * 2 * cap + 4 * SEQ)
    return pl.pallas_call(
        functools.partial(fore_kernel, cap, micro),
        in_specs=[IN_HBM] * 9,
        out_specs=[IN_HBM] * len(out_shape),
        out_shape=out_shape,
        scratch_shapes=[
            pltpu.VMEM((rows, width), BF),
            pltpu.VMEM(picks_t.shape[1:], jnp.int32),
            pltpu.VMEM(ranks.shape[1:], jnp.int32),
            pltpu.VMEM(wqkv.shape, BF),
            pltpu.VMEM(wo.shape, BF),
            pltpu.VMEM(g1.shape, F32),
            pltpu.VMEM(g2.shape, F32),
            pltpu.VMEM(router_t.shape, BF),
            pltpu.VMEM((rows, width), BF),
        ]
        + [pltpu.VMEM(v.shape, v.dtype) for v in out_shape]
        + [pltpu.VMEM((3 * rows, width), BF)]
        + [pltpu.SemaphoreType.DMA((9,)), pltpu.SemaphoreType.DMA((7 + FILLS,))],
        compiler_params=params(FORE_MB),
        cost_estimate=pl.CostEstimate(flops=4 * flops, bytes_accessed=8 * MB, transcendentals=0),
        name="fore",
    )(tokens, picks_t, ranks, wqkv, wo, g1, g2, router_t, cot)


def expert_kernel(cap, first, *refs):
    if first:
        recv_ref, up_ref, down_ref, ret_ref, dup_ref, ddown_ref = refs[:6]
    else:
        recv_ref, up_ref, down_ref, aup_ref, adown_ref, ret_ref, dup_ref, ddown_ref = refs[:8]
    h_s, g_s, out_s, row_s = refs[-4:]
    step = pl.program_id(0)
    steps = pl.num_programs(0)
    slots = h_s.shape[0]

    def position(shape, dim, start):
        slot = iota(shape, dim) + start
        block = ((slot.astype(F32) + 0.5) * (1.0 / cap)).astype(jnp.int32)
        return slot + block * cap

    part = slots // 4

    @pl.when(step == 0)
    def _():
        def take(c, carry):
            at = pl.ds(pl.multiple_of(c * part, 16), part)
            here = iota((part, 2 * slots), 1)
            there = position((part, 2 * slots), 0, c * part)
            pick = jnp.where(here == there, 1.0, 0.0).astype(BF)
            h_s[at, :] = nn(pick, recv_ref[...]).astype(BF)
            pick = jnp.where(here == there + cap, 1.0, 0.0).astype(BF)
            g_s[at, :] = nn(pick, recv_ref[...]).astype(BF)
            return carry

        lax.fori_loop(0, 4, take, 0)

    up = up_ref[0]
    down = down_ref[0]
    h = h_s[...]
    g = g_s[...]
    pre = nn(h, up)
    grad_act = nt(g, down)
    square = pre * pre
    tanh = jnp.tanh(GELU_C * pre * (1.0 + GELU_A * square))
    half = 0.5 + 0.5 * tanh
    act = (pre * half).astype(BF)
    slope = half + (0.5 * GELU_C) * pre * (1.0 - tanh * tanh) * (1.0 + 3.0 * GELU_A * square)
    grad_pre = (grad_act * slope).astype(BF)
    grad_up = tn(h, grad_pre)
    grad_down = tn(act, g)
    if not first:
        grad_up = grad_up + aup_ref[...]
        grad_down = grad_down + adown_ref[...]
    dup_ref[...] = grad_up.astype(dup_ref.dtype)
    ddown_ref[...] = grad_down.astype(ddown_ref.dtype)
    out = nn(act, down)
    row = nt(grad_pre, up)

    @pl.when(step == 0)
    def _():
        out_s[...] = out
        row_s[...] = row

    @pl.when(step > 0)
    def _():
        out_s[...] += out
        row_s[...] += row

    @pl.when(step == steps - 1)
    def _():
        def give(c, carry):
            at = pl.ds(pl.multiple_of(c * 2 * part, 16), 2 * part)
            here = iota((2 * part, slots), 0) + c * 2 * part
            there = position((2 * part, slots), 1, 0)
            pick = jnp.where(here == there, 1.0, 0.0).astype(BF)
            total = nn(pick, out_s[...].astype(BF))
            pick = jnp.where(here == there + cap, 1.0, 0.0).astype(BF)
            total = total + nn(pick, row_s[...].astype(BF))
            ret_ref[at, :] = total.astype(BF)
            return carry

        lax.fori_loop(0, 4, give, 0)


def expert(cap, recv, up, down, earlier):
    first = earlier is None
    total, width = recv.shape
    slots = total // 2
    hidden = up.shape[2]
    tile = 512
    dtype = F32 if first else BF
    up_block = pl.BlockSpec((width, tile), lambda i: (0, i))
    down_block = pl.BlockSpec((tile, width), lambda i: (i, 0))
    in_specs = [
        whole_spec(recv.shape),
        pl.BlockSpec((1, width, tile), lambda i: (0, 0, i)),
        pl.BlockSpec((1, tile, width), lambda i: (0, i, 0)),
    ]
    args = [recv, up, down]
    if not first:
        in_specs += [up_block, down_block]
        args += list(earlier)
    return pl.pallas_call(
        functools.partial(expert_kernel, cap, first),
        grid=(hidden // tile,),
        in_specs=in_specs,
        out_specs=[whole_spec(recv.shape), up_block, down_block],
        out_shape=(
            jax.ShapeDtypeStruct(recv.shape, BF),
            jax.ShapeDtypeStruct((width, hidden), dtype),
            jax.ShapeDtypeStruct((hidden, width), dtype),
        ),
        scratch_shapes=[
            pltpu.VMEM((slots, width), BF),
            pltpu.VMEM((slots, width), BF),
            pltpu.VMEM((slots, width), F32),
            pltpu.VMEM((slots, width), F32),
        ],
        compiler_params=params(EXPERT_MB),
        cost_estimate=pl.CostEstimate(
            flops=2 * 12 * slots * width * hidden, bytes_accessed=24 * MB, transcendentals=0
        ),
        name="expert",
    )(*args)


def back_kernel(last, micro, *refs):
    take = list(refs)

    def next_refs(count):
        taken, take[:] = take[:count], take[count:]
        return taken

    scal_ref, ret_ref = next_refs(2)
    sources = next_refs(BACK_INS)
    earlier_h = next_refs(4) if last else []
    block_h, dx1_h = next_refs(2)
    (dqkv_h,) = next_refs(1) if last else (None,)
    made_h = next_refs(4 if last else 3)
    held = next_refs(BACK_INS)
    (
        meta_ref,
        cot_ref,
        x1_ref,
        g2_ref,
        router_ref,
        mixed_ref,
        wo_ref,
        qkv_ref,
        level_ref,
        tok_ref,
        g1_ref,
        wqkv_ref,
    ) = held
    in_ref, out_ref, small_ref = next_refs(3)
    block_ref, dx1_ref, dqkv_ref, dmix_s, in_sem, out_sem = next_refs(6)
    if last:
        tail_s, pay_s = next_refs(2)
    sources = [h.at[micro] if h.shape[0] == MICRO else h for h in sources]
    pairs = list(zip(sources, held))
    if last:
        pairs += list(zip(earlier_h[:3], (in_ref, out_ref, small_ref)))
    loads = [move(a, b, in_sem.at[n]) for n, (a, b) in enumerate(pairs[:5])]
    stores = []
    total = ret_ref.shape[0]
    rows, width = x1_ref.shape
    experts = router_ref.shape[0]

    def store(source, target):
        stores.append(move(source, target, out_sem.at[len(stores)]))

    loads[0].wait()
    loads += [move(a, b, in_sem.at[5 + n]) for n, (a, b) in enumerate(pairs[5:8])]
    meta = meta_ref[...]
    gates = [meta[:, k : k + 1] for k in range(2)]
    place = [meta[:, 2 + k : 3 + k].astype(jnp.int32) for k in range(2)]
    picks = [meta[:, 4 + k : 5 + k].astype(jnp.int32) for k in range(2)]
    cap = total // (2 * experts)
    here = iota((rows, total), 1)
    ret = ret_ref[...]
    both = (here == place[0] + cap) | (here == place[1] + cap)
    hot = [jnp.where(m, 1.0, 0.0).astype(BF) for m in (both, here == place[0], here == place[1])]
    stacked = nn(jnp.concatenate(hot, axis=0), ret)
    grad_second = stacked[:rows]
    pair_out = [stacked[rows : 2 * rows], stacked[2 * rows :]]
    for n in range(1, 5):
        loads[n].wait()
    loads += [move(a, b, in_sem.at[8 + n]) for n, (a, b) in enumerate(pairs[8:])]
    grad_out = cot_ref[...].astype(F32)
    x_mid = x1_ref[...]
    result = x_mid
    grad_gate = []
    for k in range(2):
        result = result + gates[k] * pair_out[k]
        grad_gate.append(jnp.sum(grad_out * pair_out[k], axis=1, keepdims=True))
    block_ref[...] = result.astype(BF)
    store(block_ref, block_h.at[micro])
    mean_gate = gates[0] * grad_gate[0] + gates[1] * grad_gate[1]
    lane = iota((rows, experts), 1)
    grad_logits = jnp.zeros((rows, experts), F32)
    for k in range(2):
        grad_pick = gates[k] * (grad_gate[k] - mean_gate)
        grad_logits = grad_logits + jnp.where(lane == picks[k], grad_pick, 0.0)
    grad_logits = grad_logits.astype(BF)
    grad_second = grad_second + nn(grad_logits, router_ref[...])
    normed, factor = normalize(x_mid)
    h_second = (normed * g2_ref[...]).astype(BF)
    small = [
        tn(grad_logits, h_second),
        jnp.sum(grad_second * normed, axis=0, keepdims=True),
    ]
    grad_mid = grad_out + norm_back(grad_second * g2_ref[...], normed, factor)
    dx1_ref[...] = grad_mid
    if last:
        store(dx1_ref, dx1_h)
    for n in range(5, 9):
        loads[n].wait()
    grad_attn = grad_mid.astype(BF)
    out_grad = tn(mixed_ref[...], grad_attn)
    if last:
        slots = 2 * lax.axis_size("exp")
        half = slots // 2
        piece = width // half
        span = half * piece
        tail = SMALL * (experts // 16)

        def lay(s, b, block):
            mine = scal_ref[2] == b
            start = jnp.where(mine, 0, half)
            order = jnp.where(mine, scal_ref[0], scal_ref[1])
            for j in range(half):
                to = pl.multiple_of((start + (j ^ order)) * piece, piece)
                pay_s[s, pl.ds(to, piece), :] = block[j * piece : (j + 1) * piece].astype(BF)

        for copy in loads[13:15]:
            copy.wait()
        lay(1, 1, out_grad + out_ref[...].astype(F32))
        small[0] = small[0] + small_ref[0:experts, :]
        small[1] = small[1] + small_ref[experts : experts + 1, :]
        tail_s[:experts, :] = small[0].astype(BF)
    else:
        out_ref[...] = out_grad.astype(BF)
        small_ref[0:experts, :] = small[0]
        small_ref[experts : experts + 1, :] = small[1]
        small_ref[experts + 1 :, :] = jnp.zeros((small_ref.shape[0] - experts - 1, width), F32)
        store(out_ref, made_h[1])
        store(small_ref, made_h[2])
    dmix_s[...] = nt(grad_attn, wo_ref[...]).astype(BF)

    groups = HEADS // BACK_HEADS
    wide = BACK_HEADS * HEAD
    lines = BACK_HEADS // FORE_HEADS
    def image(i, carry):
        at = pl.ds(pl.multiple_of(i * SEQ, 16), SEQ)
        for g in range(groups):
            query = spread_heads(head_block(qkv_ref, at, 0, g, BACK_HEADS, width))
            key = head_block(qkv_ref, at, 1, g, BACK_HEADS, width)
            value = head_block(qkv_ref, at, 2, g, BACK_HEADS, width)
            grad_mixed = spread_heads(dmix_s[at, g * wide : (g + 1) * wide])
            if last:
                line = pl.multiple_of((i * groups + g) * SEQ, 16)
                probs_low = level_ref[pl.ds(line, SEQ), :]
                probs = probs_low.astype(F32)
            else:
                scores = nt(key, query) * (HEAD**-0.5)
                line = (i * groups + g) * lines
                level = [level_ref[pl.ds(line + n, 1), :] for n in range(lines)]
                probs = jnp.exp(scores - jnp.concatenate(level, axis=1))
                probs_low = probs.astype(BF)
            grad_probs = nt(value, grad_mixed)
            inner = jnp.sum(probs * grad_probs, axis=0, keepdims=True)
            grad_scores = (probs * (grad_probs - inner)).astype(BF)
            grad_value = nn(probs_low, grad_mixed)
            grad_key = nn(grad_scores, query) * (HEAD**-0.5)
            grad_query = gather_heads(tn(grad_scores, key)) * (HEAD**-0.5)
            for part, grad in enumerate((grad_query, grad_key, grad_value)):
                start = part * width + g * wide
                dqkv_ref[at, start : start + wide] = grad.astype(BF)
        return carry

    lax.fori_loop(0, rows // SEQ, image, 0, unroll=last)

    if last:
        store(dqkv_ref, dqkv_h)
    for n in range(9, 13 if last else 12):
        loads[n].wait()
    if last:
        h_first = tok_ref[...]
    else:
        normed, factor = normalize(tok_ref[...].astype(F32))
        h_first = (normed * g1_ref[...]).astype(BF)
    gain = jnp.zeros((width, 1), F32)
    for part in (2, 0, 1):
        columns = slice(part * width, (part + 1) * width)
        in_grad = tn(h_first, dqkv_ref[:, columns])
        if not last:
            in_ref[:, columns] = in_grad.astype(BF)
            continue
        in_grad = in_grad + in_ref[:, columns].astype(F32)
        gain = gain + jnp.sum(wqkv_ref[:, columns].astype(F32) * in_grad, axis=1, keepdims=True)
        lay(part // 2, part % 2, in_grad)
        if part != 0:
            s = part // 2
            store(pay_s.at[s, pl.ds(span, span)], made_h[s].at[pl.ds(0, span)])
            store(pay_s.at[s, pl.ds(0, span)], made_h[2 + s].at[pl.ds(0, span)])
    if last:
        eye = iota((width, width), 0) == iota((width, width), 1)
        gain = jnp.sum(jnp.where(eye, gain, 0.0), axis=0, keepdims=True) / g1_ref[...]
        fill = jnp.zeros((tail - experts - 2, width), F32)
        tail_s[experts:, :] = jnp.concatenate([small[1], gain, fill], axis=0).astype(BF)
        for target in (made_h[0], made_h[2]):
            store(tail_s, target.at[pl.ds(span, tail)])
    else:
        store(in_ref, made_h[0])
        grad_first = nt(dqkv_ref[...], wqkv_ref[...]) * g1_ref[...]
        dx1_ref[...] = dx1_ref[...] + norm_back(grad_first, normed, factor)
        store(dx1_ref, dx1_h.at[micro])
    for copy in stores:
        copy.wait()


BACK_INS = 12


def back(micro, scal, plan, ret, saved, tokens, cot, wqkv, wo, g1, g2, router_t, earlier):
    last = earlier is not None
    qkv, mixed, x1, level, meta, *more = saved
    _, rows, width = tokens.shape
    experts = router_t.shape[0]
    slots, piece, tail = plan
    ins = [meta, cot, x1, g2, router_t, mixed, wo, qkv, level, *(more or [tokens]), g1, wqkv]
    shapes = [
        jax.ShapeDtypeStruct(tokens.shape, BF),
        jax.ShapeDtypeStruct((rows, width), F32),
        jax.ShapeDtypeStruct((rows, 3 * width), BF),
    ]
    kept = list(shapes)
    if not last:
        shapes = [shapes[0], jax.ShapeDtypeStruct(tokens.shape, F32)]
    sums = [
        jax.ShapeDtypeStruct(wqkv.shape, BF),
        jax.ShapeDtypeStruct(wo.shape, BF),
        jax.ShapeDtypeStruct((experts + 8, width), F32),
    ]

    def hold(value):
        shape = value.shape[1:] if value.shape[0] == MICRO else value.shape
        return pltpu.VMEM(shape, value.dtype)

    scratch = [hold(a) for a in ins + sums + kept]
    scratch += [
        pltpu.VMEM((rows, width), BF),
        pltpu.SemaphoreType.DMA((16,)),
        pltpu.SemaphoreType.DMA((12,)),
    ]
    aliases = {}
    if last:
        block, *sums = earlier
        args = [scal, ret] + ins + sums + [block]
        aliases = {17: 0}
        span = slots // 2 * piece
        shapes += [jax.ShapeDtypeStruct((span + more, width), BF) for more in (tail, 0)] * 2
        scratch += [pltpu.VMEM((tail, width), BF), pltpu.VMEM((2, slots * piece, width), BF)]
    else:
        args = [scal, ret] + ins
        shapes += sums
    in_specs = [pl.BlockSpec(memory_space=pltpu.SMEM), IN_VMEM] + [IN_HBM] * (len(args) - 2)
    out_specs = [IN_HBM] * len(shapes)
    flops = 2 * rows * width * (3 * ret.shape[0] + 12 * width)
    return pl.pallas_call(
        functools.partial(back_kernel, last, micro),
        in_specs=in_specs,
        out_specs=out_specs,
        out_shape=shapes,
        scratch_shapes=scratch,
        input_output_aliases=aliases,
        compiler_params=params(LAST_MB if last else BACK_MB),
        cost_estimate=pl.CostEstimate(flops=5 * flops, bytes_accessed=20 * MB, transcendentals=0),
        name="back",
    )(*args)


def finish_kernel(dqkv_ref, dx1_ref, tok_ref, wqkv_ref, g1_ref, *refs):
    grad_first = nt(dqkv_ref[...], wqkv_ref[...])
    normed, factor = normalize(tok_ref[0].astype(F32))
    refs[-1][0] = dx1_ref[...] + norm_back(grad_first * g1_ref[...], normed, factor)


def finish(micro, dqkv, dx1, tokens, wqkv, g1, earlier):
    _, rows, width = tokens.shape
    each = rows // 2
    both = pl.BlockSpec((1, each, width), lambda i: (micro, i, 0))
    in_specs = [
        pl.BlockSpec((each, 3 * width), lambda i: (i, 0)),
        pl.BlockSpec((each, width), lambda i: (i, 0)),
        both,
        whole_spec(wqkv.shape),
        whole_spec(g1.shape),
    ]
    args = [dqkv, dx1, tokens, wqkv, g1, earlier]
    in_specs.append(IN_HBM)
    return pl.pallas_call(
        finish_kernel,
        grid=(2,),
        in_specs=in_specs,
        out_specs=both,
        out_shape=jax.ShapeDtypeStruct(tokens.shape, F32),
        input_output_aliases={5: 0},
        compiler_params=params(FINISH_MB),
        cost_estimate=pl.CostEstimate(
            flops=2 * rows * width * 3 * width, bytes_accessed=6 * MB, transcendentals=0
        ),
        name="finish",
    )(*args)


def local(kernel, shapes, args, scalars=0, scratch=()):
    specs = [pl.BlockSpec(memory_space=pltpu.SMEM)] * scalars
    specs += [pl.BlockSpec(memory_space=pltpu.VMEM)] * (len(args) - scalars)
    size = sum(a.size * 4 for a in args)
    return pl.pallas_call(
        kernel,
        in_specs=specs,
        out_specs=[pl.BlockSpec(memory_space=pltpu.VMEM)] * len(shapes),
        out_shape=shapes,
        scratch_shapes=list(scratch),
        compiler_params=params(32),
        cost_estimate=pl.CostEstimate(flops=1000, bytes_accessed=size, transcendentals=0),
    )(*args)


def halve(keep, arrived, count, piece):
    rows, width = keep.shape
    half = count // 2 * piece
    tail = rows - 2 * half

    def kernel(keep_ref, arrived_ref, send_out, keep_out):
        total = (keep_ref[...].astype(F32) + arrived_ref[...].astype(F32)).astype(BF)
        keep_out[:half, :] = total[:half]
        if tail:
            keep_out[half:, :] = total[2 * half :]
        send_out[...] = total[half:]

    shape = jax.ShapeDtypeStruct((half + tail, width), BF)
    return local(kernel, [shape] * 2, [keep, arrived])


def join(first, second):
    rows, width = first.shape

    def kernel(a, b, out):
        out[:rows, :] = a[...]
        out[rows:, :] = b[...]

    (made,) = local(kernel, [jax.ShapeDtypeStruct((2 * rows, width), BF)], [first, second])
    return made


def reduce_all(sends, keeps, scal, plan, width, experts, beside):
    slots, piece, tail = plan
    size = lax.axis_size("exp")
    bits = size.bit_length() - 1
    orders = halving_orders(size)
    low, high = 1 << (bits - 2), 1 << (bits - 1)
    groups = [low, high, low | high]

    def swap(value, step):
        pairs = []
        for core in range(2):
            mask = 1 << orders[core][step]
            pairs += [(core * size + i, core * size + (i ^ mask)) for i in range(size)]
        return lax.ppermute(value, ("grp", "exp"), pairs)

    def swap_far(value, mask):
        return lax.ppermute(value, "exp", [(i, i ^ mask) for i in range(size)])

    def swap_core(value):
        return lax.ppermute(value, "grp", [(0, 1), (1, 0)])

    arrived = [swap_core(v) for v in sends]
    count = slots // 2
    steps = bits - 2
    for step in range(steps):
        made = [halve(keeps[s], arrived[s], count, piece) for s in range(2)]
        count //= 2
        arrived = [swap(made[s][0], step) for s in range(2)]
        keeps = [v[1] for v in made]
        if step == 0:
            extra = beside()
            arrived[0], extra = lax.optimization_barrier((arrived[0], extra))

    share = tail // 4
    span = 2 * piece + share

    def quarter(scal_ref, *refs):
        small_s = refs[8]
        for s in range(2):
            total = refs[s][...].astype(F32) + refs[2 + s][...].astype(F32)
            for j in range(4):
                block = total[j * piece : (j + 1) * piece]
                refs[4 + j][s * piece : (s + 1) * piece, :] = block.astype(BF)
            if s == 0:
                small_s[...] = total[4 * piece :]
        for j in range(4):
            part = pl.multiple_of((scal_ref[3] ^ j) * share, share)
            refs[4 + j][2 * piece :, :] = small_s[pl.ds(part, share), :].astype(BF)

    shape = jax.ShapeDtypeStruct((span, width), BF)
    made = local(
        quarter,
        [shape] * 4,
        [scal] + list(keeps) + list(arrived),
        scalars=1,
        scratch=[pltpu.VMEM((tail, width), F32)],
    )
    arrived = [swap_far(made[1 + j], groups[j]) for j in range(3)]

    def add_up(a, b, c, d, mine_ref):
        total = (a[...].astype(F32) + b[...].astype(F32)) + (c[...].astype(F32) + d[...].astype(F32))
        mine_ref[...] = total.astype(BF)

    (mine,) = local(add_up, [shape], [made[0]] + arrived)

    others = [swap_far(mine, groups[j]) for j in range(3)]

    def lay(scal_ref, a, b, c, d, one_ref, two_ref, small_ref):
        for j, ref in enumerate((a, b, c, d)):
            one_ref[j * piece : (j + 1) * piece, :] = ref[:piece, :]
            two_ref[j * piece : (j + 1) * piece, :] = ref[piece : 2 * piece, :]
            part = pl.multiple_of((scal_ref[3] ^ j) * share, share)
            small_ref[pl.ds(part, share), :] = ref[2 * piece :, :].astype(F32)

    shape = jax.ShapeDtypeStruct((4 * piece, width), BF)
    *have, small = local(
        lay,
        [shape] * 2 + [jax.ShapeDtypeStruct((tail, width), F32)],
        [scal, mine] + others,
        scalars=1,
    )
    vectors = (small[experts + 1], small[experts], small[:experts].T)
    for step in reversed(range(1, steps)):
        arrived = [swap(have[s], step) for s in range(2)]
        have = [join(have[s], arrived[s]) for s in range(2)]
    count = slots // 4
    rows = count * piece

    def deal(first, whose, *refs):
        scal_ref, refs = refs[0], refs[1:]
        in_h, out_h, block_s, sems = refs[-4:]
        core = scal_ref[2]
        copies, later = [], []
        for n, (s, other) in enumerate(whose):
            order = scal_ref[other]
            part = 1 - core if other else core
            for pos in range(count):
                to = pl.multiple_of(((pos ^ order) % count) * piece, piece)
                block = refs[n][pos * piece : (pos + 1) * piece, :].astype(F32)
                block_s[n, pl.ds(to, piece), :] = block
            half = (order // count + (0 if first else 1)) % 2
            at = pl.ds(pl.multiple_of(half * rows, rows), rows)
            if s == 0:
                columns = pl.ds(pl.multiple_of(part * width, width), width)
                copies.append(move(block_s.at[n], in_h.at[at, columns], sems.at[n]))
            else:
                later.append((n, part, at))
        for n, part, at in later:

            @pl.when(part == 0)
            def _():
                target = in_h.at[at, pl.ds(2 * width, width)]
                move(block_s.at[n], target, sems.at[n]).wait()

            @pl.when(part == 1)
            def _():
                move(block_s.at[n], out_h.at[at], sems.at[n]).wait()

        for copy in copies:
            copy.wait()

    def dealt(first, whose, values, grads):
        number = len(values)
        grads = [] if grads is None else list(grads)
        return pl.pallas_call(
            functools.partial(deal, first, whose),
            in_specs=[pl.BlockSpec(memory_space=pltpu.SMEM)]
            + [IN_VMEM] * number
            + [IN_HBM] * len(grads),
            out_specs=[IN_HBM, IN_HBM],
            out_shape=(
                jax.ShapeDtypeStruct((width, 3 * width), F32),
                jax.ShapeDtypeStruct((width, width), F32),
            ),
            input_output_aliases={1 + number: 0, 2 + number: 1} if grads else {},
            scratch_shapes=[
                pltpu.VMEM((number, rows, width), F32),
                pltpu.SemaphoreType.DMA((number,)),
            ],
            compiler_params=params(16),
            cost_estimate=pl.CostEstimate(flops=1000, bytes_accessed=4 * MB, transcendentals=0),
            name="deal",
        )(scal, *values, *grads)

    arrived = [swap(have[s], 0) for s in range(2)]
    near = [swap_core(v) for v in have]
    grads = dealt(True, ((0, 0), (1, 0), (0, 1), (1, 1)), [*have, *near], None)
    arrived[1], vectors, grads = lax.optimization_barrier((arrived[1], vectors, grads))
    far = [swap_core(v) for v in arrived]
    grads = dealt(False, ((0, 0), (1, 0)), arrived, grads)
    in_grad, out_grad = dealt(False, ((0, 1), (1, 1)), far, grads)
    return in_grad, out_grad, *vectors, extra


def halving_orders(size):
    bits = size.bit_length() - 1
    first = list(range(bits - 2))
    second = [first[b ^ 1] if (b ^ 1) < len(first) else b for b in first]
    return first, second


def places(size):
    bits = size.bit_length() - 1
    core = lax.axis_index("grp")
    me = lax.axis_index("exp")
    last = me >> (bits - 2)
    made = []
    for order in halving_orders(size):
        value = jnp.zeros_like(me)
        for b in order:
            value = value * 2 + ((me >> b) & 1)
        made.append(value * 4 + last)
    own = jnp.where(core == 0, made[0], made[1])
    other = jnp.where(core == 0, made[1], made[0])
    return jnp.stack([own, other, core, last]).astype(jnp.int32)


def shards(
    tokens,
    expert_picks,
    priority_ranks,
    attn_input,
    attn_output,
    first_gain,
    second_gain,
    router_weight,
    expert_up,
    expert_down,
    cotangent,
):
    size = lax.axis_size("exp")
    experts = router_weight.shape[1]
    rows, width = tokens.shape[1:]
    cap = max(2, rows // size)
    total = experts * 2 * cap
    slots = 2 * size
    plan = (slots, 2 * width // slots, SMALL * (experts // 16))
    scal = places(size)
    picks_t = jnp.transpose(expert_picks, (0, 2, 1))
    router_t = router_weight.T
    g1 = first_gain.reshape(1, width)
    g2 = second_gain.reshape(1, width)

    def exchange(value):
        value = value.reshape(experts, 2 * cap, width)
        value = lax.all_to_all(value, "exp", split_axis=0, concat_axis=0, tiled=True)
        return value.reshape(total, width)

    saved, sent = [], []
    for micro in range(MICRO):
        made = fore(
            micro,
            cap,
            tokens,
            picks_t,
            priority_ranks,
            attn_input,
            attn_output,
            g1,
            g2,
            router_t,
            cotangent,
        )
        sent.append(made[0])
        saved.append(made[1:])
    arrived = [exchange(v) for v in sent]
    answer0, up0, down0 = expert(cap, arrived[0], expert_up, expert_down, None)
    answer1, up1, down1 = expert(cap, arrived[1], expert_up, expert_down, (up0, down0))
    ret = [exchange(v) for v in (answer0, answer1)]
    up_other = lax.ppermute(up1, "grp", [(0, 1), (1, 0)])
    down_other = lax.ppermute(down1, "grp", [(0, 1), (1, 0)])

    weights = (attn_input, attn_output, g1, g2, router_t)
    block, grad0, *sums = back(
        0, scal, plan, ret[0], saved[0], tokens, cotangent, *weights, None
    )
    halves = lax.optimization_barrier((up1, up_other, down1, down_other, sums[2]))
    up_sum = halves[0].astype(F32) + halves[1].astype(F32)
    down_sum = halves[2].astype(F32) + halves[3].astype(F32)
    up_sum, down_sum, sums[2] = lax.optimization_barrier((up_sum, down_sum, halves[4]))
    block, dx1, dqkv1, *pay = back(
        1, scal, plan, ret[1], saved[1], tokens, cotangent, *weights, (block, *sums)
    )

    def beside():
        return finish(1, dqkv1, dx1, tokens, attn_input, g1, grad0)

    *dense, tokens_grad = reduce_all(pay[:2], pay[2:], scal, plan, width, experts, beside)
    return (block, tokens_grad, *dense, up_sum[None], down_sum[None])


def solution(mesh):
    split = P(None, ("grp", "exp"), None)
    owned = P("exp", None, None)
    in_specs = (split,) * 3 + (P(),) * 5 + (owned, owned, split)
    out_specs = (split, split) + (P(),) * 5 + (owned, owned)
    return jax.shard_map(shards, mesh=mesh, in_specs=in_specs, out_specs=out_specs, check_vma=False)
```
